256 devices in a mesh: ctx: 32 (over y_hi, z, core), mp: 8 (over x, y_lo).
Axes of the slice: x: 4, y: 4 (y_hi: 2, y_lo: 2; y = y_hi * 2 + y_lo), z: 8, core: 2. Of those that a mesh axis runs over, the one named last changes fastest.
Arguments:
- query_heads: bfloat16 [4096, 8192], P('ctx', 'mp'), may hold values from -22 to 22
- key_heads: bfloat16 [4096, 1024], P('ctx', 'mp'), may hold values from -9 to 9
- value_heads: bfloat16 [4096, 1024], P('ctx', 'mp'), may hold values from -6 to 6
- residual_in: bfloat16 [4096, 8192], P('ctx', 'mp'), may hold values from -22 to 22
- norm_gain: bfloat16 [8192], P('mp'), may hold values from 0.5 to 2
- gate_weight: bfloat16 [8192, 14336], P('mp', 'ctx'), may hold values from -0.0625 to 0.0625
- up_weight: bfloat16 [8192, 14336], P('mp', 'ctx'), may hold values from -0.0625 to 0.0625
- doc_lengths: int32 [16], replicated, may hold values from 1 to 1024, 4096 in all
Outputs:
- residual: bfloat16 [4096, 8192], P('ctx', 'mp')
- hidden: bfloat16 [4096, 14336], P('mp', 'ctx')
The draws below stay inside these ranges and needn't reach their ends.
Inputs may be any that keep to these rules, and one draw needn't show every extreme that they name: `doc_lengths`: the longest document has exactly 1024 tokens.
All inputs are finite; a program needn't handle non-finite values.
Results may differ from the reference program's by a relative error of at most 0.027.
Values may be sent and summed in bfloat16 or wider, within the bound.
A program may use at most 128 MiB of HBM per device.

```python
import math
import jax
import jax.numpy as jnp
import numpy as np
from jax import lax

D = 8192
HEADS = 64
KV_HEADS = 8
HD = 128
FF = 14336
NDOCS = 16
TOKENS = 4096
MOST = 1024
N_MP = 8


def draw_key_heads(key, part):
    key = jax.random.fold_in(key, 21)
    own = jnp.clip(jax.random.normal(key, (TOKENS, KV_HEADS * HD), jnp.float32), -4.0, 4.0)
    return own.astype(jnp.bfloat16)


def draw_query_heads(key, part):
    key = jax.random.fold_in(key, 22)
    own = jnp.clip(jax.random.normal(key, (TOKENS, HEADS * HD), jnp.float32), -4.0, 4.0)
    return own.astype(jnp.bfloat16)


def draw_residual_in(key, part):
    key = jax.random.fold_in(key, 31)
    first_key, second_key = jax.random.split(key)
    row_scale = jnp.exp(jax.random.uniform(first_key, (TOKENS, 1), jnp.float32, math.log(0.3), math.log(3.0)))
    column_scale = 0.6 * jnp.exp(math.log(3.0) * jnp.arange(D, dtype=jnp.float32)[None, :] / D)
    values = jnp.clip(jax.random.normal(second_key, (TOKENS, D), jnp.float32), -4.0, 4.0)
    return (values * row_scale * column_scale).astype(jnp.bfloat16)


def levels(stream_key, dims, shards, smallest, high):
    def one(dim, shards_of):
        heights = jax.random.uniform(jax.random.fold_in(jax.random.fold_in(stream_key, 6), dim), (shards_of,), jnp.float32, smallest / len(shards), high / len(shards))
        return jnp.repeat(jnp.exp(heights), dims[dim] // shards_of).reshape((-1,) + (1,) * (len(dims) - dim - 1))

    factor_of = one(*shards[0])
    for cut in shards[1:]:
        factor_of = factor_of * one(*cut)
    return factor_of


def profile(number_of, total, limit, lean):
    loads = [(1 << 20) // math.isqrt(standing ** lean) + 1 for standing in range(2, number_of + 1)]
    spare, given = total - limit - (number_of - 1), [1] * (number_of - 1)
    while spare > 0:
        candidates = [i for i in range(number_of - 1) if given[i] < limit]
        whole, remaining = sum([loads[i] for i in candidates]), spare
        for i in candidates:
            extra = min(limit - given[i], max(1, remaining * loads[i] // whole), spare)
            given[i] = given[i] + extra
            spare = spare - extra
    return np.array([limit] + given)


def uneven(key, number_of, total, bound, skew):
    if number_of == 2:
        one = jax.random.randint(key, (), max(1, total - bound), min(bound, total - 1) + 1)
        return jnp.stack([one, total - one])
    sizes = jnp.asarray(profile(number_of, total, bound, skew), jnp.int32)
    couples = (number_of - 1) // 2
    donor, taker = sizes[1:1 + 2 * couples:2], sizes[2:2 + 2 * couples:2]
    slack = jnp.minimum(donor - 1, bound - taker)
    moved = jax.random.randint(jax.random.fold_in(key, 1), (couples,), 0, 1 << 20) % (slack + 1)
    sizes = sizes.at[1:1 + 2 * couples:2].set(donor - moved).at[2:2 + 2 * couples:2].set(taker + moved)
    return sizes[jax.random.permutation(jax.random.fold_in(key, 2), number_of)]


def noise(own_key, dims, deviation, reach, cuts=(), kind=jnp.bfloat16):
    level = levels(own_key, dims, cuts, -0.22, 0.18) if cuts else 1.0
    array = jax.random.normal(own_key, dims, jnp.float32) * deviation * level
    return jnp.minimum(jnp.maximum(array, -reach), reach).astype(kind)


def setup_inputs(seed: int = 0) -> dict:
    arg_keys = jax.random.split(jax.random.key(seed), 9)
    query_heads = draw_query_heads(jax.random.fold_in(arg_keys[8], 71), 0)
    key_heads = draw_key_heads(jax.random.fold_in(arg_keys[8], 71), 0)
    value_heads = noise(arg_keys[2], (TOKENS, KV_HEADS * HD), 1.0, 6.0, ((0, 32), (1, 8)))
    residual_in = draw_residual_in(jax.random.fold_in(arg_keys[8], 71), 0)
    norm_gain = jnp.clip(jnp.exp(math.log(2.0) - 1.3862944 * jax.random.uniform(arg_keys[4], (D,), jnp.float32) ** levels(arg_keys[4], (D,), ((0, 8),), -0.2, 0.2)), 0.5, 2.0).astype(jnp.bfloat16)
    gate_weight = noise(arg_keys[5], (D, FF), D ** -0.5, 0.0625, ((0, 8), (1, 32)))
    up_weight = noise(arg_keys[6], (D, FF), D ** -0.5, 0.0625, ((0, 8), (1, 32)))
    doc_lengths = uneven(arg_keys[7], NDOCS, TOKENS, MOST, 2).astype(jnp.int32)
    return {"query_heads": query_heads, "key_heads": key_heads, "value_heads": value_heads, "residual_in": residual_in, "norm_gain": norm_gain, "gate_weight": gate_weight, "up_weight": up_weight, "doc_lengths": doc_lengths}


def document_index(positions, doc_ends):
    return lax.optimization_barrier(jnp.sum((positions[:, None] >= doc_ends[None, :]).astype(jnp.int32), axis=1))

def reference(query_heads, key_heads, value_heads, residual_in, norm_gain, gate_weight, up_weight, doc_lengths):
    doc_ends = jnp.cumsum(doc_lengths).astype(jnp.int32)
    positions = jnp.arange(TOKENS, dtype=jnp.int32)
    documents = document_index(positions, doc_ends)
    grouping = HEADS // KV_HEADS
    key_float = key_heads.astype(jnp.float32).reshape(TOKENS, KV_HEADS, HD)
    value_float = value_heads.astype(jnp.float32).reshape(TOKENS, KV_HEADS, HD)
    block_rows = min(128, TOKENS)

    def one_block(block_index):
        first_row = (block_index * block_rows).astype(jnp.int32)
        query_block = lax.dynamic_slice_in_dim(query_heads, first_row, block_rows, 0).astype(jnp.float32)
        query_block = query_block.reshape(block_rows, KV_HEADS, grouping, HD)
        query_pos = first_row + jnp.arange(block_rows, dtype=jnp.int32)
        query_doc = lax.dynamic_slice_in_dim(documents, first_row, block_rows, 0)
        visible = (query_doc[:, None] == documents[None, :]) & (positions[None, :] <= query_pos[:, None])
        scores = jnp.einsum('qhgd,khd->hgqk', query_block, key_float) * HD ** (-0.5)
        scores = jnp.where(visible, scores, -1e+30)
        largest = lax.optimization_barrier(jnp.max(scores, axis=-1, keepdims=True))
        weights = jnp.where(visible, jnp.exp(scores - largest), 0.0)
        denominator = lax.optimization_barrier(jnp.sum(weights, axis=-1))
        rounded = lax.optimization_barrier(weights.astype(jnp.bfloat16)).astype(jnp.float32)
        mixed_heads = jnp.einsum('hgqk,khd->hgqd', rounded, value_float) / denominator[..., None]
        return jnp.transpose(mixed_heads, (2, 0, 1, 3)).reshape(block_rows, HEADS * HD)
    attended = lax.map(one_block, jnp.arange(TOKENS // block_rows, dtype=jnp.int32)).reshape(TOKENS, HEADS * HD)
    residual = (residual_in.astype(jnp.float32) + attended).astype(jnp.bfloat16)
    residual_float = residual.astype(jnp.float32)
    inverse = lax.rsqrt(lax.optimization_barrier(jnp.mean(residual_float * residual_float, axis=1, keepdims=True)) + 1e-05)
    normed = (residual_float * inverse * norm_gain.astype(jnp.float32)[None, :]).astype(jnp.bfloat16)
    shard_width = D // N_MP
    gate_sum = jnp.zeros((TOKENS, FF), jnp.float32)
    up_sum = jnp.zeros((TOKENS, FF), jnp.float32)
    for member in range(N_MP):
        columns = normed[:, member * shard_width:(member + 1) * shard_width]
        gate_part = jnp.dot(columns, gate_weight[member * shard_width:(member + 1) * shard_width], preferred_element_type=jnp.float32)
        up_part = jnp.dot(columns, up_weight[member * shard_width:(member + 1) * shard_width], preferred_element_type=jnp.float32)
        gate_sum = gate_sum + lax.optimization_barrier(gate_part.astype(jnp.bfloat16)).astype(jnp.float32)
        up_sum = up_sum + lax.optimization_barrier(up_part.astype(jnp.bfloat16)).astype(jnp.float32)
    hidden = (jax.nn.silu(gate_sum) * up_sum).astype(jnp.bfloat16)
    return (residual, hidden)
```

```python
import functools

import jax
import jax.numpy as jnp
from jax import lax
from jax.experimental import pallas as pl
from jax.experimental.pallas import tpu as pltpu
from jax.sharding import PartitionSpec as P

D = 8192
HD = 128
MESH = pl.DeviceIdType.MESH
ROWS = 128
KB = 1024
WIDTH_A = 512
WIDTH_B = 384
PARTS = ((0, WIDTH_A), (WIDTH_A, WIDTH_B))
WIDTH = WIDTH_A + WIDTH_B


def place():
    ctx = lax.axis_index("ctx")
    mp = lax.axis_index("mp")
    return ctx // 16, lax.rem(ctx // 2, 8), lax.rem(ctx, 2), mp // 2, lax.rem(mp, 2)


def device(yh, z, c, x, yl):
    return (yh * 16 + z * 2 + c, x * 2 + yl)


def pick(w, values):
    out = jnp.int32(values[0])
    for i in range(1, len(values)):
        out = jnp.where(w == i, jnp.int32(values[i]), out)
    return out


OFFSETS = ((0, 0, -1, 1), (1, -1, 2, -2), (-3, 3, -2, 2), (4, -4, 3, -3))
ONWARD_UP = ((1, 1, 1, 0), (0, 1, 0, 1), (1, 0, 1, 0), (0, 0, 0, 0))
ONWARD_DOWN = ((1, 1, 0, 1), (1, 0, 1, 0), (0, 1, 0, 1), (0, 0, 0, 0))
ORDER = ((0, 0), (1, 0), (2, 0), (0, 1), (3, 0), (1, 1), (2, 1), (3, 1))
FIRST = 4


def ffn_kernel(
    normed_ref, gate_ref, up_ref, out_ref,
    tokens, weights, staged, landed, own_sum,
    w_send, w_recv, cross_send, tok_recv, up_send, down_send, sib_send, hi_send, sum_send, sum_recv,
):
    yh, z, c, x, yl = place()
    match = lax.rem(z // 2, 2) == yl
    w = lax.rem(z - 2 * yl + 8, 4)
    my_source = (z // 4) * 2 + lax.rem(z, 2)
    sibling = device(yh, z, 1 - c, x, yl)
    lo_partner = device(yh, z, c, x, 1 - yl)
    hi_partner = device(1 - yh, z, c, x, yl)
    above = device(yh, lax.rem(z + 1, 8), c, x, yl)
    below = device(yh, lax.rem(z + 7, 8), c, x, yl)
    x_peers = [device(yh, z, c, lax.rem(x + d, 4), yl) for d in (1, 2, 3)]
    mine = pl.ds(pl.multiple_of(c * ROWS, ROWS), ROWS)

    barrier = pltpu.get_barrier_semaphore()
    peers = [sibling, lo_partner, hi_partner, above, below] + x_peers
    for peer in peers:
        pl.semaphore_signal(barrier, inc=1, device_id=peer, device_id_type=MESH)

    weights[yl, :, 0:256] = gate_ref[:, 0:256]
    weights[yl, :, 256:512] = up_ref[:, 0:256]
    weights[yl, :, 512:640] = gate_ref[:, 256:384]
    weights[yl, :, 640:768] = up_ref[:, 256:384]
    weights[yl, :, 768:896] = jnp.concatenate([gate_ref[:, 384:448], up_ref[:, 384:448]], axis=1)
    pl.semaphore_wait(barrier, len(peers))

    def weight_copy(part):
        start, size = PARTS[part]
        view = weights.at[yl, :, pl.ds(start, size)]
        return pltpu.make_async_remote_copy(
            src_ref=view, dst_ref=view, send_sem=w_send.at[part], recv_sem=w_recv.at[part],
            device_id=lo_partner, device_id_type=MESH,
        )

    def cross_copy():
        return pltpu.make_async_remote_copy(
            src_ref=normed_ref, dst_ref=tokens.at[yh, my_source, yl, mine],
            send_sem=cross_send.at[0], recv_sem=tok_recv.at[yh, my_source, yl, c],
            device_id=lo_partner, device_id_type=MESH,
        )

    def token_copy(h, source, kb, sems, target):
        view = tokens.at[h, source, kb, mine]
        return pltpu.make_async_remote_copy(
            src_ref=view, dst_ref=view, send_sem=sems.at[h, source, kb],
            recv_sem=tok_recv.at[h, source, kb, c], device_id=target, device_id_type=MESH,
        )

    def token_arrival(h, source, kb, core):
        view = tokens.at[h, source, kb, pl.ds(pl.multiple_of(core * ROWS, ROWS), ROWS)]
        return pltpu.make_async_remote_copy(
            src_ref=view, dst_ref=view, send_sem=sib_send.at[h, source, kb],
            recv_sem=tok_recv.at[h, source, kb, core], device_id=sibling, device_id_type=MESH,
        )

    def unit_of(step):
        unit = pick(step, [u for u, _ in ORDER])
        half = pick(step, [h for _, h in ORDER])
        table = lambda rows: pick(unit * 4 + w, [v for row in rows for v in row])
        source_z = lax.rem(z + table(OFFSETS) + 8, 8)
        source = (source_z // 4) * 2 + lax.rem(source_z, 2)
        h = lax.rem(yh + half, 2)
        own = jnp.logical_and(match, unit == 0)
        return h, half, source, own, table(ONWARD_UP) == 1, table(ONWARD_DOWN) == 1

    def order_of_blocks(i):
        return lax.rem(yl + i, 2)

    def handle(step):
        h, half, source, own, go_up, go_down = unit_of(step)
        at_home = jnp.logical_and(own, half == 0)
        for i in range(2):
            kb = order_of_blocks(i)
            if i == 0:
                @pl.when(jnp.logical_not(at_home))
                def _():
                    token_arrival(h, source, kb, c).wait_recv()
            else:
                token_arrival(h, source, kb, c).wait_recv()

            @pl.when(go_up)
            def _():
                token_copy(h, source, kb, up_send, above).start()

            @pl.when(go_down)
            def _():
                token_copy(h, source, kb, down_send, below).start()

            token_copy(h, source, kb, sib_send, sibling).start()

            @pl.when(at_home)
            def _():
                token_copy(h, source, kb, hi_send, hi_partner).start()

    def sum_copy(h, source, part, peer):
        start, size = PARTS[part]
        low = lax.rem(source, 2)
        owner = h * 2 + source // 2
        slot = lax.rem(x - owner + 4, 4) - 1
        return pltpu.make_async_remote_copy(
            src_ref=staged.at[h, source, :, pl.ds(start, size)],
            dst_ref=landed.at[slot, low, :, pl.ds(start, size)],
            send_sem=sum_send.at[h, source, part], recv_sem=sum_recv.at[slot, low, part],
            device_id=device(yh, z, c, owner, yl), device_id_type=MESH,
        )

    def multiply(step, part):
        h, _, source, _, _, _ = unit_of(step)
        start, size = PARTS[part]
        columns = pl.ds(start, size)
        product = jnp.dot(
            tokens[h, source, 0], weights[0, :, columns], preferred_element_type=jnp.float32
        ) + jnp.dot(
            tokens[h, source, 1], weights[1, :, columns], preferred_element_type=jnp.float32
        )
        owned = h * 2 + source // 2 == x

        @pl.when(owned)
        def _():
            own_sum[lax.rem(source, 2), :, columns] = product

        @pl.when(jnp.logical_not(owned))
        def _():
            staged[h, source, :, columns] = product.astype(jnp.bfloat16)
            sum_copy(h, source, part, None).start()

    def sibling_arrived(step):
        h, _, source, _, _, _ = unit_of(step)
        for i in range(2):
            token_arrival(h, source, i, 1 - c).wait_recv()

    @pl.when(match)
    def _():
        tokens[yh, my_source, yl, mine] = normed_ref[...]

    @pl.when(jnp.logical_not(match))
    def _():
        cross_copy().start()

    for part in range(2):
        weight_copy(part).start()

    def weights_arrived(part):
        start, size = PARTS[part]
        view = weights.at[1 - yl, :, pl.ds(start, size)]
        pltpu.make_async_remote_copy(
            src_ref=view, dst_ref=view, send_sem=w_send.at[part], recv_sem=w_recv.at[part],
            device_id=lo_partner, device_id_type=MESH,
        ).wait_recv()

    handle(0)
    weights_arrived(0)

    def first(step, _):
        handle(step + 1)
        sibling_arrived(step)
        multiply(step, 0)
        return 0

    lax.fori_loop(0, FIRST, first, 0)
    weights_arrived(1)

    def catch_up(step, _):
        multiply(step, 1)
        return 0

    lax.fori_loop(0, FIRST, catch_up, 0)

    def second(step, _):
        @pl.when(step < 7)
        def _():
            handle(step + 1)

        sibling_arrived(step)
        multiply(step, 0)
        multiply(step, 1)
        return 0

    lax.fori_loop(FIRST, 8, second, 0)

    def finish(low, _):
        rows = pl.ds(pl.multiple_of(low * 256, 256), 256)
        totals = []
        for part in range(2):
            start, size = PARTS[part]
            columns = pl.ds(start, size)
            total = own_sum[low, :, columns]
            for slot in range(3):
                view = landed.at[slot, low, :, columns]
                pltpu.make_async_remote_copy(
                    src_ref=view, dst_ref=view, send_sem=sum_send.at[0, 0, part],
                    recv_sem=sum_recv.at[slot, low, part], device_id=x_peers[0], device_id_type=MESH,
                ).wait_recv()
                total = total + landed[slot, low, :, columns].astype(jnp.float32)
            totals.append(total)
        a, b = totals
        silu = lambda v: v / (1.0 + jnp.exp(-v))
        out_ref[rows, 0:256] = (silu(a[:, :256]) * a[:, 256:]).astype(jnp.bfloat16)
        out_ref[rows, 256:384] = (silu(b[:, :128]) * b[:, 128:256]).astype(jnp.bfloat16)
        tail = b[:, 256:384]
        mixed = silu(tail) * pltpu.roll(tail, 64, 1)
        out_ref[rows, 384:448] = mixed[:, :64].astype(jnp.bfloat16)
        return 0

    lax.fori_loop(0, 2, finish, 0)

    for part in range(2):
        weight_copy(part).wait_send()

    @pl.when(jnp.logical_not(match))
    def _():
        cross_copy().wait_send()

    def drain(step, _):
        h, half, source, own, go_up, go_down = unit_of(step)
        for kb in range(2):
            @pl.when(go_up)
            def _():
                token_copy(h, source, kb, up_send, above).wait_send()

            @pl.when(go_down)
            def _():
                token_copy(h, source, kb, down_send, below).wait_send()

            token_copy(h, source, kb, sib_send, sibling).wait_send()

            @pl.when(jnp.logical_and(own, half == 0))
            def _():
                token_copy(h, source, kb, hi_send, hi_partner).wait_send()

        @pl.when(h * 2 + source // 2 != x)
        def _():
            for part in range(2):
                sum_copy(h, source, part, None).wait_send()
        return 0

    lax.fori_loop(0, 8, drain, 0)


def feed_forward(normed, gate_weight, up_weight):
    dma = pltpu.SemaphoreType.DMA
    vmem = pl.BlockSpec(memory_space=pltpu.VMEM)
    return pl.pallas_call(
        ffn_kernel,
        out_shape=jax.ShapeDtypeStruct((512, 448), jnp.bfloat16),
        in_specs=[vmem] * 3,
        out_specs=vmem,
        scratch_shapes=[
            pltpu.VMEM((2, 4, 2, 2 * ROWS, KB), jnp.bfloat16),
            pltpu.VMEM((2, KB, WIDTH), jnp.bfloat16),
            pltpu.VMEM((2, 4, 2 * ROWS, WIDTH), jnp.bfloat16),
            pltpu.VMEM((3, 2, 2 * ROWS, WIDTH), jnp.bfloat16),
            pltpu.VMEM((2, 2 * ROWS, WIDTH), jnp.float32),
            dma((2,)), dma((2,)), dma((1,)), dma((2, 4, 2, 2)),
            dma((2, 4, 2)), dma((2, 4, 2)), dma((2, 4, 2)), dma((2, 4, 2)),
            dma((2, 4, 2)), dma((3, 2, 2)),
        ],
        compiler_params=pltpu.CompilerParams(
            collective_id=0, has_side_effects=True, vmem_limit_bytes=56 * 2**20
        ),
        name="feed_forward",
    )(normed, gate_weight, up_weight)


def from_behind(block, axis, distance):
    devices = range(lax.axis_size(axis))
    route = [(i - distance, i) for i in devices if i - distance in devices]
    return lax.ppermute(block, axis, route)


def document_index(positions, doc_ends):
    return jnp.sum((positions[:, None] >= doc_ends[None, :]).astype(jnp.int32), axis=1)


def on_device(
    query_heads, key_heads, value_heads, residual_in, norm_gain, gate_weight, up_weight, doc_lengths
):
    local_rows = query_heads.shape[0]
    ctx_count = lax.axis_size("ctx")
    ctx_index = lax.axis_index("ctx")
    doc_ends = jnp.cumsum(doc_lengths)
    query_pos = ctx_index * local_rows + jnp.arange(local_rows, dtype=jnp.int32)
    query_doc = document_index(query_pos, doc_ends)
    kv_groups = key_heads.shape[1] // HD
    group_size = query_heads.shape[1] // HD // kv_groups
    query_split = query_heads.reshape(local_rows, kv_groups, group_size, HD)

    def attend(carried, key_piece, value_piece, offset):
        key_count = key_piece.shape[0]
        key_pos = offset + jnp.arange(key_count, dtype=jnp.int32)
        key_doc = document_index(key_pos, doc_ends)
        visible = (
            (query_doc[:, None] == key_doc[None, :])
            & (key_pos[None, :] <= query_pos[:, None])
            & (key_pos[None, :] >= 0)
        )

        def update(previous):
            running_max, denominator, weighted = previous
            key_split = key_piece.reshape(key_count, kv_groups, HD)
            value_split = value_piece.reshape(key_count, kv_groups, HD)
            scores = jnp.einsum(
                "qhgd,khd->hgqk", query_split, key_split, preferred_element_type=jnp.float32
            ) * HD ** (-0.5)
            scores = jnp.where(visible, scores, -1e30)
            new_max = jnp.maximum(running_max, jnp.max(scores, axis=-1))
            factor = jnp.exp(running_max - new_max)
            weights = jnp.where(visible, jnp.exp(scores - new_max[..., None]), 0.0)
            denominator = denominator * factor + jnp.sum(weights, axis=-1)
            weighted = weighted * factor[..., None] + jnp.einsum(
                "hgqk,khd->hgqd",
                weights.astype(jnp.bfloat16),
                value_split,
                preferred_element_type=jnp.float32,
            )
            return (new_max, denominator, weighted)

        return lax.cond(jnp.any(visible), update, lambda previous: previous, carried)

    starting = (
        jnp.full((kv_groups, group_size, local_rows), -1e30, jnp.float32),
        jnp.zeros((kv_groups, group_size, local_rows), jnp.float32),
        jnp.zeros((kv_groups, group_size, local_rows, HD), jnp.float32),
    )
    finished = attend(starting, key_heads, value_heads, ctx_index * local_rows)
    travelling = jnp.stack([key_heads, value_heads])
    for distance in range(1, ctx_count // 4 + 1):
        travelling = from_behind(travelling, "ctx", 1)
        finished = attend(
            finished, travelling[0], travelling[1], (ctx_index - distance) * local_rows
        )
    running_max, denominator, weighted = finished
    attended = jnp.transpose(weighted / denominator[..., None], (2, 0, 1, 3)).reshape(
        local_rows, kv_groups * group_size * HD
    )
    residual = (residual_in.astype(jnp.float32) + attended).astype(jnp.bfloat16)
    residual_float = residual.astype(jnp.float32)
    squares = lax.psum(jnp.sum(residual_float * residual_float, axis=1), "mp")
    inverse = lax.rsqrt(squares / D + 1e-05)
    normed = (residual_float * inverse[:, None] * norm_gain.astype(jnp.float32)[None, :]).astype(
        jnp.bfloat16
    )
    hidden = feed_forward(normed, gate_weight, up_weight)
    return (residual, hidden)


def solution(mesh):
    in_specs = (
        P("ctx", "mp"),
        P("ctx", "mp"),
        P("ctx", "mp"),
        P("ctx", "mp"),
        P("mp"),
        P("mp", "ctx"),
        P("mp", "ctx"),
        P(),
    )
    out_specs = (P("ctx", "mp"), P("mp", "ctx"))
    return jax.shard_map(
        on_device, mesh=mesh, in_specs=in_specs, out_specs=out_specs, check_vma=False
    )
```

```python
import functools

import jax
import jax.numpy as jnp
from jax import lax
from jax.experimental import pallas as pl
from jax.experimental.pallas import tpu as pltpu
from jax.sharding import PartitionSpec as P

D = 8192
HD = 128
MESH = pl.DeviceIdType.MESH
ROWS = 128
KB = 1024
WIDTH_A = 512
WIDTH_B = 384
PARTS = ((0, WIDTH_A), (WIDTH_A, WIDTH_B))
WIDTH = WIDTH_A + WIDTH_B


def place():
    ctx = lax.axis_index("ctx")
    mp = lax.axis_index("mp")
    return ctx // 16, lax.rem(ctx // 2, 8), lax.rem(ctx, 2), mp // 2, lax.rem(mp, 2)


def device(yh, z, c, x, yl):
    return (yh * 16 + z * 2 + c, x * 2 + yl)


def pick(w, values):
    out = jnp.int32(values[0])
    for i in range(1, len(values)):
        out = jnp.where(w == i, jnp.int32(values[i]), out)
    return out


OFFSETS = ((0, 0, -1, 1), (1, -1, 2, -2), (-3, 3, -2, 2), (4, -4, 3, -3))
ONWARD_UP = ((1, 1, 1, 0), (0, 1, 0, 1), (1, 0, 1, 0), (0, 0, 0, 0))
ONWARD_DOWN = ((1, 1, 0, 1), (1, 0, 1, 0), (0, 1, 0, 1), (0, 0, 0, 0))
ORDER = ((0, 0), (1, 0), (2, 0), (0, 1), (3, 0), (1, 1), (2, 1), (3, 1))
FIRST = 4


def document_starts(lengths_ref, positions):
    starts = jnp.zeros_like(positions)
    end = jnp.int32(0)
    for i in range(lengths_ref.shape[0]):
        end = end + lengths_ref[i]
        starts = jnp.where(positions >= end, end, starts)
    return starts


def layer_kernel(
    lengths_ref, query_ref, key_ref, value_ref, residual_in_ref, gain_ref, gate_ref, up_ref,
    residual_ref, out_ref,
    tokens, weights, staged, landed, own_sum,
    query, by_head, keys_values, residual_in, tails, normed_ref, squares,
    running_max, denominator, weighted,
    load_sem, kv_send, kv_sib_send, kv_recv, sq_send, sq_recv,
    w_send, w_recv, cross_send, tok_recv, up_send, down_send, sib_send, hi_send, sum_send, sum_recv,
):
    yh, z, c, x, yl = place()
    match = lax.rem(z // 2, 2) == yl
    w = lax.rem(z - 2 * yl + 8, 4)
    my_source = (z // 4) * 2 + lax.rem(z, 2)
    sibling = device(yh, z, 1 - c, x, yl)
    lo_partner = device(yh, z, c, x, 1 - yl)
    hi_partner = device(1 - yh, z, c, x, yl)
    above = device(yh, lax.rem(z + 1, 8), c, x, yl)
    below = device(yh, lax.rem(z + 7, 8), c, x, yl)
    x_peers = [device(yh, z, c, lax.rem(x + d, 4), yl) for d in (1, 2, 3)]
    mine = pl.ds(pl.multiple_of(c * ROWS, ROWS), ROWS)

    mp = x * 2 + yl
    chip = yh * 8 + z
    after = device(lax.rem((chip + 1) // 8, 2), lax.rem(chip + 1, 8), c, x, yl)
    before = device(lax.rem((chip + 15) // 8, 2), lax.rem(chip + 15, 8), c, x, yl)

    loads = [
        pltpu.make_async_copy(key_ref, keys_values.at[0, 0, mine], load_sem.at[0]),
        pltpu.make_async_copy(value_ref, keys_values.at[0, 1, mine], load_sem.at[1]),
        pltpu.make_async_copy(query_ref, query, load_sem.at[2]),
        pltpu.make_async_copy(residual_in_ref, residual_in, load_sem.at[3]),
        pltpu.make_async_copy(gate_ref.at[:, pl.ds(0, 256)], weights.at[yl, :, pl.ds(0, 256)], load_sem.at[4]),
        pltpu.make_async_copy(up_ref.at[:, pl.ds(0, 256)], weights.at[yl, :, pl.ds(256, 256)], load_sem.at[5]),
        pltpu.make_async_copy(gate_ref.at[:, pl.ds(256, 128)], weights.at[yl, :, pl.ds(512, 128)], load_sem.at[6]),
        pltpu.make_async_copy(up_ref.at[:, pl.ds(256, 128)], weights.at[yl, :, pl.ds(640, 128)], load_sem.at[7]),
        pltpu.make_async_copy(gate_ref.at[:, pl.ds(384, 64)], tails.at[0], load_sem.at[8]),
        pltpu.make_async_copy(up_ref.at[:, pl.ds(384, 64)], tails.at[1], load_sem.at[9]),
    ]
    for load in loads:
        load.start()

    barrier = pltpu.get_barrier_semaphore()
    across = [device(yh, z, c, lax.rem(x + d, 4), 1 - yl) for d in (1, 2, 3)]
    peers = [sibling, lo_partner, hi_partner, above, below] + x_peers + across
    for peer in peers:
        pl.semaphore_signal(barrier, inc=1, device_id=peer, device_id_type=MESH)

    @pl.when(chip == 8)
    def _():
        pl.semaphore_signal(barrier, inc=1, device_id=before, device_id_type=MESH)

    pl.semaphore_wait(barrier, len(peers) + jnp.where(chip == 7, 1, 0))
    for load in loads[:2]:
        load.wait()

    def kv_onward(j):
        return pltpu.make_async_remote_copy(
            src_ref=keys_values.at[j, :, mine], dst_ref=keys_values.at[j + 1, :, mine],
            send_sem=kv_send.at[j], recv_sem=kv_recv.at[j + 1, c],
            device_id=after, device_id_type=MESH,
        )

    def kv_sibling(j):
        view = keys_values.at[j, :, mine]
        return pltpu.make_async_remote_copy(
            src_ref=view, dst_ref=view, send_sem=kv_sib_send.at[j], recv_sem=kv_recv.at[j, c],
            device_id=sibling, device_id_type=MESH,
        )

    def kv_arrival(j, core):
        view = keys_values.at[j, :, pl.ds(pl.multiple_of(core * ROWS, ROWS), ROWS)]
        return pltpu.make_async_remote_copy(
            src_ref=view, dst_ref=view, send_sem=kv_sib_send.at[j], recv_sem=kv_recv.at[j, core],
            device_id=sibling, device_id_type=MESH,
        )

    @pl.when(chip < 15)
    def _():
        kv_onward(0).start()

    kv_sibling(0).start()

    for load in loads[4:]:
        load.wait()
    weights[yl, :, 768:896] = jnp.concatenate([tails[0], tails[1]], axis=1)

    def weight_copy(part):
        start, size = PARTS[part]
        view = weights.at[yl, :, pl.ds(start, size)]
        return pltpu.make_async_remote_copy(
            src_ref=view, dst_ref=view, send_sem=w_send.at[part], recv_sem=w_recv.at[part],
            device_id=lo_partner, device_id_type=MESH,
        )

    def cross_copy():
        return pltpu.make_async_remote_copy(
            src_ref=normed_ref, dst_ref=tokens.at[yh, my_source, yl, mine],
            send_sem=cross_send.at[0], recv_sem=tok_recv.at[yh, my_source, yl, c],
            device_id=lo_partner, device_id_type=MESH,
        )

    def token_copy(h, source, kb, sems, target):
        view = tokens.at[h, source, kb, mine]
        return pltpu.make_async_remote_copy(
            src_ref=view, dst_ref=view, send_sem=sems.at[h, source, kb],
            recv_sem=tok_recv.at[h, source, kb, c], device_id=target, device_id_type=MESH,
        )

    def token_arrival(h, source, kb, core):
        view = tokens.at[h, source, kb, pl.ds(pl.multiple_of(core * ROWS, ROWS), ROWS)]
        return pltpu.make_async_remote_copy(
            src_ref=view, dst_ref=view, send_sem=sib_send.at[h, source, kb],
            recv_sem=tok_recv.at[h, source, kb, core], device_id=sibling, device_id_type=MESH,
        )

    def unit_of(step):
        unit = pick(step, [u for u, _ in ORDER])
        half = pick(step, [h for _, h in ORDER])
        table = lambda rows: pick(unit * 4 + w, [v for row in rows for v in row])
        source_z = lax.rem(z + table(OFFSETS) + 8, 8)
        source = (source_z // 4) * 2 + lax.rem(source_z, 2)
        h = lax.rem(yh + half, 2)
        own = jnp.logical_and(match, unit == 0)
        return h, half, source, own, table(ONWARD_UP) == 1, table(ONWARD_DOWN) == 1

    def order_of_blocks(i):
        return lax.rem(yl + i, 2)

    def handle(step):
        h, half, source, own, go_up, go_down = unit_of(step)
        at_home = jnp.logical_and(own, half == 0)
        for i in range(2):
            kb = order_of_blocks(i)
            if i == 0:
                @pl.when(jnp.logical_not(at_home))
                def _():
                    token_arrival(h, source, kb, c).wait_recv()
            else:
                token_arrival(h, source, kb, c).wait_recv()

            @pl.when(go_up)
            def _():
                token_copy(h, source, kb, up_send, above).start()

            @pl.when(go_down)
            def _():
                token_copy(h, source, kb, down_send, below).start()

            token_copy(h, source, kb, sib_send, sibling).start()

            @pl.when(at_home)
            def _():
                token_copy(h, source, kb, hi_send, hi_partner).start()

    def sum_copy(h, source, part, peer):
        start, size = PARTS[part]
        low = lax.rem(source, 2)
        owner = h * 2 + source // 2
        slot = lax.rem(x - owner + 4, 4) - 1
        return pltpu.make_async_remote_copy(
            src_ref=staged.at[h, source, :, pl.ds(start, size)],
            dst_ref=landed.at[slot, low, :, pl.ds(start, size)],
            send_sem=sum_send.at[h, source, part], recv_sem=sum_recv.at[slot, low, part],
            device_id=device(yh, z, c, owner, yl), device_id_type=MESH,
        )

    def multiply(step, part):
        h, _, source, _, _, _ = unit_of(step)
        start, size = PARTS[part]
        columns = pl.ds(start, size)
        product = jnp.dot(
            tokens[h, source, 0], weights[0, :, columns], preferred_element_type=jnp.float32
        ) + jnp.dot(
            tokens[h, source, 1], weights[1, :, columns], preferred_element_type=jnp.float32
        )
        owned = h * 2 + source // 2 == x

        @pl.when(owned)
        def _():
            own_sum[lax.rem(source, 2), :, columns] = product

        @pl.when(jnp.logical_not(owned))
        def _():
            staged[h, source, :, columns] = product.astype(jnp.bfloat16)
            sum_copy(h, source, part, None).start()

    def sibling_arrived(step):
        h, _, source, _, _, _ = unit_of(step)
        for i in range(2):
            token_arrival(h, source, i, 1 - c).wait_recv()

    for part in range(2):
        weight_copy(part).start()

    def weights_arrived(part):
        start, size = PARTS[part]
        view = weights.at[1 - yl, :, pl.ds(start, size)]
        pltpu.make_async_remote_copy(
            src_ref=view, dst_ref=view, send_sem=w_send.at[part], recv_sem=w_recv.at[part],
            device_id=lo_partner, device_id_type=MESH,
        ).wait_recv()

    for load in loads[2:4]:
        load.wait()
    for head in range(8):
        by_head[head // 2, (head % 2) * ROWS:(head % 2 + 1) * ROWS] = query[:, head * HD:(head + 1) * HD]
    running_max[...] = jnp.full_like(running_max, -1e30)
    denominator[...] = jnp.zeros_like(denominator)
    weighted[...] = jnp.zeros_like(weighted)
    query_pos = (chip * 2 + c) * ROWS + lax.broadcasted_iota(jnp.int32, (1, ROWS), 1)
    starts = document_starts(lengths_ref, query_pos)

    def attend(j):
        key_pos = (chip - j) * 256 + lax.broadcasted_iota(jnp.int32, (256, ROWS), 0)
        visible = jnp.logical_and(key_pos >= starts, key_pos <= query_pos)
        bias = jnp.where(visible, 0.0, -1e30)
        bias = jnp.concatenate([bias, bias], axis=1)

        def pair(i, _):
            scores = lax.dot_general(
                keys_values[j, 0], by_head[i], (((1,), (1,)), ((), ())),
                preferred_element_type=jnp.float32,
            ) * HD ** (-0.5)
            scores = jnp.where(bias < 0.0, -1e30, scores)
            old = running_max[i]
            new = jnp.maximum(old, jnp.max(scores, axis=0, keepdims=True))
            factor = jnp.exp(old - new)
            parts = jnp.exp(scores - new)
            running_max[i] = new
            denominator[i] = denominator[i] * factor + jnp.sum(parts, axis=0, keepdims=True)
            weighted[i] = weighted[i] * factor + lax.dot_general(
                keys_values[j, 1], parts.astype(jnp.bfloat16), (((0,), (0,)), ((), ())),
                preferred_element_type=jnp.float32,
            )
            return 0

        lax.fori_loop(0, 4, pair, 0)

    def attend_step(j, _):
        @pl.when(jnp.logical_and(j < 4, chip > j))
        def _():
            kv_arrival(j + 1, c).wait_recv()

            @pl.when(jnp.logical_and(j < 3, chip < 15))
            def _():
                kv_onward(j + 1).start()

            kv_sibling(j + 1).start()

        @pl.when(jnp.logical_and(j < 4, chip <= j))
        def _():
            keys_values[j + 1] = jnp.zeros_like(keys_values[0])

        @pl.when(chip >= j)
        def _():
            kv_arrival(j, 1 - c).wait_recv()

        attend(j)
        return 0

    lax.fori_loop(0, 5, attend_step, 0)

    total = jnp.zeros((ROWS, HD), jnp.float32)
    for head in range(8):
        lanes = slice((head % 2) * ROWS, (head % 2 + 1) * ROWS)
        columns = slice(head * HD, (head + 1) * HD)
        attended = (weighted[head // 2, :, lanes] / denominator[head // 2, :, lanes]).T
        rounded = (residual_in[:, columns].astype(jnp.float32) + attended).astype(jnp.bfloat16)
        residual_ref[:, columns] = rounded
        wide = rounded.astype(jnp.float32)
        total = total + wide * wide
    squares[mp] = jnp.broadcast_to(jnp.sum(total.T, axis=0, keepdims=True), (8, ROWS))

    def square_copy(peer, i):
        view = squares.at[mp]
        return pltpu.make_async_remote_copy(
            src_ref=view, dst_ref=view, send_sem=sq_send.at[i], recv_sem=sq_recv.at[mp],
            device_id=peer, device_id_type=MESH,
        )

    mp_peers = [lo_partner] + x_peers + across
    for i, peer in enumerate(mp_peers):
        square_copy(peer, i).start()
    for i in range(1, 8):
        slot = lax.rem(mp + i, 8)
        view = squares.at[slot]
        pltpu.make_async_remote_copy(
            src_ref=view, dst_ref=view, send_sem=sq_send.at[0], recv_sem=sq_recv.at[slot],
            device_id=lo_partner, device_id_type=MESH,
        ).wait_recv()
    mean = jnp.sum(squares[...], axis=0) / D
    inverse = jnp.broadcast_to(lax.rsqrt(mean + 1e-05)[0:1], (ROWS, ROWS)).T
    for head in range(8):
        columns = slice(head * HD, (head + 1) * HD)
        normed_ref[:, columns] = (
            residual_ref[:, columns].astype(jnp.float32) * inverse * gain_ref[:, columns].astype(jnp.float32)
        ).astype(jnp.bfloat16)

    @pl.when(match)
    def _():
        tokens[yh, my_source, yl, mine] = normed_ref[...]

    @pl.when(jnp.logical_not(match))
    def _():
        cross_copy().start()

    handle(0)
    weights_arrived(0)

    def first(step, _):
        handle(step + 1)
        sibling_arrived(step)
        multiply(step, 0)
        return 0

    lax.fori_loop(0, FIRST, first, 0)
    weights_arrived(1)

    def catch_up(step, _):
        multiply(step, 1)
        return 0

    lax.fori_loop(0, FIRST, catch_up, 0)

    def second(step, _):
        @pl.when(step < 7)
        def _():
            handle(step + 1)

        sibling_arrived(step)
        multiply(step, 0)
        multiply(step, 1)
        return 0

    lax.fori_loop(FIRST, 8, second, 0)

    def finish(low, _):
        rows = pl.ds(pl.multiple_of(low * 256, 256), 256)
        totals = []
        for part in range(2):
            start, size = PARTS[part]
            columns = pl.ds(start, size)
            total = own_sum[low, :, columns]
            for slot in range(3):
                view = landed.at[slot, low, :, columns]
                pltpu.make_async_remote_copy(
                    src_ref=view, dst_ref=view, send_sem=sum_send.at[0, 0, part],
                    recv_sem=sum_recv.at[slot, low, part], device_id=x_peers[0], device_id_type=MESH,
                ).wait_recv()
                total = total + landed[slot, low, :, columns].astype(jnp.float32)
            totals.append(total)
        a, b = totals
        silu = lambda v: v / (1.0 + jnp.exp(-v))
        out_ref[rows, 0:256] = (silu(a[:, :256]) * a[:, 256:]).astype(jnp.bfloat16)
        out_ref[rows, 256:384] = (silu(b[:, :128]) * b[:, 128:256]).astype(jnp.bfloat16)
        tail = b[:, 256:384]
        mixed = silu(tail) * pltpu.roll(tail, 64, 1)
        out_ref[rows, 384:448] = mixed[:, :64].astype(jnp.bfloat16)
        return 0

    lax.fori_loop(0, 2, finish, 0)

    for j in range(5):
        if j < 4:
            @pl.when(jnp.logical_and(chip < 15, chip >= j))
            def _():
                kv_onward(j).wait_send()

        @pl.when(chip >= j)
        def _():
            kv_sibling(j).wait_send()
    for i, peer in enumerate(mp_peers):
        square_copy(peer, i).wait_send()
    for part in range(2):
        weight_copy(part).wait_send()

    @pl.when(jnp.logical_not(match))
    def _():
        cross_copy().wait_send()

    def drain(step, _):
        h, half, source, own, go_up, go_down = unit_of(step)
        for kb in range(2):
            @pl.when(go_up)
            def _():
                token_copy(h, source, kb, up_send, above).wait_send()

            @pl.when(go_down)
            def _():
                token_copy(h, source, kb, down_send, below).wait_send()

            token_copy(h, source, kb, sib_send, sibling).wait_send()

            @pl.when(jnp.logical_and(own, half == 0))
            def _():
                token_copy(h, source, kb, hi_send, hi_partner).wait_send()

        @pl.when(h * 2 + source // 2 != x)
        def _():
            for part in range(2):
                sum_copy(h, source, part, None).wait_send()
        return 0

    lax.fori_loop(0, 8, drain, 0)


def on_device(
    query_heads, key_heads, value_heads, residual_in, norm_gain, gate_weight, up_weight, doc_lengths
):
    dma = pltpu.SemaphoreType.DMA
    vmem = pl.BlockSpec(memory_space=pltpu.VMEM)
    anywhere = pl.BlockSpec(memory_space=pl.ANY)
    return pl.pallas_call(
        layer_kernel,
        out_shape=(
            jax.ShapeDtypeStruct((ROWS, KB), jnp.bfloat16),
            jax.ShapeDtypeStruct((512, 448), jnp.bfloat16),
        ),
        in_specs=[pl.BlockSpec(memory_space=pltpu.SMEM)] + [anywhere] * 4 + [vmem] + [anywhere] * 2,
        out_specs=(vmem, vmem),
        scratch_shapes=[
            pltpu.VMEM((2, 4, 2, 2 * ROWS, KB), jnp.bfloat16),
            pltpu.VMEM((2, KB, WIDTH), jnp.bfloat16),
            pltpu.VMEM((2, 4, 2 * ROWS, WIDTH), jnp.bfloat16),
            pltpu.VMEM((3, 2, 2 * ROWS, WIDTH), jnp.bfloat16),
            pltpu.VMEM((2, 2 * ROWS, WIDTH), jnp.float32),
            pltpu.VMEM((ROWS, KB), jnp.bfloat16),
            pltpu.VMEM((4, 2 * ROWS, HD), jnp.bfloat16),
            pltpu.VMEM((5, 2, 2 * ROWS, HD), jnp.bfloat16),
            pltpu.VMEM((ROWS, KB), jnp.bfloat16),
            pltpu.VMEM((2, KB, 64), jnp.bfloat16),
            pltpu.VMEM((ROWS, KB), jnp.bfloat16),
            pltpu.VMEM((8, 8, ROWS), jnp.float32),
            pltpu.VMEM((4, 1, 2 * ROWS), jnp.float32),
            pltpu.VMEM((4, 1, 2 * ROWS), jnp.float32),
            pltpu.VMEM((4, HD, 2 * ROWS), jnp.float32),
            dma((10,)), dma((4,)), dma((5,)), dma((5, 2)), dma((7,)), dma((8,)),
            dma((2,)), dma((2,)), dma((1,)), dma((2, 4, 2, 2)),
            dma((2, 4, 2)), dma((2, 4, 2)), dma((2, 4, 2)), dma((2, 4, 2)),
            dma((2, 4, 2)), dma((3, 2, 2)),
        ],
        compiler_params=pltpu.CompilerParams(
            collective_id=0, has_side_effects=True, vmem_limit_bytes=56 * 2**20
        ),
        name="layer",
    )(
        doc_lengths, query_heads, key_heads, value_heads, residual_in,
        norm_gain.reshape(1, KB), gate_weight, up_weight,
    )


def solution(mesh):
    in_specs = (
        P("ctx", "mp"),
        P("ctx", "mp"),
        P("ctx", "mp"),
        P("ctx", "mp"),
        P("mp"),
        P("mp", "ctx"),
        P("mp", "ctx"),
        P(),
    )
    out_specs = (P("ctx", "mp"), P("mp", "ctx"))
    return jax.shard_map(
        on_device, mesh=mesh, in_specs=in_specs, out_specs=out_specs, check_vma=False
    )
```

```python
import functools

import jax
import jax.numpy as jnp
from jax import lax
from jax.experimental import pallas as pl
from jax.experimental.pallas import tpu as pltpu
from jax.sharding import PartitionSpec as P

D = 8192
HD = 128
MESH = pl.DeviceIdType.MESH
ROWS = 128
KB = 1024
HALF = 448
WIDTH = 2 * HALF


def place():
    ctx = lax.axis_index("ctx")
    mp = lax.axis_index("mp")
    return ctx // 16, lax.rem(ctx // 2, 8), lax.rem(ctx, 2), mp // 2, lax.rem(mp, 2)


def device(yh, z, c, x, yl):
    return (yh * 16 + z * 2 + c, x * 2 + yl)


def pick(w, values):
    out = jnp.int32(values[0])
    for i in range(1, len(values)):
        out = jnp.where(w == i, jnp.int32(values[i]), out)
    return out


OFFSETS = ((0, 0, -1, 1), (1, -1, 2, -2), (-3, 3, -2, 2), (4, -4, 3, -3))
ONWARD_UP = ((1, 1, 1, 0), (0, 1, 0, 1), (1, 0, 1, 0), (0, 0, 0, 0))
ONWARD_DOWN = ((1, 1, 0, 1), (1, 0, 1, 0), (0, 1, 0, 1), (0, 0, 0, 0))
ORDER = ((0, 0), (1, 0), (0, 1), (1, 1), (2, 0), (2, 1), (3, 0), (3, 1))
FIRST = 4


def document_starts(lengths_ref, positions):
    starts = jnp.zeros_like(positions)
    end = jnp.int32(0)
    for i in range(lengths_ref.shape[0]):
        end = end + lengths_ref[i]
        starts = jnp.where(positions >= end, end, starts)
    return starts


def layer_kernel(
    lengths_ref, query_ref, key_ref, value_ref, residual_in_ref, gain_ref, gate_ref, up_ref,
    residual_ref, out_ref,
    tokens, weights, staged, relayed, landed, own_sum,
    query, by_head, keys_values, residual_in, normed_ref, squares,
    running_max, denominator, weighted,
    load_sem, kv_send, kv_sib_send, kv_recv, sq_send, sq_recv,
    w_send, w_recv, cross_send, tok_recv, up_send, down_send, sib_send, hi_send, relay_send, relay_recv, sum_send, sum_recv,
):
    yh, z, c, x, yl = place()
    match = lax.rem(z // 2, 2) == yl
    w = lax.rem(z - 2 * yl + 8, 4)
    my_source = (z // 4) * 2 + lax.rem(z, 2)
    sibling = device(yh, z, 1 - c, x, yl)
    lo_partner = device(yh, z, c, x, 1 - yl)
    hi_partner = device(1 - yh, z, c, x, yl)
    above = device(yh, lax.rem(z + 1, 8), c, x, yl)
    below = device(yh, lax.rem(z + 7, 8), c, x, yl)
    x_peers = [device(yh, z, c, lax.rem(x + d, 4), yl) for d in (1, 2, 3)]
    mine = pl.ds(pl.multiple_of(c * ROWS, ROWS), ROWS)

    mp = x * 2 + yl
    chip = yh * 8 + z
    step_on = lambda k: device(lax.rem((chip + 16 + k) // 8, 2), lax.rem(chip + 16 + k, 8), c, x, yl)
    after, after_two = step_on(1), step_on(2)

    loads = [
        pltpu.make_async_copy(key_ref, keys_values.at[0, 0, mine], load_sem.at[0]),
        pltpu.make_async_copy(value_ref, keys_values.at[0, 1, mine], load_sem.at[1]),
        pltpu.make_async_copy(query_ref, query, load_sem.at[2]),
        pltpu.make_async_copy(residual_in_ref, residual_in, load_sem.at[3]),
        pltpu.make_async_copy(gate_ref, weights.at[yl, pl.ds(0, HALF)], load_sem.at[4]),
        pltpu.make_async_copy(up_ref, weights.at[yl, pl.ds(HALF, HALF)], load_sem.at[5]),
    ]
    for load in loads:
        load.start()

    barrier = pltpu.get_barrier_semaphore()
    across = [device(yh, z, c, lax.rem(x + d, 4), 1 - yl) for d in (1, 2, 3)]
    peers = [sibling, lo_partner, hi_partner, above, below] + x_peers + across
    for peer in peers:
        pl.semaphore_signal(barrier, inc=1, device_id=peer, device_id_type=MESH)

    @pl.when(chip == 8)
    def _():
        pl.semaphore_signal(barrier, inc=1, device_id=step_on(-1), device_id_type=MESH)

    @pl.when(chip >= 2)
    def _():
        pl.semaphore_signal(barrier, inc=1, device_id=step_on(-2), device_id_type=MESH)

    pl.semaphore_wait(
        barrier, len(peers) + jnp.where(chip == 7, 1, 0) + jnp.where(chip <= 13, 1, 0)
    )
    for load in loads[:2]:
        load.wait()

    def kv_onward(i, j, ahead, target):
        return pltpu.make_async_remote_copy(
            src_ref=keys_values.at[j, :, mine], dst_ref=keys_values.at[j + ahead, :, mine],
            send_sem=kv_send.at[i], recv_sem=kv_recv.at[j + ahead, c],
            device_id=target, device_id_type=MESH,
        )

    def kv_sibling(j):
        view = keys_values.at[j, :, mine]
        return pltpu.make_async_remote_copy(
            src_ref=view, dst_ref=view, send_sem=kv_sib_send.at[j], recv_sem=kv_recv.at[j, c],
            device_id=sibling, device_id_type=MESH,
        )

    def kv_arrival(j, core):
        view = keys_values.at[j, :, pl.ds(pl.multiple_of(core * ROWS, ROWS), ROWS)]
        return pltpu.make_async_remote_copy(
            src_ref=view, dst_ref=view, send_sem=kv_sib_send.at[j], recv_sem=kv_recv.at[j, core],
            device_id=sibling, device_id_type=MESH,
        )

    @pl.when(chip < 15)
    def _():
        kv_onward(0, 0, 1, after).start()

    @pl.when(chip < 14)
    def _():
        kv_onward(1, 0, 2, after_two).start()

    kv_sibling(0).start()

    for load in loads[4:]:
        load.wait()

    def weight_copy(part):
        view = weights.at[yl, pl.ds(part * HALF, HALF)]
        return pltpu.make_async_remote_copy(
            src_ref=view, dst_ref=view, send_sem=w_send.at[part], recv_sem=w_recv.at[part],
            device_id=lo_partner, device_id_type=MESH,
        )

    weight_copy(0).start()

    def cross_copy():
        return pltpu.make_async_remote_copy(
            src_ref=normed_ref, dst_ref=tokens.at[yh, my_source, yl, mine],
            send_sem=cross_send.at[0], recv_sem=tok_recv.at[yh, my_source, yl, c],
            device_id=lo_partner, device_id_type=MESH,
        )

    def token_copy(h, source, kb, sems, target):
        view = tokens.at[h, source, kb, mine]
        return pltpu.make_async_remote_copy(
            src_ref=view, dst_ref=view, send_sem=sems.at[h, source, kb],
            recv_sem=tok_recv.at[h, source, kb, c], device_id=target, device_id_type=MESH,
        )

    def token_arrival(h, source, kb, core):
        view = tokens.at[h, source, kb, pl.ds(pl.multiple_of(core * ROWS, ROWS), ROWS)]
        return pltpu.make_async_remote_copy(
            src_ref=view, dst_ref=view, send_sem=sib_send.at[h, source, kb],
            recv_sem=tok_recv.at[h, source, kb, core], device_id=sibling, device_id_type=MESH,
        )

    def unit_of(step):
        unit = pick(step, [u for u, _ in ORDER])
        half = pick(step, [h for _, h in ORDER])
        table = lambda rows: pick(unit * 4 + w, [v for row in rows for v in row])
        source_z = lax.rem(z + table(OFFSETS) + 8, 8)
        source = (source_z // 4) * 2 + lax.rem(source_z, 2)
        h = lax.rem(yh + half, 2)
        own = jnp.logical_and(match, unit == 0)
        return h, half, source, own, table(ONWARD_UP) == 1, table(ONWARD_DOWN) == 1

    def order_of_blocks(i):
        return lax.rem(yl + i, 2)

    def handle(step):
        h, half, source, own, go_up, go_down = unit_of(step)
        at_home = jnp.logical_and(own, half == 0)
        for i in range(2):
            kb = order_of_blocks(i)
            if i == 0:
                @pl.when(jnp.logical_not(at_home))
                def _():
                    token_arrival(h, source, kb, c).wait_recv()
            else:
                token_arrival(h, source, kb, c).wait_recv()

            @pl.when(go_up)
            def _():
                token_copy(h, source, kb, up_send, above).start()

            @pl.when(go_down)
            def _():
                token_copy(h, source, kb, down_send, below).start()

            token_copy(h, source, kb, sib_send, sibling).start()

            @pl.when(at_home)
            def _():
                token_copy(h, source, kb, hi_send, hi_partner).start()

    def role_of(h, source):
        return lax.rem(x - (h * 2 + source // 2) + 4, 4)

    def goes_up(source, part):
        return lax.rem(source + part, 2) == 0

    def sum_copy(h, source, part):
        rows = pl.ds(part * HALF, HALF)
        slot = role_of(h, source) // 2
        low = lax.rem(source, 2)
        return pltpu.make_async_remote_copy(
            src_ref=staged.at[h, source, rows], dst_ref=landed.at[slot, low, rows],
            send_sem=sum_send.at[h, source, part], recv_sem=sum_recv.at[slot, low, part],
            device_id=device(yh, z, c, h * 2 + source // 2, yl), device_id_type=MESH,
        )

    def relay_copy(h, source, part):
        towards = lax.rem(x + jnp.where(goes_up(source, part), 1, 3), 4)
        return pltpu.make_async_remote_copy(
            src_ref=staged.at[h, source, pl.ds(part * HALF, HALF)], dst_ref=relayed.at[h, source],
            send_sem=relay_send.at[h, source, part], recv_sem=relay_recv.at[h, source],
            device_id=device(yh, z, c, towards, yl), device_id_type=MESH,
        )

    def relays(role, source, part):
        return jnp.logical_and(lax.rem(role, 2) == 1, (role == 3) == goes_up(source, part))

    def multiply(step, part):
        h, _, source, _, _, _ = unit_of(step)
        rows = pl.ds(part * HALF, HALF)
        across_k = (((1,), (1,)), ((), ()))
        product = lax.dot_general(
            weights[0, rows], tokens[h, source, 0], across_k, preferred_element_type=jnp.float32
        ) + lax.dot_general(
            weights[1, rows], tokens[h, source, 1], across_k, preferred_element_type=jnp.float32
        )
        role = role_of(h, source)

        @pl.when(role == 0)
        def _():
            own_sum[lax.rem(source, 2), rows] = product

        @pl.when(role != 0)
        def _():
            staged[h, source, rows] = product.astype(jnp.bfloat16)

        @pl.when(role == 2)
        def _():
            relay_copy(h, source, part).start()

        @pl.when(jnp.logical_and(lax.rem(role, 2) == 1, jnp.logical_not(relays(role, source, part))))
        def _():
            sum_copy(h, source, part).start()

    def add_relayed(step, part):
        h, _, source, _, _, _ = unit_of(step)
        rows = pl.ds(part * HALF, HALF)

        @pl.when(relays(role_of(h, source), source, part))
        def _():
            relay_copy(h, source, part).wait_recv()
            staged[h, source, rows] = (
                staged[h, source, rows].astype(jnp.float32) + relayed[h, source].astype(jnp.float32)
            ).astype(jnp.bfloat16)
            sum_copy(h, source, part).start()

    def sibling_arrived(step):
        h, _, source, _, _, _ = unit_of(step)
        for i in range(2):
            token_arrival(h, source, i, 1 - c).wait_recv()

    def weights_arrived(part):
        view = weights.at[1 - yl, pl.ds(part * HALF, HALF)]
        pltpu.make_async_remote_copy(
            src_ref=view, dst_ref=view, send_sem=w_send.at[part], recv_sem=w_recv.at[part],
            device_id=lo_partner, device_id_type=MESH,
        ).wait_recv()

    for load in loads[2:4]:
        load.wait()
    for head in range(8):
        by_head[head // 2, (head % 2) * ROWS:(head % 2 + 1) * ROWS] = query[:, head * HD:(head + 1) * HD]
    running_max[...] = jnp.full_like(running_max, -1e30)
    denominator[...] = jnp.zeros_like(denominator)
    weighted[...] = jnp.zeros_like(weighted)
    query_pos = (chip * 2 + c) * ROWS + lax.broadcasted_iota(jnp.int32, (1, ROWS), 1)
    starts = document_starts(lengths_ref, query_pos)

    def attend(j):
        key_pos = (chip - j) * 256 + lax.broadcasted_iota(jnp.int32, (256, ROWS), 0)
        visible = jnp.logical_and(key_pos >= starts, key_pos <= query_pos)
        bias = jnp.where(visible, 0.0, -1e30)
        bias = jnp.concatenate([bias, bias], axis=1)

        def pair(i, _):
            scores = lax.dot_general(
                keys_values[j, 0], by_head[i], (((1,), (1,)), ((), ())),
                preferred_element_type=jnp.float32,
            ) * HD ** (-0.5)
            scores = jnp.where(bias < 0.0, -1e30, scores)
            old = running_max[i]
            new = jnp.maximum(old, jnp.max(scores, axis=0, keepdims=True))
            factor = jnp.exp(old - new)
            parts = jnp.exp(scores - new)
            running_max[i] = new
            denominator[i] = denominator[i] * factor + jnp.sum(parts, axis=0, keepdims=True)
            weighted[i] = weighted[i] * factor + lax.dot_general(
                keys_values[j, 1], parts.astype(jnp.bfloat16), (((0,), (0,)), ((), ())),
                preferred_element_type=jnp.float32,
            )
            return 0

        lax.fori_loop(0, 4, pair, 0)

    def attend_step(j, _):
        @pl.when(jnp.logical_and(j < 4, chip > j))
        def _():
            kv_arrival(j + 1, c).wait_recv()

            @pl.when(jnp.logical_and(j < 2, chip < 14))
            def _():
                kv_onward(j + 2, j + 1, 2, after_two).start()

            kv_sibling(j + 1).start()

        @pl.when(jnp.logical_and(j < 4, chip <= j))
        def _():
            keys_values[j + 1] = jnp.zeros_like(keys_values[0])

        @pl.when(chip >= j)
        def _():
            kv_arrival(j, 1 - c).wait_recv()

        attend(j)
        return 0

    lax.fori_loop(0, 5, attend_step, 0)

    total = jnp.zeros((ROWS, HD), jnp.float32)
    for head in range(8):
        lanes = slice((head % 2) * ROWS, (head % 2 + 1) * ROWS)
        columns = slice(head * HD, (head + 1) * HD)
        attended = (weighted[head // 2, :, lanes] / denominator[head // 2, :, lanes]).T
        rounded = (residual_in[:, columns].astype(jnp.float32) + attended).astype(jnp.bfloat16)
        residual_ref[:, columns] = rounded
        wide = rounded.astype(jnp.float32)
        total = total + wide * wide
    squares[mp] = jnp.broadcast_to(jnp.sum(total.T, axis=0, keepdims=True), (8, ROWS))

    def square_copy(peer, i):
        view = squares.at[mp]
        return pltpu.make_async_remote_copy(
            src_ref=view, dst_ref=view, send_sem=sq_send.at[i], recv_sem=sq_recv.at[mp],
            device_id=peer, device_id_type=MESH,
        )

    mp_peers = [lo_partner] + x_peers + across
    for i, peer in enumerate(mp_peers):
        square_copy(peer, i).start()
    for i in range(1, 8):
        slot = lax.rem(mp + i, 8)
        view = squares.at[slot]
        pltpu.make_async_remote_copy(
            src_ref=view, dst_ref=view, send_sem=sq_send.at[0], recv_sem=sq_recv.at[slot],
            device_id=lo_partner, device_id_type=MESH,
        ).wait_recv()
    mean = jnp.sum(squares[...], axis=0) / D
    inverse = jnp.broadcast_to(lax.rsqrt(mean + 1e-05)[0:1], (ROWS, ROWS)).T
    for head in range(8):
        columns = slice(head * HD, (head + 1) * HD)
        normed_ref[:, columns] = (
            residual_ref[:, columns].astype(jnp.float32) * inverse * gain_ref[columns].astype(jnp.float32)[None, :]
        ).astype(jnp.bfloat16)

    @pl.when(match)
    def _():
        tokens[yh, my_source, yl, mine] = normed_ref[...]

    @pl.when(jnp.logical_not(match))
    def _():
        cross_copy().start()

    handle(0)
    weight_copy(1).start()
    weights_arrived(0)

    def first(step, _):
        handle(step + 1)
        sibling_arrived(step)
        multiply(step, 0)

        @pl.when(step > 0)
        def _():
            add_relayed(step - 1, 0)

        return 0

    lax.fori_loop(0, FIRST, first, 0)
    weights_arrived(1)

    def catch_up(step, _):
        multiply(step, 1)
        return 0

    lax.fori_loop(0, FIRST, catch_up, 0)
    add_relayed(FIRST - 1, 0)

    def catch_up_relayed(step, _):
        add_relayed(step, 1)
        return 0

    lax.fori_loop(0, FIRST - 1, catch_up_relayed, 0)

    def second(step, _):
        @pl.when(step < 7)
        def _():
            handle(step + 1)

        sibling_arrived(step)
        for part in range(2):
            multiply(step, part)

        @pl.when(step > FIRST)
        def _():
            add_relayed(step - 1, 0)

        add_relayed(step - 1, 1)
        return 0

    lax.fori_loop(FIRST, 8, second, 0)
    for part in range(2):
        add_relayed(7, part)

    for low in range(2):
        totals = []
        for part in range(2):
            rows = pl.ds(part * HALF, HALF)
            total = own_sum[low, rows]
            for slot in range(2):
                view = landed.at[slot, low, rows]
                pltpu.make_async_remote_copy(
                    src_ref=view, dst_ref=view, send_sem=sum_send.at[0, 0, part],
                    recv_sem=sum_recv.at[slot, low, part], device_id=x_peers[0], device_id_type=MESH,
                ).wait_recv()
                total = total + landed[slot, low, rows].astype(jnp.float32)
            totals.append(total)
        gate, up = totals
        out_ref[:, low * 256:(low + 1) * 256] = (gate / (1.0 + jnp.exp(-gate)) * up).astype(jnp.bfloat16)

    for i, j, ahead, target in ((0, 0, 1, after), (1, 0, 2, after_two), (2, 1, 2, after_two), (3, 2, 2, after_two)):
        @pl.when(jnp.logical_and(chip < 16 - ahead, chip >= j))
        def _():
            kv_onward(i, j, ahead, target).wait_send()
    for j in range(5):
        @pl.when(chip >= j)
        def _():
            kv_sibling(j).wait_send()
    for i, peer in enumerate(mp_peers):
        square_copy(peer, i).wait_send()
    for part in range(2):
        weight_copy(part).wait_send()

    @pl.when(jnp.logical_not(match))
    def _():
        cross_copy().wait_send()

    def drain(step, _):
        h, half, source, own, go_up, go_down = unit_of(step)
        for kb in range(2):
            @pl.when(go_up)
            def _():
                token_copy(h, source, kb, up_send, above).wait_send()

            @pl.when(go_down)
            def _():
                token_copy(h, source, kb, down_send, below).wait_send()

            token_copy(h, source, kb, sib_send, sibling).wait_send()

            @pl.when(jnp.logical_and(own, half == 0))
            def _():
                token_copy(h, source, kb, hi_send, hi_partner).wait_send()

        role = role_of(h, source)
        for part in range(2):
            @pl.when(role == 2)
            def _():
                relay_copy(h, source, part).wait_send()

            @pl.when(lax.rem(role, 2) == 1)
            def _():
                sum_copy(h, source, part).wait_send()
        return 0

    lax.fori_loop(0, 8, drain, 0)


def on_device(
    query_heads, key_heads, value_heads, residual_in, norm_gain, gate_weight, up_weight, doc_lengths
):
    dma = pltpu.SemaphoreType.DMA
    vmem = pl.BlockSpec(memory_space=pltpu.VMEM)
    anywhere = pl.BlockSpec(memory_space=pl.ANY)
    residual, hidden = pl.pallas_call(
        layer_kernel,
        out_shape=(
            jax.ShapeDtypeStruct((ROWS, KB), jnp.bfloat16),
            jax.ShapeDtypeStruct((HALF, 4 * ROWS), jnp.bfloat16),
        ),
        in_specs=[pl.BlockSpec(memory_space=pltpu.SMEM)] + [anywhere] * 4 + [vmem] + [anywhere] * 2,
        out_specs=(vmem, vmem),
        scratch_shapes=[
            pltpu.VMEM((2, 4, 2, 2 * ROWS, KB), jnp.bfloat16),
            pltpu.VMEM((2, WIDTH, KB), jnp.bfloat16),
            pltpu.VMEM((2, 4, WIDTH, 2 * ROWS), jnp.bfloat16),
            pltpu.VMEM((2, 4, HALF, 2 * ROWS), jnp.bfloat16),
            pltpu.VMEM((2, 2, WIDTH, 2 * ROWS), jnp.bfloat16),
            pltpu.VMEM((2, WIDTH, 2 * ROWS), jnp.float32),
            pltpu.VMEM((ROWS, KB), jnp.bfloat16),
            pltpu.VMEM((4, 2 * ROWS, HD), jnp.bfloat16),
            pltpu.VMEM((5, 2, 2 * ROWS, HD), jnp.bfloat16),
            pltpu.VMEM((ROWS, KB), jnp.bfloat16),
            pltpu.VMEM((ROWS, KB), jnp.bfloat16),
            pltpu.VMEM((8, 8, ROWS), jnp.float32),
            pltpu.VMEM((4, 1, 2 * ROWS), jnp.float32),
            pltpu.VMEM((4, 1, 2 * ROWS), jnp.float32),
            pltpu.VMEM((4, HD, 2 * ROWS), jnp.float32),
            dma((6,)), dma((4,)), dma((5,)), dma((5, 2)), dma((7,)), dma((8,)),
            dma((2,)), dma((2,)), dma((1,)), dma((2, 4, 2, 2)),
            dma((2, 4, 2)), dma((2, 4, 2)), dma((2, 4, 2)), dma((2, 4, 2)),
            dma((2, 4, 2)), dma((2, 4)), dma((2, 4, 2)), dma((2, 2, 2)),
        ],
        compiler_params=pltpu.CompilerParams(
            collective_id=0, has_side_effects=True, vmem_limit_bytes=56 * 2**20
        ),
        name="layer",
    )(
        doc_lengths, query_heads, key_heads, value_heads, residual_in,
        norm_gain, gate_weight.T, up_weight.T,
    )
    return residual, hidden.T


def solution(mesh):
    in_specs = (
        P("ctx", "mp"),
        P("ctx", "mp"),
        P("ctx", "mp"),
        P("ctx", "mp"),
        P("mp"),
        P("mp", "ctx"),
        P("mp", "ctx"),
        P(),
    )
    out_specs = (P("ctx", "mp"), P("mp", "ctx"))
    return jax.shard_map(
        on_device, mesh=mesh, in_specs=in_specs, out_specs=out_specs, check_vma=False
    )
```

```python
import functools

import jax
import jax.numpy as jnp
from jax import lax
from jax.experimental import pallas as pl
from jax.experimental.pallas import tpu as pltpu
from jax.sharding import PartitionSpec as P

D = 8192
HD = 128
MESH = pl.DeviceIdType.MESH
ROWS = 128
KB = 1024
HALF = 448
WIDTH = 2 * HALF


def place():
    ctx = lax.axis_index("ctx")
    mp = lax.axis_index("mp")
    return ctx // 16, lax.rem(ctx // 2, 8), lax.rem(ctx, 2), mp // 2, lax.rem(mp, 2)


def device(yh, z, c, x, yl):
    return (yh * 16 + z * 2 + c, x * 2 + yl)


def pick(w, values):
    out = jnp.int32(values[0])
    for i in range(1, len(values)):
        out = jnp.where(w == i, jnp.int32(values[i]), out)
    return out


OFFSETS = ((0, 0, -1, 1), (1, -1, 2, -2), (-3, 3, -2, 2), (4, -4, 3, -3))
ONWARD_UP = ((1, 1, 1, 0), (0, 1, 0, 1), (1, 0, 1, 0), (0, 0, 0, 0))
ONWARD_DOWN = ((1, 1, 0, 1), (1, 0, 1, 0), (0, 1, 0, 1), (0, 0, 0, 0))
EVENTS = (
    ((0, 0, 0), (0, 0, 1), (1, 0, 0), (0, 1, 0), (0, 1, 1), (1, 0, 1), (1, 1, 0), (2, 0, 0), (1, 1, 1), (2, 0, 1), (3, 0, 0), (2, 1, 0), (3, 0, 1), (2, 1, 1), (3, 1, 0), (3, 1, 1)),
    ((0, 0, 0), (0, 0, 1), (1, 0, 0), (2, 0, 0), (1, 0, 1), (0, 1, 0), (0, 1, 1), (1, 1, 0), (2, 0, 1), (1, 1, 1), (2, 1, 0), (3, 0, 0), (2, 1, 1), (3, 0, 1), (3, 1, 0), (3, 1, 1)),
)
GROUPS = (
    ((0, 0), (0, 1), (1, 0), (1, 1), (2, 0), (3, 0), (2, 1), (3, 1)),
    ((0, 0), (1, 0), (0, 1), (2, 0), (1, 1), (2, 1), (3, 0), (3, 1)),
)
BEFORE = (3, 6, 8, 10, 11, 14, 15, 16)
FIRST = 4


def document_starts(lengths_ref, positions):
    starts = jnp.zeros_like(positions)
    end = jnp.int32(0)
    for i in range(lengths_ref.shape[0]):
        end = end + lengths_ref[i]
        starts = jnp.where(positions >= end, end, starts)
    return starts


def layer_kernel(
    lengths_ref, query_ref, key_ref, value_ref, residual_in_ref, gain_ref, gate_ref, up_ref,
    residual_ref, out_ref,
    tokens, weights, staged, relayed, landed, own_sum,
    query, by_head, keys_values, residual_in, normed_ref, squares,
    running_max, denominator, weighted,
    load_sem, kv_send, kv_sib_send, kv_recv, sq_send, sq_recv,
    w_send, w_recv, cross_send, tok_recv, up_send, down_send, sib_send, hi_send, relay_send, relay_recv, sum_send, sum_recv,
):
    yh, z, c, x, yl = place()
    match = lax.rem(z // 2, 2) == yl
    w = lax.rem(z - 2 * yl + 8, 4)
    my_source = (z // 4) * 2 + lax.rem(z, 2)
    sibling = device(yh, z, 1 - c, x, yl)
    lo_partner = device(yh, z, c, x, 1 - yl)
    hi_partner = device(1 - yh, z, c, x, yl)
    above = device(yh, lax.rem(z + 1, 8), c, x, yl)
    below = device(yh, lax.rem(z + 7, 8), c, x, yl)
    x_peers = [device(yh, z, c, lax.rem(x + d, 4), yl) for d in (1, 2, 3)]
    mine = pl.ds(pl.multiple_of(c * ROWS, ROWS), ROWS)

    mp = x * 2 + yl
    chip = yh * 8 + z
    step_on = lambda k: device(lax.rem((chip + 16 + k) // 8, 2), lax.rem(chip + 16 + k, 8), c, x, yl)
    after, after_two = step_on(1), step_on(2)

    loads = [
        pltpu.make_async_copy(key_ref, keys_values.at[0, 0, mine], load_sem.at[0]),
        pltpu.make_async_copy(value_ref, keys_values.at[0, 1, mine], load_sem.at[1]),
        pltpu.make_async_copy(query_ref, query, load_sem.at[2]),
        pltpu.make_async_copy(residual_in_ref, residual_in, load_sem.at[3]),
        pltpu.make_async_copy(gate_ref, weights.at[yl, pl.ds(0, HALF)], load_sem.at[4]),
        pltpu.make_async_copy(up_ref, weights.at[yl, pl.ds(HALF, HALF)], load_sem.at[5]),
    ]
    for load in loads:
        load.start()

    barrier = pltpu.get_barrier_semaphore()
    across = [device(yh, z, c, lax.rem(x + d, 4), 1 - yl) for d in (1, 2, 3)]
    peers = [sibling, lo_partner, hi_partner, above, below] + x_peers + across
    for peer in peers:
        pl.semaphore_signal(barrier, inc=1, device_id=peer, device_id_type=MESH)

    @pl.when(chip == 8)
    def _():
        pl.semaphore_signal(barrier, inc=1, device_id=step_on(-1), device_id_type=MESH)

    @pl.when(chip >= 2)
    def _():
        pl.semaphore_signal(barrier, inc=1, device_id=step_on(-2), device_id_type=MESH)

    pl.semaphore_wait(
        barrier, len(peers) + jnp.where(chip == 7, 1, 0) + jnp.where(chip <= 13, 1, 0)
    )
    for load in loads[:2]:
        load.wait()

    def kv_onward(i, j, ahead, target):
        return pltpu.make_async_remote_copy(
            src_ref=keys_values.at[j, :, mine], dst_ref=keys_values.at[j + ahead, :, mine],
            send_sem=kv_send.at[i], recv_sem=kv_recv.at[j + ahead, c],
            device_id=target, device_id_type=MESH,
        )

    def kv_sibling(j):
        view = keys_values.at[j, :, mine]
        return pltpu.make_async_remote_copy(
            src_ref=view, dst_ref=view, send_sem=kv_sib_send.at[j], recv_sem=kv_recv.at[j, c],
            device_id=sibling, device_id_type=MESH,
        )

    def kv_arrival(j, core):
        view = keys_values.at[j, :, pl.ds(pl.multiple_of(core * ROWS, ROWS), ROWS)]
        return pltpu.make_async_remote_copy(
            src_ref=view, dst_ref=view, send_sem=kv_sib_send.at[j], recv_sem=kv_recv.at[j, core],
            device_id=sibling, device_id_type=MESH,
        )

    @pl.when(chip < 15)
    def _():
        kv_onward(0, 0, 1, after).start()

    @pl.when(chip < 14)
    def _():
        kv_onward(1, 0, 2, after_two).start()

    kv_sibling(0).start()

    for load in loads[4:]:
        load.wait()

    def weight_copy(part):
        view = weights.at[yl, pl.ds(part * HALF, HALF)]
        return pltpu.make_async_remote_copy(
            src_ref=view, dst_ref=view, send_sem=w_send.at[part], recv_sem=w_recv.at[part],
            device_id=lo_partner, device_id_type=MESH,
        )

    weight_copy(0).start()

    def cross_copy():
        return pltpu.make_async_remote_copy(
            src_ref=normed_ref, dst_ref=tokens.at[yh, my_source, yl, mine],
            send_sem=cross_send.at[0], recv_sem=tok_recv.at[yh, my_source, yl, c],
            device_id=lo_partner, device_id_type=MESH,
        )

    def token_copy(h, source, kb, sems, target):
        view = tokens.at[h, source, kb, mine]
        return pltpu.make_async_remote_copy(
            src_ref=view, dst_ref=view, send_sem=sems.at[h, source, kb],
            recv_sem=tok_recv.at[h, source, kb, c], device_id=target, device_id_type=MESH,
        )

    def token_arrival(h, source, kb, core):
        view = tokens.at[h, source, kb, pl.ds(pl.multiple_of(core * ROWS, ROWS), ROWS)]
        return pltpu.make_async_remote_copy(
            src_ref=view, dst_ref=view, send_sem=sib_send.at[h, source, kb],
            recv_sem=tok_recv.at[h, source, kb, core], device_id=sibling, device_id_type=MESH,
        )

    def by_place(step, tables):
        codes = [[u * 4 + sum(b << i for i, b in enumerate(rest)) for u, *rest in t] for t in tables]
        code = jnp.where(w < 2, pick(step, codes[0]), pick(step, codes[1]))
        return code // 4, lax.rem(code, 2), lax.rem(code // 2, 2)

    def unit_of(unit, half):
        table = lambda rows: pick(unit * 4 + w, [v for row in rows for v in row])
        source_z = lax.rem(z + table(OFFSETS) + 8, 8)
        source = (source_z // 4) * 2 + lax.rem(source_z, 2)
        return lax.rem(yh + half, 2), source, table

    def group_of(step):
        unit, half, _ = by_place(step, GROUPS)
        h, source, _ = unit_of(unit, half)
        return h, source

    def onward(unit, half, kb):
        h, source, table = unit_of(unit, half)
        own = jnp.logical_and(match, unit == 0)
        return (
            (table(ONWARD_UP) == 1, token_copy(h, source, kb, up_send, above)),
            (table(ONWARD_DOWN) == 1, token_copy(h, source, kb, down_send, below)),
            (unit >= 0, token_copy(h, source, kb, sib_send, sibling)),
            (jnp.logical_and(own, half == 0), token_copy(h, source, kb, hi_send, hi_partner)),
        )

    def handle(event):
        unit, half, block = by_place(event, EVENTS)
        h, source, _ = unit_of(unit, half)
        kb = lax.rem(yl + block, 2)
        own = jnp.logical_and(match, unit == 0)

        @pl.when(jnp.logical_not(jnp.logical_and(own, jnp.logical_and(half == 0, block == 0))))
        def _():
            token_arrival(h, source, kb, c).wait_recv()

        for wanted, copy in onward(unit, half, kb):
            @pl.when(wanted)
            def _():
                copy.start()

    def role_of(h, source):
        return lax.rem(x - (h * 2 + source // 2) + 4, 4)

    def goes_up(source, part):
        return lax.rem(source + part, 2) == 0

    def sum_copy(h, source, part):
        rows = pl.ds(part * HALF, HALF)
        slot = role_of(h, source) // 2
        low = lax.rem(source, 2)
        return pltpu.make_async_remote_copy(
            src_ref=staged.at[h, source, rows], dst_ref=landed.at[slot, low, rows],
            send_sem=sum_send.at[h, source, part], recv_sem=sum_recv.at[slot, low, part],
            device_id=device(yh, z, c, h * 2 + source // 2, yl), device_id_type=MESH,
        )

    def relay_copy(h, source, part):
        towards = lax.rem(x + jnp.where(goes_up(source, part), 1, 3), 4)
        return pltpu.make_async_remote_copy(
            src_ref=staged.at[h, source, pl.ds(part * HALF, HALF)], dst_ref=relayed.at[h, source],
            send_sem=relay_send.at[h, source, part], recv_sem=relay_recv.at[h, source],
            device_id=device(yh, z, c, towards, yl), device_id_type=MESH,
        )

    def relays(role, source, part):
        return jnp.logical_and(lax.rem(role, 2) == 1, (role == 3) == goes_up(source, part))

    def multiply(step, part):
        h, source = group_of(step)
        rows = pl.ds(part * HALF, HALF)
        across_k = (((1,), (1,)), ((), ()))
        product = lax.dot_general(
            weights[0, rows], tokens[h, source, 0], across_k, preferred_element_type=jnp.float32
        ) + lax.dot_general(
            weights[1, rows], tokens[h, source, 1], across_k, preferred_element_type=jnp.float32
        )
        role = role_of(h, source)

        @pl.when(role == 0)
        def _():
            own_sum[lax.rem(source, 2), rows] = product

        @pl.when(role != 0)
        def _():
            staged[h, source, rows] = product.astype(jnp.bfloat16)

        @pl.when(role == 2)
        def _():
            relay_copy(h, source, part).start()

        @pl.when(jnp.logical_and(lax.rem(role, 2) == 1, jnp.logical_not(relays(role, source, part))))
        def _():
            sum_copy(h, source, part).start()

    def add_relayed(step, part):
        h, source = group_of(step)
        rows = pl.ds(part * HALF, HALF)

        @pl.when(relays(role_of(h, source), source, part))
        def _():
            relay_copy(h, source, part).wait_recv()
            staged[h, source, rows] = (
                staged[h, source, rows].astype(jnp.float32) + relayed[h, source].astype(jnp.float32)
            ).astype(jnp.bfloat16)
            sum_copy(h, source, part).start()

    def sibling_arrived(step):
        h, source = group_of(step)
        for i in range(2):
            token_arrival(h, source, i, 1 - c).wait_recv()

    def weights_arrived(part):
        view = weights.at[1 - yl, pl.ds(part * HALF, HALF)]
        pltpu.make_async_remote_copy(
            src_ref=view, dst_ref=view, send_sem=w_send.at[part], recv_sem=w_recv.at[part],
            device_id=lo_partner, device_id_type=MESH,
        ).wait_recv()

    for load in loads[2:4]:
        load.wait()
    for head in range(8):
        by_head[head // 2, (head % 2) * ROWS:(head % 2 + 1) * ROWS] = query[:, head * HD:(head + 1) * HD]
    running_max[...] = jnp.full_like(running_max, -1e30)
    denominator[...] = jnp.zeros_like(denominator)
    weighted[...] = jnp.zeros_like(weighted)
    query_pos = (chip * 2 + c) * ROWS + lax.broadcasted_iota(jnp.int32, (1, ROWS), 1)
    starts = document_starts(lengths_ref, query_pos)

    def attend(j):
        key_pos = (chip - j) * 256 + lax.broadcasted_iota(jnp.int32, (256, ROWS), 0)
        visible = jnp.logical_and(key_pos >= starts, key_pos <= query_pos)
        bias = jnp.where(visible, 0.0, -1e30)
        bias = jnp.concatenate([bias, bias], axis=1)

        def pair(i, _):
            scores = lax.dot_general(
                keys_values[j, 0], by_head[i], (((1,), (1,)), ((), ())),
                preferred_element_type=jnp.float32,
            ) * HD ** (-0.5)
            scores = jnp.where(bias < 0.0, -1e30, scores)
            old = running_max[i]
            new = jnp.maximum(old, jnp.max(scores, axis=0, keepdims=True))
            factor = jnp.exp(old - new)
            parts = jnp.exp(scores - new)
            running_max[i] = new
            denominator[i] = denominator[i] * factor + jnp.sum(parts, axis=0, keepdims=True)
            weighted[i] = weighted[i] * factor + lax.dot_general(
                keys_values[j, 1], parts.astype(jnp.bfloat16), (((0,), (0,)), ((), ())),
                preferred_element_type=jnp.float32,
            )
            return 0

        lax.fori_loop(0, 4, pair, 0)

    def attend_step(j, _):
        @pl.when(jnp.logical_and(j < 4, chip > j))
        def _():
            kv_arrival(j + 1, c).wait_recv()

            @pl.when(jnp.logical_and(j < 2, chip < 14))
            def _():
                kv_onward(j + 2, j + 1, 2, after_two).start()

            kv_sibling(j + 1).start()

        @pl.when(jnp.logical_and(j < 4, chip <= j))
        def _():
            keys_values[j + 1] = jnp.zeros_like(keys_values[0])

        @pl.when(chip >= j)
        def _():
            kv_arrival(j, 1 - c).wait_recv()

        attend(j)
        return 0

    lax.fori_loop(0, 5, attend_step, 0)

    total = jnp.zeros((ROWS, HD), jnp.float32)
    for head in range(8):
        lanes = slice((head % 2) * ROWS, (head % 2 + 1) * ROWS)
        columns = slice(head * HD, (head + 1) * HD)
        attended = (weighted[head // 2, :, lanes] / denominator[head // 2, :, lanes]).T
        rounded = (residual_in[:, columns].astype(jnp.float32) + attended).astype(jnp.bfloat16)
        residual_ref[:, columns] = rounded
        wide = rounded.astype(jnp.float32)
        total = total + wide * wide
    squares[mp] = jnp.broadcast_to(jnp.sum(total.T, axis=0, keepdims=True), (8, ROWS))

    def square_copy(peer, i):
        view = squares.at[mp]
        return pltpu.make_async_remote_copy(
            src_ref=view, dst_ref=view, send_sem=sq_send.at[i], recv_sem=sq_recv.at[mp],
            device_id=peer, device_id_type=MESH,
        )

    mp_peers = [lo_partner] + x_peers + across
    for i, peer in enumerate(mp_peers):
        square_copy(peer, i).start()
    for i in range(1, 8):
        slot = lax.rem(mp + i, 8)
        view = squares.at[slot]
        pltpu.make_async_remote_copy(
            src_ref=view, dst_ref=view, send_sem=sq_send.at[0], recv_sem=sq_recv.at[slot],
            device_id=lo_partner, device_id_type=MESH,
        ).wait_recv()
    mean = jnp.sum(squares[...], axis=0) / D
    inverse = jnp.broadcast_to(lax.rsqrt(mean + 1e-05)[0:1], (ROWS, ROWS)).T
    for head in range(8):
        columns = slice(head * HD, (head + 1) * HD)
        normed_ref[:, columns] = (
            residual_ref[:, columns].astype(jnp.float32) * inverse * gain_ref[columns].astype(jnp.float32)[None, :]
        ).astype(jnp.bfloat16)

    @pl.when(match)
    def _():
        tokens[yh, my_source, yl, mine] = normed_ref[...]

    @pl.when(jnp.logical_not(match))
    def _():
        cross_copy().start()

    def handle_until(step):
        def one(event, _):
            handle(event)
            return 0

        lax.fori_loop(pick(step, (0,) + BEFORE[:-1]), pick(step, BEFORE), one, 0)

    def first(step, _):
        handle_until(step)

        @pl.when(step == 0)
        def _():
            weight_copy(1).start()
            weights_arrived(0)

        sibling_arrived(step)
        multiply(step, 0)
        return 0

    lax.fori_loop(0, FIRST, first, 0)
    weights_arrived(1)

    def catch_up(step, _):
        multiply(step, 1)
        return 0

    lax.fori_loop(0, FIRST, catch_up, 0)

    def second(step, _):
        handle_until(step)
        sibling_arrived(step)
        for part in range(2):
            multiply(step, part)
        for part in range(2):
            add_relayed(step - FIRST, part)
        return 0

    lax.fori_loop(FIRST, 8, second, 0)

    def last(step, _):
        for part in range(2):
            add_relayed(step, part)
        return 0

    lax.fori_loop(8 - FIRST, 8, last, 0)

    for low in range(2):
        totals = []
        for part in range(2):
            rows = pl.ds(part * HALF, HALF)
            total = own_sum[low, rows]
            for slot in range(2):
                view = landed.at[slot, low, rows]
                pltpu.make_async_remote_copy(
                    src_ref=view, dst_ref=view, send_sem=sum_send.at[0, 0, part],
                    recv_sem=sum_recv.at[slot, low, part], device_id=x_peers[0], device_id_type=MESH,
                ).wait_recv()
                total = total + landed[slot, low, rows].astype(jnp.float32)
            totals.append(total)
        gate, up = totals
        out_ref[:, low * 256:(low + 1) * 256] = (gate / (1.0 + jnp.exp(-gate)) * up).astype(jnp.bfloat16)

    for i, j, ahead, target in ((0, 0, 1, after), (1, 0, 2, after_two), (2, 1, 2, after_two), (3, 2, 2, after_two)):
        @pl.when(jnp.logical_and(chip < 16 - ahead, chip >= j))
        def _():
            kv_onward(i, j, ahead, target).wait_send()
    for j in range(5):
        @pl.when(chip >= j)
        def _():
            kv_sibling(j).wait_send()
    for i, peer in enumerate(mp_peers):
        square_copy(peer, i).wait_send()
    for part in range(2):
        weight_copy(part).wait_send()

    @pl.when(jnp.logical_not(match))
    def _():
        cross_copy().wait_send()

    def drain(step, _):
        unit, half = step // 2, lax.rem(step, 2)
        h, source, _ = unit_of(unit, half)
        for kb in range(2):
            for wanted, copy in onward(unit, half, kb):
                @pl.when(wanted)
                def _():
                    copy.wait_send()

        role = role_of(h, source)
        for part in range(2):
            @pl.when(role == 2)
            def _():
                relay_copy(h, source, part).wait_send()

            @pl.when(lax.rem(role, 2) == 1)
            def _():
                sum_copy(h, source, part).wait_send()
        return 0

    lax.fori_loop(0, 8, drain, 0)


def on_device(
    query_heads, key_heads, value_heads, residual_in, norm_gain, gate_weight, up_weight, doc_lengths
):
    dma = pltpu.SemaphoreType.DMA
    vmem = pl.BlockSpec(memory_space=pltpu.VMEM)
    anywhere = pl.BlockSpec(memory_space=pl.ANY)
    residual, hidden = pl.pallas_call(
        layer_kernel,
        out_shape=(
            jax.ShapeDtypeStruct((ROWS, KB), jnp.bfloat16),
            jax.ShapeDtypeStruct((HALF, 4 * ROWS), jnp.bfloat16),
        ),
        in_specs=[pl.BlockSpec(memory_space=pltpu.SMEM)] + [anywhere] * 4 + [vmem] + [anywhere] * 2,
        out_specs=(vmem, vmem),
        scratch_shapes=[
            pltpu.VMEM((2, 4, 2, 2 * ROWS, KB), jnp.bfloat16),
            pltpu.VMEM((2, WIDTH, KB), jnp.bfloat16),
            pltpu.VMEM((2, 4, WIDTH, 2 * ROWS), jnp.bfloat16),
            pltpu.VMEM((2, 4, HALF, 2 * ROWS), jnp.bfloat16),
            pltpu.VMEM((2, 2, WIDTH, 2 * ROWS), jnp.bfloat16),
            pltpu.VMEM((2, WIDTH, 2 * ROWS), jnp.float32),
            pltpu.VMEM((ROWS, KB), jnp.bfloat16),
            pltpu.VMEM((4, 2 * ROWS, HD), jnp.bfloat16),
            pltpu.VMEM((5, 2, 2 * ROWS, HD), jnp.bfloat16),
            pltpu.VMEM((ROWS, KB), jnp.bfloat16),
            pltpu.VMEM((ROWS, KB), jnp.bfloat16),
            pltpu.VMEM((8, 8, ROWS), jnp.float32),
            pltpu.VMEM((4, 1, 2 * ROWS), jnp.float32),
            pltpu.VMEM((4, 1, 2 * ROWS), jnp.float32),
            pltpu.VMEM((4, HD, 2 * ROWS), jnp.float32),
            dma((6,)), dma((4,)), dma((5,)), dma((5, 2)), dma((7,)), dma((8,)),
            dma((2,)), dma((2,)), dma((1,)), dma((2, 4, 2, 2)),
            dma((2, 4, 2)), dma((2, 4, 2)), dma((2, 4, 2)), dma((2, 4, 2)),
            dma((2, 4, 2)), dma((2, 4)), dma((2, 4, 2)), dma((2, 2, 2)),
        ],
        compiler_params=pltpu.CompilerParams(
            collective_id=0, has_side_effects=True, vmem_limit_bytes=56 * 2**20
        ),
        name="layer",
    )(
        doc_lengths, query_heads, key_heads, value_heads, residual_in,
        norm_gain, gate_weight.T, up_weight.T,
    )
    return residual, hidden.T


def solution(mesh):
    in_specs = (
        P("ctx", "mp"),
        P("ctx", "mp"),
        P("ctx", "mp"),
        P("ctx", "mp"),
        P("mp"),
        P("mp", "ctx"),
        P("mp", "ctx"),
        P(),
    )
    out_specs = (P("ctx", "mp"), P("mp", "ctx"))
    return jax.shard_map(
        on_device, mesh=mesh, in_specs=in_specs, out_specs=out_specs, check_vma=False
    )
```

```python
import functools

import jax
import jax.numpy as jnp
from jax import lax
from jax.experimental import pallas as pl
from jax.experimental.pallas import tpu as pltpu
from jax.sharding import PartitionSpec as P

D = 8192
HD = 128
MESH = pl.DeviceIdType.MESH
ROWS = 128
KB = 1024
HALF = 448
WIDTH = 2 * HALF


def place():
    ctx = lax.axis_index("ctx")
    mp = lax.axis_index("mp")
    return ctx // 16, lax.rem(ctx // 2, 8), lax.rem(ctx, 2), mp // 2, lax.rem(mp, 2)


def device(yh, z, c, x, yl):
    return (yh * 16 + z * 2 + c, x * 2 + yl)


def pick(w, values):
    out = jnp.int32(values[0])
    for i in range(1, len(values)):
        out = jnp.where(w == i, jnp.int32(values[i]), out)
    return out


OFFSETS = ((0, 0, -1, 1), (1, -1, 2, -2), (-3, 3, -2, 2), (4, -4, 3, -3))
ONWARD_UP = (
    ((1, 1, 1, 0), (0, 1, 0, 1), (1, 0, 1, 0), (0, 0, 0, 0)),
    ((1, 1, 1, 0), (0, 1, 0, 1), (1, 0, 1, 0), (0, 0, 0, 0)),
)
ONWARD_DOWN = (
    ((1, 1, 0, 1), (1, 0, 1, 0), (0, 1, 0, 1), (0, 0, 0, 0)),
    ((1, 1, 0, 1), (1, 0, 1, 0), (0, 1, 0, 1), (0, 0, 0, 0)),
)
CROSSES = ((1, 1, 0, 0), (0, 0, 0, 0), (0, 0, 0, 0), (0, 0, 0, 0))
EVENTS = (
    ((0, 0, 0), (0, 0, 1), (1, 0, 0), (0, 1, 0), (0, 1, 1), (1, 0, 1), (2, 0, 0), (1, 1, 0), (2, 0, 1), (3, 0, 0), (1, 1, 1), (2, 1, 0), (3, 0, 1), (2, 1, 1), (3, 1, 0), (3, 1, 1)),
    ((0, 0, 0), (0, 0, 1), (1, 0, 0), (2, 0, 0), (1, 0, 1), (0, 1, 0), (0, 1, 1), (1, 1, 0), (3, 0, 0), (1, 1, 1), (2, 0, 1), (2, 1, 0), (2, 1, 1), (3, 0, 1), (3, 1, 0), (3, 1, 1)),
)
GROUPS = (
    ((0, 0), (0, 1), (1, 0), (2, 0), (1, 1), (3, 0), (2, 1), (3, 1)),
    ((0, 0), (1, 0), (0, 1), (1, 1), (2, 0), (2, 1), (3, 0), (3, 1)),
)
BEFORE = (3, 6, 8, 11, 12, 14, 15, 16)
PIECES = ((0, 320, -1), (320, 128, 0), (448, 448, 0))
GATED = (0, 0, 3, 4, 5, 6, 7, 8)
UPPED = (0, 0, 0, 4, 5, 6, 7, 8)
RELAYED = (0, 0, 0, 0, 1, 2, 3, 4)


def document_starts(lengths_ref, positions):
    starts = jnp.zeros_like(positions)
    end = jnp.int32(0)
    for i in range(lengths_ref.shape[0]):
        end = end + lengths_ref[i]
        starts = jnp.where(positions >= end, end, starts)
    return starts


def layer_kernel(
    lengths_ref, query_ref, key_ref, value_ref, residual_in_ref, gain_ref, gate_ref, up_ref,
    residual_ref, out_ref,
    tokens, weights, staged, relayed, landed, own_sum,
    query, by_head, keys_values, residual_in, scaled, squares, inverse,
    running_max, denominator, weighted,
    load_sem, kv_send, kv_sib_send, kv_recv, sq_send, sq_recv, inv_send, inv_recv,
    w_send, w_recv, cross_send, tok_recv, up_send, down_send, sib_send, hi_send, relay_send, relay_recv, sum_send, sum_recv,
):
    yh, z, c, x, yl = place()
    match = lax.rem(z // 2, 2) == yl
    w = lax.rem(z - 2 * yl + 8, 4)
    my_source = (z // 4) * 2 + lax.rem(z, 2)
    sibling = device(yh, z, 1 - c, x, yl)
    lo_partner = device(yh, z, c, x, 1 - yl)
    hi_partner = device(1 - yh, z, c, x, yl)
    above = device(yh, lax.rem(z + 1, 8), c, x, yl)
    below = device(yh, lax.rem(z + 7, 8), c, x, yl)
    x_peers = [device(yh, z, c, lax.rem(x + d, 4), yl) for d in (1, 2, 3)]
    mine = pl.ds(pl.multiple_of(c * ROWS, ROWS), ROWS)

    mp = x * 2 + yl
    chip = yh * 8 + z
    step_on = lambda k: device(lax.rem((chip + 16 + k) // 8, 2), lax.rem(chip + 16 + k, 8), c, x, yl)
    kv_hops = ((0, 1, step_on(1)), (0, 2, step_on(2)), (0, 4, step_on(4)), (2, 1, step_on(1)))

    loads = [
        pltpu.make_async_copy(key_ref, keys_values.at[0, 0, mine], load_sem.at[0]),
        pltpu.make_async_copy(value_ref, keys_values.at[0, 1, mine], load_sem.at[1]),
        pltpu.make_async_copy(query_ref, query, load_sem.at[2]),
        pltpu.make_async_copy(residual_in_ref, residual_in, load_sem.at[3]),
        pltpu.make_async_copy(gate_ref, weights.at[yl, pl.ds(0, HALF)], load_sem.at[4]),
        pltpu.make_async_copy(up_ref, weights.at[yl, pl.ds(HALF, HALF)], load_sem.at[5]),
    ]
    for load in loads:
        load.start()

    barrier = pltpu.get_barrier_semaphore()
    across = [device(yh, z, c, lax.rem(x + d, 4), 1 - yl) for d in (1, 2, 3)]
    peers = [sibling, lo_partner, hi_partner, above, below] + x_peers + across
    for peer in peers:
        pl.semaphore_signal(barrier, inc=1, device_id=peer, device_id_type=MESH)

    @pl.when(chip == 8)
    def _():
        pl.semaphore_signal(barrier, inc=1, device_id=step_on(-1), device_id_type=MESH)

    for k in (2, 4):
        @pl.when(chip >= k)
        def _():
            pl.semaphore_signal(barrier, inc=1, device_id=step_on(-k), device_id_type=MESH)

    pl.semaphore_wait(
        barrier,
        len(peers) + jnp.where(chip == 7, 1, 0) + jnp.where(chip < 14, 1, 0) + jnp.where(chip < 12, 1, 0),
    )
    for load in loads[:2]:
        load.wait()

    def kv_onward(i):
        j, ahead, target = kv_hops[i]
        return pltpu.make_async_remote_copy(
            src_ref=keys_values.at[j, :, mine], dst_ref=keys_values.at[j + ahead, :, mine],
            send_sem=kv_send.at[i], recv_sem=kv_recv.at[j + ahead, c],
            device_id=target, device_id_type=MESH,
        )

    def kv_sent(i):
        j, ahead, _ = kv_hops[i]
        return jnp.logical_and(chip >= j, chip < 16 - ahead)

    def kv_sibling(j):
        view = keys_values.at[j, :, mine]
        return pltpu.make_async_remote_copy(
            src_ref=view, dst_ref=view, send_sem=kv_sib_send.at[j], recv_sem=kv_recv.at[j, c],
            device_id=sibling, device_id_type=MESH,
        )

    def kv_arrival(j, core):
        view = keys_values.at[j, :, pl.ds(pl.multiple_of(core * ROWS, ROWS), ROWS)]
        return pltpu.make_async_remote_copy(
            src_ref=view, dst_ref=view, send_sem=kv_sib_send.at[j], recv_sem=kv_recv.at[j, core],
            device_id=sibling, device_id_type=MESH,
        )

    for i in range(3):
        @pl.when(kv_sent(i))
        def _():
            kv_onward(i).start()

    kv_sibling(0).start()

    for load in loads[4:]:
        load.wait()

    def weight_copy(i):
        start, rows, _ = PIECES[i]
        view = weights.at[yl, pl.ds(start, rows)]
        return pltpu.make_async_remote_copy(
            src_ref=view, dst_ref=view, send_sem=w_send.at[i], recv_sem=w_recv.at[i],
            device_id=lo_partner, device_id_type=MESH,
        )

    for i, (_, _, when) in enumerate(PIECES):
        if when < 0:
            weight_copy(i).start()

    def cross_copy():
        return pltpu.make_async_remote_copy(
            src_ref=scaled, dst_ref=tokens.at[yh, my_source, yl, mine],
            send_sem=cross_send.at[0], recv_sem=tok_recv.at[yh, my_source, yl, c],
            device_id=lo_partner, device_id_type=MESH,
        )

    def token_copy(h, source, kb, sems, target):
        view = tokens.at[h, source, kb, mine]
        return pltpu.make_async_remote_copy(
            src_ref=view, dst_ref=view, send_sem=sems.at[h, source, kb],
            recv_sem=tok_recv.at[h, source, kb, c], device_id=target, device_id_type=MESH,
        )

    def token_arrival(h, source, kb, core):
        view = tokens.at[h, source, kb, pl.ds(pl.multiple_of(core * ROWS, ROWS), ROWS)]
        return pltpu.make_async_remote_copy(
            src_ref=view, dst_ref=view, send_sem=sib_send.at[h, source, kb],
            recv_sem=tok_recv.at[h, source, kb, core], device_id=sibling, device_id_type=MESH,
        )

    def by_place(step, tables):
        codes = [[u * 4 + sum(b << i for i, b in enumerate(rest)) for u, *rest in t] for t in tables]
        code = jnp.where(w < 2, pick(step, codes[0]), pick(step, codes[1]))
        return code // 4, lax.rem(code, 2), lax.rem(code // 2, 2)

    def unit_of(unit, half):
        table = lambda rows: pick(unit * 4 + w, [v for row in rows for v in row])
        source_z = lax.rem(z + table(OFFSETS) + 8, 8)
        source = (source_z // 4) * 2 + lax.rem(source_z, 2)
        return lax.rem(yh + half, 2), source, table

    def group_of(step):
        unit, half, _ = by_place(step, GROUPS)
        h, source, _ = unit_of(unit, half)
        return h, source

    def ways_on(unit, half):
        _, _, table = unit_of(unit, half)
        by_half = lambda tables: jnp.where(half == 0, table(tables[0]), table(tables[1])) == 1
        crosses = jnp.logical_and(table(CROSSES) == 1, half == 0)
        return by_half(ONWARD_UP), by_half(ONWARD_DOWN), unit >= 0, crosses

    def onward(unit, half, kb):
        h, source, _ = unit_of(unit, half)
        ways = ((up_send, above), (down_send, below), (sib_send, sibling), (hi_send, hi_partner))
        return [
            (wanted, token_copy(h, source, kb, sems, target))
            for wanted, (sems, target) in zip(ways_on(unit, half), ways)
        ]

    def owned_here(h, source):
        return h * 2 + source // 2 == x

    def handle(event):
        unit, half, block = by_place(event, EVENTS)
        h, source, _ = unit_of(unit, half)
        kb = lax.rem(yl + block, 2)
        own = jnp.logical_and(match, unit == 0)

        @pl.when(jnp.logical_not(jnp.logical_and(own, jnp.logical_and(half == 0, block == 0))))
        def _():
            token_arrival(h, source, kb, c).wait_recv()

        for wanted, copy in onward(unit, half, kb):
            @pl.when(wanted)
            def _():
                copy.start()

        @pl.when(jnp.logical_and(owned_here(h, source), block == 1))
        def _():
            low = lax.rem(source, 2)
            at_home = jnp.logical_and(own, half == 0)

            @pl.when(at_home)
            def _():
                squares_to_inverse()

            @pl.when(jnp.logical_not(at_home))
            def _():
                inverse_copy(low, c, 0, sibling).wait_recv()

            for wanted, copy in inverse_onward(ways_on(unit, half), low):
                @pl.when(wanted)
                def _():
                    copy.start()

    def role_of(h, source):
        return lax.rem(x - (h * 2 + source // 2) + 4, 4)

    def goes_up(source, part):
        return lax.rem(source + part, 2) == 0

    def sum_copy(h, source, part):
        rows = pl.ds(part * HALF, HALF)
        slot = role_of(h, source) // 2
        low = lax.rem(source, 2)
        return pltpu.make_async_remote_copy(
            src_ref=staged.at[h, source, rows], dst_ref=landed.at[slot, low, rows],
            send_sem=sum_send.at[h, source, part], recv_sem=sum_recv.at[slot, low, part],
            device_id=device(yh, z, c, h * 2 + source // 2, yl), device_id_type=MESH,
        )

    def relay_copy(h, source, part):
        towards = lax.rem(x + jnp.where(goes_up(source, part), 1, 3), 4)
        return pltpu.make_async_remote_copy(
            src_ref=staged.at[h, source, pl.ds(part * HALF, HALF)], dst_ref=relayed.at[h, source],
            send_sem=relay_send.at[h, source, part], recv_sem=relay_recv.at[h, source],
            device_id=device(yh, z, c, towards, yl), device_id_type=MESH,
        )

    def relays(role, source, part):
        return jnp.logical_and(lax.rem(role, 2) == 1, (role == 3) == goes_up(source, part))

    def multiply(step, part):
        h, source = group_of(step)
        rows = pl.ds(part * HALF, HALF)
        across_k = (((1,), (1,)), ((), ()))
        product = lax.dot_general(
            weights[0, rows], tokens[h, source, 0], across_k, preferred_element_type=jnp.float32
        ) + lax.dot_general(
            weights[1, rows], tokens[h, source, 1], across_k, preferred_element_type=jnp.float32
        )
        role = role_of(h, source)

        @pl.when(role == 0)
        def _():
            own_sum[lax.rem(source, 2), rows] = product

        @pl.when(role != 0)
        def _():
            staged[h, source, rows] = product.astype(jnp.bfloat16)

        @pl.when(role == 2)
        def _():
            relay_copy(h, source, part).start()

        @pl.when(jnp.logical_and(lax.rem(role, 2) == 1, jnp.logical_not(relays(role, source, part))))
        def _():
            sum_copy(h, source, part).start()

    def add_relayed(step, part):
        h, source = group_of(step)
        rows = pl.ds(part * HALF, HALF)

        @pl.when(relays(role_of(h, source), source, part))
        def _():
            relay_copy(h, source, part).wait_recv()
            staged[h, source, rows] = (
                staged[h, source, rows].astype(jnp.float32) + relayed[h, source].astype(jnp.float32)
            ).astype(jnp.bfloat16)
            sum_copy(h, source, part).start()

    def sibling_arrived(step):
        h, source = group_of(step)
        for i in range(2):
            token_arrival(h, source, i, 1 - c).wait_recv()

    owner_mp = (yh * 2 + z // 4) * 2 + lax.rem(z // 2, 2)

    def square_copy():
        view = squares.at[mp]
        return pltpu.make_async_remote_copy(
            src_ref=view, dst_ref=view, send_sem=sq_send.at[0], recv_sem=sq_recv.at[mp],
            device_id=(chip * 2 + c, owner_mp), device_id_type=MESH,
        )

    def squares_to_inverse():
        for i in range(1, 8):
            slot = lax.rem(mp + i, 8)
            view = squares.at[slot]
            pltpu.make_async_remote_copy(
                src_ref=view, dst_ref=view, send_sem=sq_send.at[0], recv_sem=sq_recv.at[slot],
                device_id=lo_partner, device_id_type=MESH,
            ).wait_recv()
        inverse[lax.rem(z, 2), c] = lax.rsqrt(jnp.sum(squares[...], axis=0) / D + 1e-05)

    def inverse_copy(low, core, way, target):
        view = inverse.at[low, core]
        return pltpu.make_async_remote_copy(
            src_ref=view, dst_ref=view, send_sem=inv_send.at[low, way], recv_sem=inv_recv.at[low, core],
            device_id=target, device_id_type=MESH,
        )

    def inverse_onward(wanted, low):
        targets = (above, below, sibling, hi_partner)
        return [(want, inverse_copy(low, c, way, target)) for way, (want, target) in enumerate(zip(wanted, targets))]

    def weights_arrived(part):
        for i, (start, rows, _) in enumerate(PIECES):
            if start // HALF == part:
                view = weights.at[1 - yl, pl.ds(start, rows)]
                pltpu.make_async_remote_copy(
                    src_ref=view, dst_ref=view, send_sem=w_send.at[i], recv_sem=w_recv.at[i],
                    device_id=lo_partner, device_id_type=MESH,
                ).wait_recv()

    for load in loads[2:4]:
        load.wait()
    for head in range(8):
        by_head[head // 2, (head % 2) * ROWS:(head % 2 + 1) * ROWS] = query[:, head * HD:(head + 1) * HD]
    running_max[...] = jnp.full_like(running_max, -1e30)
    denominator[...] = jnp.zeros_like(denominator)
    weighted[...] = jnp.zeros_like(weighted)
    query_pos = (chip * 2 + c) * ROWS + lax.broadcasted_iota(jnp.int32, (1, ROWS), 1)
    starts = document_starts(lengths_ref, query_pos)

    def attend(j):
        key_pos = (chip - j) * 256 + lax.broadcasted_iota(jnp.int32, (256, ROWS), 0)
        visible = jnp.logical_and(key_pos >= starts, key_pos <= query_pos)
        bias = jnp.where(visible, 0.0, -1e30)
        bias = jnp.concatenate([bias, bias], axis=1)

        scores = [
            lax.dot_general(
                keys_values[j, 0], by_head[i], (((1,), (1,)), ((), ())),
                preferred_element_type=jnp.float32,
            ) * HD ** (-0.5) + bias
            for i in range(4)
        ]
        olds = [running_max[i] for i in range(4)]
        news = [jnp.maximum(olds[i], jnp.max(scores[i], axis=0, keepdims=True)) for i in range(4)]
        for i in range(4):
            factor = jnp.exp(olds[i] - news[i])
            parts = jnp.exp(scores[i] - news[i])
            running_max[i] = news[i]
            denominator[i] = denominator[i] * factor + jnp.sum(parts, axis=0, keepdims=True)
            weighted[i] = weighted[i] * factor + lax.dot_general(
                keys_values[j, 1], parts.astype(jnp.bfloat16), (((0,), (0,)), ((), ())),
                preferred_element_type=jnp.float32,
            )

    def attend_step(j, _):
        @pl.when(jnp.logical_and(j < 4, chip > j))
        def _():
            kv_arrival(j + 1, c).wait_recv()

            @pl.when(jnp.logical_and(j == 1, kv_sent(3)))
            def _():
                kv_onward(3).start()

            kv_sibling(j + 1).start()

        @pl.when(jnp.logical_and(j < 4, chip <= j))
        def _():
            keys_values[j + 1] = jnp.zeros_like(keys_values[0])

        @pl.when(chip >= j)
        def _():
            kv_arrival(j, 1 - c).wait_recv()

        attend(j)
        return 0

    lax.fori_loop(0, 5, attend_step, 0)

    total = jnp.zeros((ROWS, HD), jnp.float32)
    for head in range(8):
        lanes = slice((head % 2) * ROWS, (head % 2 + 1) * ROWS)
        columns = slice(head * HD, (head + 1) * HD)
        attended = (weighted[head // 2, :, lanes] / denominator[head // 2, :, lanes]).T
        rounded = (residual_in[:, columns].astype(jnp.float32) + attended).astype(jnp.bfloat16)
        residual_ref[:, columns] = rounded
        wide = rounded.astype(jnp.float32)
        total = total + wide * wide
        scaled[:, columns] = (wide * gain_ref[columns].astype(jnp.float32)[None, :]).astype(jnp.bfloat16)

    @pl.when(match)
    def _():
        tokens[yh, my_source, yl, mine] = scaled[...]

    @pl.when(jnp.logical_not(match))
    def _():
        cross_copy().start()

    squares[mp] = jnp.broadcast_to(jnp.sum(total.T, axis=0, keepdims=True), (8, ROWS))

    @pl.when(mp != owner_mp)
    def _():
        square_copy().start()

    def handle_until(step):
        def one(event, _):
            handle(event)
            return 0

        lax.fori_loop(pick(step, (0,) + BEFORE[:-1]), pick(step, BEFORE), one, 0)

    def step_through(step, _):
        handle_until(step)
        for i, (_, _, when) in enumerate(PIECES):
            if when >= 0:
                @pl.when(step == when)
                def _():
                    weight_copy(i).start()

        def each(counts, work):
            def one(group, _):
                work(group)
                return 0

            lax.fori_loop(pick(step, (0,) + counts[:-1]), pick(step, counts), one, 0)

        def gate_group(group):
            sibling_arrived(group)
            multiply(group, 0)

        @pl.when(step == 2)
        def _():
            weights_arrived(0)

        each(GATED, gate_group)

        @pl.when(step == 3)
        def _():
            weights_arrived(1)

        each(UPPED, lambda group: multiply(group, 1))

        def relay_group(group):
            for part in range(2):
                add_relayed(group, part)

        each(RELAYED, relay_group)
        return 0

    lax.fori_loop(0, 8, step_through, 0)

    def last(step, _):
        for part in range(2):
            add_relayed(step, part)
        return 0

    lax.fori_loop(RELAYED[-1], 8, last, 0)

    for low in range(2):
        totals = []
        inverse_copy(low, 1 - c, 0, sibling).wait_recv()
        scale = jnp.concatenate([inverse[low, 0], inverse[low, 1]], axis=1)[0:1]
        for part in range(2):
            rows = pl.ds(part * HALF, HALF)
            total = own_sum[low, rows]
            for slot in range(2):
                view = landed.at[slot, low, rows]
                pltpu.make_async_remote_copy(
                    src_ref=view, dst_ref=view, send_sem=sum_send.at[0, 0, part],
                    recv_sem=sum_recv.at[slot, low, part], device_id=x_peers[0], device_id_type=MESH,
                ).wait_recv()
                total = total + landed[slot, low, rows].astype(jnp.float32)
            totals.append(total * scale)
        gate, up = totals
        out_ref[:, low * 256:(low + 1) * 256] = (gate / (1.0 + jnp.exp(-gate)) * up).astype(jnp.bfloat16)

    for i in range(4):
        @pl.when(kv_sent(i))
        def _():
            kv_onward(i).wait_send()
    for j in range(5):
        @pl.when(chip >= j)
        def _():
            kv_sibling(j).wait_send()

    @pl.when(mp != owner_mp)
    def _():
        square_copy().wait_send()

    for i in range(len(PIECES)):
        weight_copy(i).wait_send()

    @pl.when(jnp.logical_not(match))
    def _():
        cross_copy().wait_send()

    def drain(step, _):
        unit, half = step // 2, lax.rem(step, 2)
        h, source, _ = unit_of(unit, half)
        for kb in range(2):
            for wanted, copy in onward(unit, half, kb):
                @pl.when(wanted)
                def _():
                    copy.wait_send()

        @pl.when(owned_here(h, source))
        def _():
            for wanted, copy in inverse_onward(ways_on(unit, half), lax.rem(source, 2)):
                @pl.when(wanted)
                def _():
                    copy.wait_send()

        role = role_of(h, source)
        for part in range(2):
            @pl.when(role == 2)
            def _():
                relay_copy(h, source, part).wait_send()

            @pl.when(lax.rem(role, 2) == 1)
            def _():
                sum_copy(h, source, part).wait_send()
        return 0

    lax.fori_loop(0, 8, drain, 0)


def on_device(
    query_heads, key_heads, value_heads, residual_in, norm_gain, gate_weight, up_weight, doc_lengths
):
    dma = pltpu.SemaphoreType.DMA
    vmem = pl.BlockSpec(memory_space=pltpu.VMEM)
    anywhere = pl.BlockSpec(memory_space=pl.ANY)
    residual, hidden = pl.pallas_call(
        layer_kernel,
        out_shape=(
            jax.ShapeDtypeStruct((ROWS, KB), jnp.bfloat16),
            jax.ShapeDtypeStruct((HALF, 4 * ROWS), jnp.bfloat16),
        ),
        in_specs=[pl.BlockSpec(memory_space=pltpu.SMEM)] + [anywhere] * 4 + [vmem] + [anywhere] * 2,
        out_specs=(vmem, vmem),
        scratch_shapes=[
            pltpu.VMEM((2, 4, 2, 2 * ROWS, KB), jnp.bfloat16),
            pltpu.VMEM((2, WIDTH, KB), jnp.bfloat16),
            pltpu.VMEM((2, 4, WIDTH, 2 * ROWS), jnp.bfloat16),
            pltpu.VMEM((2, 4, HALF, 2 * ROWS), jnp.bfloat16),
            pltpu.VMEM((2, 2, WIDTH, 2 * ROWS), jnp.bfloat16),
            pltpu.VMEM((2, WIDTH, 2 * ROWS), jnp.float32),
            pltpu.VMEM((ROWS, KB), jnp.bfloat16),
            pltpu.VMEM((4, 2 * ROWS, HD), jnp.bfloat16),
            pltpu.VMEM((5, 2, 2 * ROWS, HD), jnp.bfloat16),
            pltpu.VMEM((ROWS, KB), jnp.bfloat16),
            pltpu.VMEM((ROWS, KB), jnp.bfloat16),
            pltpu.VMEM((8, 8, ROWS), jnp.float32),
            pltpu.VMEM((2, 2, 8, ROWS), jnp.float32),
            pltpu.VMEM((4, 1, 2 * ROWS), jnp.float32),
            pltpu.VMEM((4, 1, 2 * ROWS), jnp.float32),
            pltpu.VMEM((4, HD, 2 * ROWS), jnp.float32),
            dma((6,)), dma((4,)), dma((5,)), dma((5, 2)), dma((1,)), dma((8,)), dma((2, 4)), dma((2, 2)),
            dma((3,)), dma((3,)), dma((1,)), dma((2, 4, 2, 2)),
            dma((2, 4, 2)), dma((2, 4, 2)), dma((2, 4, 2)), dma((2, 4, 2)),
            dma((2, 4, 2)), dma((2, 4)), dma((2, 4, 2)), dma((2, 2, 2)),
        ],
        compiler_params=pltpu.CompilerParams(
            collective_id=0, has_side_effects=True, vmem_limit_bytes=56 * 2**20
        ),
        name="layer",
    )(
        doc_lengths, query_heads, key_heads, value_heads, residual_in,
        norm_gain, gate_weight.T, up_weight.T,
    )
    return residual, hidden.T


def solution(mesh):
    in_specs = (
        P("ctx", "mp"),
        P("ctx", "mp"),
        P("ctx", "mp"),
        P("ctx", "mp"),
        P("mp"),
        P("mp", "ctx"),
        P("mp", "ctx"),
        P(),
    )
    out_specs = (P("ctx", "mp"), P("mp", "ctx"))
    return jax.shard_map(
        on_device, mesh=mesh, in_specs=in_specs, out_specs=out_specs, check_vma=False
    )
```

```python
import functools

import jax
import jax.numpy as jnp
from jax import lax
from jax.experimental import pallas as pl
from jax.experimental.pallas import tpu as pltpu
from jax.sharding import PartitionSpec as P

D = 8192
HD = 128
MESH = pl.DeviceIdType.MESH
ROWS = 128
KB = 1024
HALF = 448
WIDTH = 2 * HALF
QUARTER = HALF // 2


def place():
    ctx = lax.axis_index("ctx")
    mp = lax.axis_index("mp")
    return ctx // 16, lax.rem(ctx // 2, 8), lax.rem(ctx, 2), mp // 2, lax.rem(mp, 2)


def device(yh, z, c, x, yl):
    return (yh * 16 + z * 2 + c, x * 2 + yl)


def pick(w, values):
    out = jnp.int32(values[0])
    for i in range(1, len(values)):
        out = jnp.where(w == i, jnp.int32(values[i]), out)
    return out


OFFSETS = ((0, 0, -1, 1), (1, -1, 2, -2), (-3, 3, -2, 2), (4, -4, 3, -3))
ONWARD_UP = (
    ((1, 1, 1, 0), (0, 1, 0, 1), (1, 0, 1, 0), (0, 0, 0, 0)),
    ((1, 1, 1, 0), (0, 1, 0, 1), (1, 0, 1, 0), (0, 0, 0, 0)),
)
ONWARD_DOWN = (
    ((1, 1, 0, 1), (1, 0, 1, 0), (0, 1, 0, 1), (0, 0, 0, 0)),
    ((1, 1, 0, 1), (1, 0, 1, 0), (0, 1, 0, 1), (0, 0, 0, 0)),
)
CROSSES = ((1, 1, 0, 0), (0, 0, 0, 0), (0, 0, 0, 0), (0, 0, 0, 0))
EVENTS = (
    ((0, 0, 0), (0, 0, 1), (1, 0, 0), (0, 1, 0), (0, 1, 1), (1, 0, 1), (2, 0, 0), (1, 1, 0), (2, 0, 1), (3, 0, 0), (1, 1, 1), (2, 1, 0), (3, 0, 1), (2, 1, 1), (3, 1, 0), (3, 1, 1)),
    ((0, 0, 0), (0, 0, 1), (1, 0, 0), (2, 0, 0), (1, 0, 1), (0, 1, 0), (0, 1, 1), (1, 1, 0), (3, 0, 0), (1, 1, 1), (2, 0, 1), (2, 1, 0), (2, 1, 1), (3, 0, 1), (3, 1, 0), (3, 1, 1)),
)
GROUPS = (
    ((0, 0), (0, 1), (1, 0), (2, 0), (1, 1), (3, 0), (2, 1), (3, 1)),
    ((0, 0), (1, 0), (0, 1), (1, 1), (2, 0), (2, 1), (3, 0), (3, 1)),
)
BEFORE = (3, 6, 8, 11, 12, 14, 15, 16)
PIECES = ((0, 320, -1), (320, 128, 0), (448, 448, 0))
GATED = (0, 0, 3, 4, 5, 6, 7, 8)
UPPED = (0, 0, 0, 4, 5, 6, 7, 8)
RELAYED = (0, 0, 0, 0, 1, 2, 3, 4)


def document_starts(lengths_ref, positions):
    starts = jnp.zeros_like(positions)
    end = jnp.int32(0)
    for i in range(lengths_ref.shape[0]):
        end = end + lengths_ref[i]
        starts = jnp.where(positions >= end, end, starts)
    return starts


def layer_kernel(
    lengths_ref, query_ref, key_ref, value_ref, residual_in_ref, gain_ref, gate_ref, up_ref,
    residual_ref, out_ref,
    tokens, weights, staged, relayed, landed, own_sum,
    query, by_head, keys_values, residual_in, scaled, squares, inverse,
    running_max, denominator, weighted,
    load_sem, kv_send, kv_sib_send, kv_recv, sq_send, sq_recv, inv_send, inv_recv,
    w_send, w_recv, cross_send, tok_recv, up_send, down_send, sib_send, hi_send, relay_send, relay_recv, sum_send, sum_recv,
):
    yh, z, c, x, yl = place()
    match = lax.rem(z // 2, 2) == yl
    w = lax.rem(z - 2 * yl + 8, 4)
    my_source = (z // 4) * 2 + lax.rem(z, 2)
    sibling = device(yh, z, 1 - c, x, yl)
    lo_partner = device(yh, z, c, x, 1 - yl)
    hi_partner = device(1 - yh, z, c, x, yl)
    above = device(yh, lax.rem(z + 1, 8), c, x, yl)
    below = device(yh, lax.rem(z + 7, 8), c, x, yl)
    x_peers = [device(yh, z, c, lax.rem(x + d, 4), yl) for d in (1, 2, 3)]
    mine = pl.ds(pl.multiple_of(c * ROWS, ROWS), ROWS)

    mp = x * 2 + yl
    chip = yh * 8 + z
    step_on = lambda k: device(lax.rem((chip + 16 + k) // 8, 2), lax.rem(chip + 16 + k, 8), c, x, yl)
    kv_hops = ((0, 1, step_on(1)), (0, 2, step_on(2)), (0, 4, step_on(4)), (2, 1, step_on(1)))

    loads = [
        pltpu.make_async_copy(key_ref, keys_values.at[0, 0, mine], load_sem.at[0]),
        pltpu.make_async_copy(value_ref, keys_values.at[0, 1, mine], load_sem.at[1]),
        pltpu.make_async_copy(query_ref, query, load_sem.at[2]),
        pltpu.make_async_copy(residual_in_ref, residual_in, load_sem.at[3]),
        pltpu.make_async_copy(gate_ref, weights.at[yl, pl.ds(0, HALF)], load_sem.at[4]),
        pltpu.make_async_copy(up_ref, weights.at[yl, pl.ds(HALF, HALF)], load_sem.at[5]),
    ]
    for load in loads:
        load.start()

    barrier = pltpu.get_barrier_semaphore()
    across = [device(yh, z, c, lax.rem(x + d, 4), 1 - yl) for d in (1, 2, 3)]
    peers = [sibling, lo_partner, hi_partner, above, below] + x_peers + across
    for peer in peers:
        pl.semaphore_signal(barrier, inc=1, device_id=peer, device_id_type=MESH)

    @pl.when(chip == 8)
    def _():
        pl.semaphore_signal(barrier, inc=1, device_id=step_on(-1), device_id_type=MESH)

    for k in (2, 4):
        @pl.when(chip >= k)
        def _():
            pl.semaphore_signal(barrier, inc=1, device_id=step_on(-k), device_id_type=MESH)

    pl.semaphore_wait(
        barrier,
        len(peers) + jnp.where(chip == 7, 1, 0) + jnp.where(chip < 14, 1, 0) + jnp.where(chip < 12, 1, 0),
    )
    for load in loads[:2]:
        load.wait()

    def kv_onward(i):
        j, ahead, target = kv_hops[i]
        return pltpu.make_async_remote_copy(
            src_ref=keys_values.at[j, :, mine], dst_ref=keys_values.at[j + ahead, :, mine],
            send_sem=kv_send.at[i], recv_sem=kv_recv.at[j + ahead, c],
            device_id=target, device_id_type=MESH,
        )

    def kv_sent(i):
        j, ahead, _ = kv_hops[i]
        return jnp.logical_and(chip >= j, chip < 16 - ahead)

    def kv_sibling(j):
        view = keys_values.at[j, :, mine]
        return pltpu.make_async_remote_copy(
            src_ref=view, dst_ref=view, send_sem=kv_sib_send.at[j], recv_sem=kv_recv.at[j, c],
            device_id=sibling, device_id_type=MESH,
        )

    def kv_arrival(j, core):
        view = keys_values.at[j, :, pl.ds(pl.multiple_of(core * ROWS, ROWS), ROWS)]
        return pltpu.make_async_remote_copy(
            src_ref=view, dst_ref=view, send_sem=kv_sib_send.at[j], recv_sem=kv_recv.at[j, core],
            device_id=sibling, device_id_type=MESH,
        )

    for i in range(3):
        @pl.when(kv_sent(i))
        def _():
            kv_onward(i).start()

    kv_sibling(0).start()

    for load in loads[4:]:
        load.wait()

    def weight_copy(i):
        start, rows, _ = PIECES[i]
        view = weights.at[yl, pl.ds(start, rows)]
        return pltpu.make_async_remote_copy(
            src_ref=view, dst_ref=view, send_sem=w_send.at[i], recv_sem=w_recv.at[i],
            device_id=lo_partner, device_id_type=MESH,
        )

    for i, (_, _, when) in enumerate(PIECES):
        if when < 0:
            weight_copy(i).start()

    def cross_copy():
        return pltpu.make_async_remote_copy(
            src_ref=scaled, dst_ref=tokens.at[yh, my_source, yl, mine],
            send_sem=cross_send.at[0], recv_sem=tok_recv.at[yh, my_source, yl, c],
            device_id=lo_partner, device_id_type=MESH,
        )

    def token_copy(h, source, kb, sems, target):
        view = tokens.at[h, source, kb, mine]
        return pltpu.make_async_remote_copy(
            src_ref=view, dst_ref=view, send_sem=sems.at[h, source, kb],
            recv_sem=tok_recv.at[h, source, kb, c], device_id=target, device_id_type=MESH,
        )

    def token_arrival(h, source, kb, core):
        view = tokens.at[h, source, kb, pl.ds(pl.multiple_of(core * ROWS, ROWS), ROWS)]
        return pltpu.make_async_remote_copy(
            src_ref=view, dst_ref=view, send_sem=sib_send.at[h, source, kb],
            recv_sem=tok_recv.at[h, source, kb, core], device_id=sibling, device_id_type=MESH,
        )

    def by_place(step, tables):
        codes = [[u * 4 + sum(b << i for i, b in enumerate(rest)) for u, *rest in t] for t in tables]
        code = jnp.where(w < 2, pick(step, codes[0]), pick(step, codes[1]))
        return code // 4, lax.rem(code, 2), lax.rem(code // 2, 2)

    def unit_of(unit, half):
        table = lambda rows: pick(unit * 4 + w, [v for row in rows for v in row])
        source_z = lax.rem(z + table(OFFSETS) + 8, 8)
        source = (source_z // 4) * 2 + lax.rem(source_z, 2)
        return lax.rem(yh + half, 2), source, table

    def group_of(step):
        unit, half, _ = by_place(step, GROUPS)
        h, source, _ = unit_of(unit, half)
        return h, source

    def ways_on(unit, half):
        _, _, table = unit_of(unit, half)
        by_half = lambda tables: jnp.where(half == 0, table(tables[0]), table(tables[1])) == 1
        crosses = jnp.logical_and(table(CROSSES) == 1, half == 0)
        return by_half(ONWARD_UP), by_half(ONWARD_DOWN), unit >= 0, crosses

    def onward(unit, half, kb):
        h, source, _ = unit_of(unit, half)
        ways = ((up_send, above), (down_send, below), (sib_send, sibling), (hi_send, hi_partner))
        return [
            (wanted, token_copy(h, source, kb, sems, target))
            for wanted, (sems, target) in zip(ways_on(unit, half), ways)
        ]

    def owned_here(h, source):
        return h * 2 + source // 2 == x

    def handle(event):
        unit, half, block = by_place(event, EVENTS)
        h, source, _ = unit_of(unit, half)
        kb = lax.rem(yl + block, 2)
        own = jnp.logical_and(match, unit == 0)

        @pl.when(jnp.logical_not(jnp.logical_and(own, jnp.logical_and(half == 0, block == 0))))
        def _():
            token_arrival(h, source, kb, c).wait_recv()

        for wanted, copy in onward(unit, half, kb):
            @pl.when(wanted)
            def _():
                copy.start()

        @pl.when(jnp.logical_and(owned_here(h, source), block == 1))
        def _():
            low = lax.rem(source, 2)
            at_home = jnp.logical_and(own, half == 0)

            @pl.when(at_home)
            def _():
                squares_to_inverse()

            @pl.when(jnp.logical_not(at_home))
            def _():
                inverse_copy(low, c, 0, sibling).wait_recv()

            for wanted, copy in inverse_onward(ways_on(unit, half), low):
                @pl.when(wanted)
                def _():
                    copy.start()

    def role_of(h, source):
        return lax.rem(x - (h * 2 + source // 2) + 4, 4)

    def goes_up(source, part):
        return lax.rem(source + part, 2) == 0

    def sum_copy(h, source, quarter):
        rows = pl.ds(quarter * QUARTER, QUARTER)
        slot = role_of(h, source) // 2
        low = lax.rem(source, 2)
        return pltpu.make_async_remote_copy(
            src_ref=staged.at[h, source, rows], dst_ref=landed.at[slot, low, rows],
            send_sem=sum_send.at[h, source, quarter], recv_sem=sum_recv.at[slot, low, quarter],
            device_id=device(yh, z, c, h * 2 + source // 2, yl), device_id_type=MESH,
        )

    def relay_copy(h, source, quarter):
        towards = lax.rem(x + jnp.where(goes_up(source, quarter // 2), 1, 3), 4)
        return pltpu.make_async_remote_copy(
            src_ref=staged.at[h, source, pl.ds(quarter * QUARTER, QUARTER)],
            dst_ref=relayed.at[h, source, quarter % 2],
            send_sem=relay_send.at[h, source, quarter], recv_sem=relay_recv.at[h, source, quarter % 2],
            device_id=device(yh, z, c, towards, yl), device_id_type=MESH,
        )

    def relays(role, source, part):
        return jnp.logical_and(lax.rem(role, 2) == 1, (role == 3) == goes_up(source, part))

    def multiply(step, part):
        h, source = group_of(step)
        rows = pl.ds(part * HALF, HALF)
        across_k = (((1,), (1,)), ((), ()))
        product = lax.dot_general(
            weights[0, rows], tokens[h, source, 0], across_k, preferred_element_type=jnp.float32
        ) + lax.dot_general(
            weights[1, rows], tokens[h, source, 1], across_k, preferred_element_type=jnp.float32
        )
        role = role_of(h, source)

        @pl.when(role == 0)
        def _():
            own_sum[lax.rem(source, 2), rows] = product

        @pl.when(role != 0)
        def _():
            staged[h, source, rows] = product.astype(jnp.bfloat16)

        @pl.when(role == 2)
        def _():
            for quarter in (2 * part, 2 * part + 1):
                relay_copy(h, source, quarter).start()

        @pl.when(jnp.logical_and(lax.rem(role, 2) == 1, jnp.logical_not(relays(role, source, part))))
        def _():
            for quarter in (2 * part, 2 * part + 1):
                sum_copy(h, source, quarter).start()

    def add_relayed(step, part):
        h, source = group_of(step)

        @pl.when(relays(role_of(h, source), source, part))
        def _():
            for quarter in (2 * part, 2 * part + 1):
                rows = pl.ds(quarter * QUARTER, QUARTER)
                relay_copy(h, source, quarter).wait_recv()
                staged[h, source, rows] = (
                    staged[h, source, rows].astype(jnp.float32)
                    + relayed[h, source, quarter % 2].astype(jnp.float32)
                ).astype(jnp.bfloat16)
                sum_copy(h, source, quarter).start()

    def sibling_arrived(step):
        h, source = group_of(step)
        for i in range(2):
            token_arrival(h, source, i, 1 - c).wait_recv()

    owner_mp = (yh * 2 + z // 4) * 2 + lax.rem(z // 2, 2)

    def square_copy():
        view = squares.at[mp]
        return pltpu.make_async_remote_copy(
            src_ref=view, dst_ref=view, send_sem=sq_send.at[0], recv_sem=sq_recv.at[mp],
            device_id=(chip * 2 + c, owner_mp), device_id_type=MESH,
        )

    def squares_to_inverse():
        for i in range(1, 8):
            slot = lax.rem(mp + i, 8)
            view = squares.at[slot]
            pltpu.make_async_remote_copy(
                src_ref=view, dst_ref=view, send_sem=sq_send.at[0], recv_sem=sq_recv.at[slot],
                device_id=lo_partner, device_id_type=MESH,
            ).wait_recv()
        inverse[lax.rem(z, 2), c] = lax.rsqrt(jnp.sum(squares[...], axis=0) / D + 1e-05)

    def inverse_copy(low, core, way, target):
        view = inverse.at[low, core]
        return pltpu.make_async_remote_copy(
            src_ref=view, dst_ref=view, send_sem=inv_send.at[low, way], recv_sem=inv_recv.at[low, core],
            device_id=target, device_id_type=MESH,
        )

    def inverse_onward(wanted, low):
        targets = (above, below, sibling, hi_partner)
        return [(want, inverse_copy(low, c, way, target)) for way, (want, target) in enumerate(zip(wanted, targets))]

    def weights_arrived(part):
        for i, (start, rows, _) in enumerate(PIECES):
            if start // HALF == part:
                view = weights.at[1 - yl, pl.ds(start, rows)]
                pltpu.make_async_remote_copy(
                    src_ref=view, dst_ref=view, send_sem=w_send.at[i], recv_sem=w_recv.at[i],
                    device_id=lo_partner, device_id_type=MESH,
                ).wait_recv()

    for load in loads[2:4]:
        load.wait()
    for head in range(8):
        by_head[head // 2, (head % 2) * ROWS:(head % 2 + 1) * ROWS] = query[:, head * HD:(head + 1) * HD]
    running_max[...] = jnp.full_like(running_max, -1e30)
    denominator[...] = jnp.zeros_like(denominator)
    weighted[...] = jnp.zeros_like(weighted)
    query_pos = (chip * 2 + c) * ROWS + lax.broadcasted_iota(jnp.int32, (1, ROWS), 1)
    starts = document_starts(lengths_ref, query_pos)

    def attend(j):
        key_pos = (chip - j) * 256 + lax.broadcasted_iota(jnp.int32, (256, ROWS), 0)
        visible = jnp.logical_and(key_pos >= starts, key_pos <= query_pos)
        bias = jnp.where(visible, 0.0, -1e30)
        bias = jnp.concatenate([bias, bias], axis=1)

        scores = [
            lax.dot_general(
                keys_values[j, 0], by_head[i], (((1,), (1,)), ((), ())),
                preferred_element_type=jnp.float32,
            ) * HD ** (-0.5) + bias
            for i in range(4)
        ]
        olds = [running_max[i] for i in range(4)]
        news = [jnp.maximum(olds[i], jnp.max(scores[i], axis=0, keepdims=True)) for i in range(4)]
        for i in range(4):
            factor = jnp.exp(olds[i] - news[i])
            parts = jnp.exp(scores[i] - news[i])
            running_max[i] = news[i]
            denominator[i] = denominator[i] * factor + jnp.sum(parts, axis=0, keepdims=True)
            weighted[i] = weighted[i] * factor + lax.dot_general(
                keys_values[j, 1], parts.astype(jnp.bfloat16), (((0,), (0,)), ((), ())),
                preferred_element_type=jnp.float32,
            )

    def attend_step(j, _):
        @pl.when(jnp.logical_and(j < 4, chip > j))
        def _():
            kv_arrival(j + 1, c).wait_recv()

            @pl.when(jnp.logical_and(j == 1, kv_sent(3)))
            def _():
                kv_onward(3).start()

            kv_sibling(j + 1).start()

        @pl.when(jnp.logical_and(j < 4, chip <= j))
        def _():
            keys_values[j + 1] = jnp.zeros_like(keys_values[0])

        @pl.when(chip >= j)
        def _():
            kv_arrival(j, 1 - c).wait_recv()

        attend(j)
        return 0

    lax.fori_loop(0, 5, attend_step, 0)

    total = jnp.zeros((ROWS, HD), jnp.float32)
    for head in range(8):
        lanes = slice((head % 2) * ROWS, (head % 2 + 1) * ROWS)
        columns = slice(head * HD, (head + 1) * HD)
        attended = (weighted[head // 2, :, lanes] / denominator[head // 2, :, lanes]).T
        rounded = (residual_in[:, columns].astype(jnp.float32) + attended).astype(jnp.bfloat16)
        residual_ref[:, columns] = rounded
        wide = rounded.astype(jnp.float32)
        total = total + wide * wide
        scaled[:, columns] = (wide * gain_ref[columns].astype(jnp.float32)[None, :]).astype(jnp.bfloat16)

    @pl.when(match)
    def _():
        tokens[yh, my_source, yl, mine] = scaled[...]

    @pl.when(jnp.logical_not(match))
    def _():
        cross_copy().start()

    squares[mp] = jnp.broadcast_to(jnp.sum(total.T, axis=0, keepdims=True), (8, ROWS))

    @pl.when(mp != owner_mp)
    def _():
        square_copy().start()

    def handle_until(step):
        def one(event, _):
            handle(event)
            return 0

        lax.fori_loop(pick(step, (0,) + BEFORE[:-1]), pick(step, BEFORE), one, 0)

    def step_through(step, _):
        handle_until(step)
        for i, (_, _, when) in enumerate(PIECES):
            if when >= 0:
                @pl.when(step == when)
                def _():
                    weight_copy(i).start()

        def each(counts, work):
            def one(group, _):
                work(group)
                return 0

            lax.fori_loop(pick(step, (0,) + counts[:-1]), pick(step, counts), one, 0)

        def gate_group(group):
            sibling_arrived(group)
            multiply(group, 0)

        @pl.when(step == 2)
        def _():
            weights_arrived(0)

        each(GATED, gate_group)

        @pl.when(step == 3)
        def _():
            weights_arrived(1)

        each(UPPED, lambda group: multiply(group, 1))

        def relay_group(group):
            for part in range(2):
                add_relayed(group, part)

        each(RELAYED, relay_group)
        return 0

    lax.fori_loop(0, 8, step_through, 0)

    def last(step, _):
        for part in range(2):
            add_relayed(step, part)
        return 0

    lax.fori_loop(RELAYED[-1], 8, last, 0)

    for low in range(2):
        inverse_copy(low, 1 - c, 0, sibling).wait_recv()
        scale = jnp.concatenate([inverse[low, 0], inverse[low, 1]], axis=1)[0:1]
        def total_of(quarter):
            rows = pl.ds(quarter * QUARTER, QUARTER)
            total = own_sum[low, rows]
            for slot in range(2):
                view = landed.at[slot, low, rows]
                pltpu.make_async_remote_copy(
                    src_ref=view, dst_ref=view, send_sem=sum_send.at[0, 0, quarter],
                    recv_sem=sum_recv.at[slot, low, quarter], device_id=x_peers[0], device_id_type=MESH,
                ).wait_recv()
                total = total + landed[slot, low, rows].astype(jnp.float32)
            return total * scale

        for i in range(2):
            gate, up = total_of(i), total_of(2 + i)
            out_ref[i * QUARTER:(i + 1) * QUARTER, low * 256:(low + 1) * 256] = (
                gate / (1.0 + jnp.exp(-gate)) * up
            ).astype(jnp.bfloat16)

    for i in range(4):
        @pl.when(kv_sent(i))
        def _():
            kv_onward(i).wait_send()
    for j in range(5):
        @pl.when(chip >= j)
        def _():
            kv_sibling(j).wait_send()

    @pl.when(mp != owner_mp)
    def _():
        square_copy().wait_send()

    for i in range(len(PIECES)):
        weight_copy(i).wait_send()

    @pl.when(jnp.logical_not(match))
    def _():
        cross_copy().wait_send()

    def drain(step, _):
        unit, half = step // 2, lax.rem(step, 2)
        h, source, _ = unit_of(unit, half)
        for kb in range(2):
            for wanted, copy in onward(unit, half, kb):
                @pl.when(wanted)
                def _():
                    copy.wait_send()

        @pl.when(owned_here(h, source))
        def _():
            for wanted, copy in inverse_onward(ways_on(unit, half), lax.rem(source, 2)):
                @pl.when(wanted)
                def _():
                    copy.wait_send()

        role = role_of(h, source)
        for quarter in range(4):
            @pl.when(role == 2)
            def _():
                relay_copy(h, source, quarter).wait_send()

            @pl.when(lax.rem(role, 2) == 1)
            def _():
                sum_copy(h, source, quarter).wait_send()
        return 0

    lax.fori_loop(0, 8, drain, 0)


def hand_over_kernel(residual_ref, hidden_ref, residual_out, hidden_out, sems):
    copies = (
        pltpu.make_async_copy(residual_ref, residual_out, sems.at[0]),
        pltpu.make_async_copy(hidden_ref, hidden_out, sems.at[1]),
    )
    for copy in copies:
        copy.start()
    for copy in copies:
        copy.wait()


def on_device(
    query_heads, key_heads, value_heads, residual_in, norm_gain, gate_weight, up_weight, doc_lengths
):
    dma = pltpu.SemaphoreType.DMA
    vmem = pl.BlockSpec(memory_space=pltpu.VMEM)
    anywhere = pl.BlockSpec(memory_space=pl.ANY)
    residual, hidden = pl.pallas_call(
        layer_kernel,
        out_shape=(
            jax.ShapeDtypeStruct((ROWS, KB), jnp.bfloat16),
            jax.ShapeDtypeStruct((HALF, 4 * ROWS), jnp.bfloat16),
        ),
        in_specs=[pl.BlockSpec(memory_space=pltpu.SMEM)] + [anywhere] * 4 + [vmem] + [anywhere] * 2,
        out_specs=(vmem, vmem),
        scratch_shapes=[
            pltpu.VMEM((2, 4, 2, 2 * ROWS, KB), jnp.bfloat16),
            pltpu.VMEM((2, WIDTH, KB), jnp.bfloat16),
            pltpu.VMEM((2, 4, WIDTH, 2 * ROWS), jnp.bfloat16),
            pltpu.VMEM((2, 4, 2, QUARTER, 2 * ROWS), jnp.bfloat16),
            pltpu.VMEM((2, 2, WIDTH, 2 * ROWS), jnp.bfloat16),
            pltpu.VMEM((2, WIDTH, 2 * ROWS), jnp.float32),
            pltpu.VMEM((ROWS, KB), jnp.bfloat16),
            pltpu.VMEM((4, 2 * ROWS, HD), jnp.bfloat16),
            pltpu.VMEM((5, 2, 2 * ROWS, HD), jnp.bfloat16),
            pltpu.VMEM((ROWS, KB), jnp.bfloat16),
            pltpu.VMEM((ROWS, KB), jnp.bfloat16),
            pltpu.VMEM((8, 8, ROWS), jnp.float32),
            pltpu.VMEM((2, 2, 8, ROWS), jnp.float32),
            pltpu.VMEM((4, 1, 2 * ROWS), jnp.float32),
            pltpu.VMEM((4, 1, 2 * ROWS), jnp.float32),
            pltpu.VMEM((4, HD, 2 * ROWS), jnp.float32),
            dma((6,)), dma((4,)), dma((5,)), dma((5, 2)), dma((1,)), dma((8,)), dma((2, 4)), dma((2, 2)),
            dma((3,)), dma((3,)), dma((1,)), dma((2, 4, 2, 2)),
            dma((2, 4, 2)), dma((2, 4, 2)), dma((2, 4, 2)), dma((2, 4, 2)),
            dma((2, 4, 4)), dma((2, 4, 2)), dma((2, 4, 4)), dma((2, 2, 4)),
        ],
        compiler_params=pltpu.CompilerParams(
            collective_id=0, has_side_effects=True, vmem_limit_bytes=56 * 2**20
        ),
        name="layer",
    )(
        doc_lengths, query_heads, key_heads, value_heads, residual_in,
        norm_gain, gate_weight.T, up_weight.T,
    )
    residual, hidden = pl.pallas_call(
        hand_over_kernel,
        out_shape=(
            jax.ShapeDtypeStruct((ROWS, KB), jnp.bfloat16),
            jax.ShapeDtypeStruct((HALF, 4 * ROWS), jnp.bfloat16),
        ),
        in_specs=[anywhere] * 2,
        out_specs=(anywhere, anywhere),
        scratch_shapes=[dma((2,))],
        name="hand_over",
    )(residual, hidden)
    return residual, hidden.T


def solution(mesh):
    in_specs = (
        P("ctx", "mp"),
        P("ctx", "mp"),
        P("ctx", "mp"),
        P("ctx", "mp"),
        P("mp"),
        P("mp", "ctx"),
        P("mp", "ctx"),
        P(),
    )
    out_specs = (P("ctx", "mp"), P("mp", "ctx"))
    return jax.shard_map(
        on_device, mesh=mesh, in_specs=in_specs, out_specs=out_specs, check_vma=False
    )
```

```python
import functools

import jax
import jax.numpy as jnp
from jax import lax
from jax.experimental import pallas as pl
from jax.experimental.pallas import tpu as pltpu
from jax.sharding import PartitionSpec as P

D = 8192
HD = 128
MESH = pl.DeviceIdType.MESH
ROWS = 128
KB = 1024
HALF = 448
WIDTH = 2 * HALF
QUARTER = HALF // 2


def place():
    ctx = lax.axis_index("ctx")
    mp = lax.axis_index("mp")
    return ctx // 16, lax.rem(ctx // 2, 8), lax.rem(ctx, 2), mp // 2, lax.rem(mp, 2)


def device(yh, z, c, x, yl):
    return (yh * 16 + z * 2 + c, x * 2 + yl)


def pick(w, values):
    out = jnp.int32(values[0])
    for i in range(1, len(values)):
        out = jnp.where(w == i, jnp.int32(values[i]), out)
    return out


OFFSETS = ((0, 0, -1, 1), (1, -1, 2, -2), (-3, 3, -2, 2), (4, -4, 3, -3))
ONWARD_UP = (
    ((1, 1, 1, 0), (0, 1, 0, 1), (1, 0, 1, 0), (0, 0, 0, 0)),
    ((1, 1, 1, 0), (0, 1, 0, 1), (1, 0, 1, 0), (0, 0, 0, 0)),
)
ONWARD_DOWN = (
    ((1, 1, 0, 1), (1, 0, 1, 0), (0, 1, 0, 1), (0, 0, 0, 0)),
    ((1, 1, 0, 1), (1, 0, 1, 0), (0, 1, 0, 1), (0, 0, 0, 0)),
)
CROSSES = ((1, 1, 0, 0), (0, 0, 0, 0), (0, 0, 0, 0), (0, 0, 0, 0))
EVENTS = (
    ((0, 0, 0), (0, 0, 1), (1, 0, 0), (0, 1, 0), (0, 1, 1), (1, 0, 1), (2, 0, 0), (1, 1, 0), (2, 0, 1), (3, 0, 0), (1, 1, 1), (2, 1, 0), (3, 0, 1), (2, 1, 1), (3, 1, 0), (3, 1, 1)),
    ((0, 0, 0), (0, 0, 1), (1, 0, 0), (2, 0, 0), (1, 0, 1), (0, 1, 0), (0, 1, 1), (1, 1, 0), (3, 0, 0), (1, 1, 1), (2, 0, 1), (2, 1, 0), (2, 1, 1), (3, 0, 1), (3, 1, 0), (3, 1, 1)),
)
GROUPS = (
    ((0, 0), (0, 1), (1, 0), (2, 0), (1, 1), (3, 0), (2, 1), (3, 1)),
    ((0, 0), (1, 0), (0, 1), (1, 1), (2, 0), (2, 1), (3, 0), (3, 1)),
)
BEFORE = (3, 6, 8, 11, 12, 14, 15, 16)
PIECES = ((0, 320, -1), (320, 128, 0), (448, 448, 0))
GATED = (0, 0, 3, 4, 5, 6, 7, 8)
UPPED = (0, 0, 0, 4, 5, 6, 7, 8)
RELAYED = (0, 0, 0, 0, 1, 2, 3, 4)


def document_starts(lengths_ref, positions):
    starts = jnp.zeros_like(positions)
    end = jnp.int32(0)
    for i in range(lengths_ref.shape[0]):
        end = end + lengths_ref[i]
        starts = jnp.where(positions >= end, end, starts)
    return starts


def layer_kernel(
    lengths_ref, query_ref, key_ref, value_ref, residual_in_ref, gain_ref, gate_ref, up_ref,
    residual_ref, out_ref,
    tokens, weights, staged, relayed, landed, own_sum,
    query, by_head, keys_values, residual_in, scaled, squares, inverse,
    running_max, denominator, weighted,
    load_sem, kv_send, kv_sib_send, kv_recv, sq_send, sq_recv, inv_send, inv_recv,
    w_send, w_recv, cross_send, tok_recv, up_send, down_send, sib_send, hi_send, relay_send, relay_recv, sum_send, sum_recv,
):
    yh, z, c, x, yl = place()
    match = lax.rem(z // 2, 2) == yl
    w = lax.rem(z - 2 * yl + 8, 4)
    my_source = (z // 4) * 2 + lax.rem(z, 2)
    sibling = device(yh, z, 1 - c, x, yl)
    lo_partner = device(yh, z, c, x, 1 - yl)
    hi_partner = device(1 - yh, z, c, x, yl)
    above = device(yh, lax.rem(z + 1, 8), c, x, yl)
    below = device(yh, lax.rem(z + 7, 8), c, x, yl)
    x_peers = [device(yh, z, c, lax.rem(x + d, 4), yl) for d in (1, 2, 3)]
    mine = pl.ds(pl.multiple_of(c * ROWS, ROWS), ROWS)

    mp = x * 2 + yl
    chip = yh * 8 + z
    step_on = lambda k: device(lax.rem((chip + 16 + k) // 8, 2), lax.rem(chip + 16 + k, 8), c, x, yl)
    kv_hops = ((0, 1, step_on(1)), (0, 2, step_on(2)), (0, 4, step_on(4)), (2, 1, step_on(1)))

    loads = [
        pltpu.make_async_copy(key_ref, keys_values.at[0, 0, mine], load_sem.at[0]),
        pltpu.make_async_copy(value_ref, keys_values.at[0, 1, mine], load_sem.at[1]),
        pltpu.make_async_copy(query_ref, query, load_sem.at[2]),
        pltpu.make_async_copy(residual_in_ref, residual_in, load_sem.at[3]),
        pltpu.make_async_copy(gate_ref, weights.at[yl, pl.ds(0, HALF)], load_sem.at[4]),
        pltpu.make_async_copy(up_ref, weights.at[yl, pl.ds(HALF, HALF)], load_sem.at[5]),
    ]
    for load in loads:
        load.start()

    barrier = pltpu.get_barrier_semaphore()
    across = [device(yh, z, c, lax.rem(x + d, 4), 1 - yl) for d in (1, 2, 3)]
    peers = [sibling, lo_partner, hi_partner, above, below] + x_peers + across
    for peer in peers:
        pl.semaphore_signal(barrier, inc=1, device_id=peer, device_id_type=MESH)

    @pl.when(chip == 8)
    def _():
        pl.semaphore_signal(barrier, inc=1, device_id=step_on(-1), device_id_type=MESH)

    for k in (2, 4):
        @pl.when(chip >= k)
        def _():
            pl.semaphore_signal(barrier, inc=1, device_id=step_on(-k), device_id_type=MESH)

    pl.semaphore_wait(
        barrier,
        len(peers) + jnp.where(chip == 7, 1, 0) + jnp.where(chip < 14, 1, 0) + jnp.where(chip < 12, 1, 0),
    )
    for load in loads[:2]:
        load.wait()

    def kv_onward(i):
        j, ahead, target = kv_hops[i]
        return pltpu.make_async_remote_copy(
            src_ref=keys_values.at[j, :, mine], dst_ref=keys_values.at[j + ahead, :, mine],
            send_sem=kv_send.at[i], recv_sem=kv_recv.at[j + ahead, c],
            device_id=target, device_id_type=MESH,
        )

    def kv_sent(i):
        j, ahead, _ = kv_hops[i]
        return jnp.logical_and(chip >= j, chip < 16 - ahead)

    def kv_sibling(j):
        view = keys_values.at[j, :, mine]
        return pltpu.make_async_remote_copy(
            src_ref=view, dst_ref=view, send_sem=kv_sib_send.at[j], recv_sem=kv_recv.at[j, c],
            device_id=sibling, device_id_type=MESH,
        )

    def kv_arrival(j, core):
        view = keys_values.at[j, :, pl.ds(pl.multiple_of(core * ROWS, ROWS), ROWS)]
        return pltpu.make_async_remote_copy(
            src_ref=view, dst_ref=view, send_sem=kv_sib_send.at[j], recv_sem=kv_recv.at[j, core],
            device_id=sibling, device_id_type=MESH,
        )

    for i in range(3):
        @pl.when(kv_sent(i))
        def _():
            kv_onward(i).start()

    kv_sibling(0).start()

    for load in loads[4:]:
        load.wait()

    def weight_copy(i):
        start, rows, _ = PIECES[i]
        view = weights.at[yl, pl.ds(start, rows)]
        return pltpu.make_async_remote_copy(
            src_ref=view, dst_ref=view, send_sem=w_send.at[i], recv_sem=w_recv.at[i],
            device_id=lo_partner, device_id_type=MESH,
        )

    for i, (_, _, when) in enumerate(PIECES):
        if when < 0:
            weight_copy(i).start()

    def cross_copy():
        return pltpu.make_async_remote_copy(
            src_ref=scaled, dst_ref=tokens.at[yh, my_source, yl, mine],
            send_sem=cross_send.at[0], recv_sem=tok_recv.at[yh, my_source, yl, c],
            device_id=lo_partner, device_id_type=MESH,
        )

    def token_copy(h, source, kb, sems, target):
        view = tokens.at[h, source, kb, mine]
        return pltpu.make_async_remote_copy(
            src_ref=view, dst_ref=view, send_sem=sems.at[h, source, kb],
            recv_sem=tok_recv.at[h, source, kb, c], device_id=target, device_id_type=MESH,
        )

    def token_arrival(h, source, kb, core):
        view = tokens.at[h, source, kb, pl.ds(pl.multiple_of(core * ROWS, ROWS), ROWS)]
        return pltpu.make_async_remote_copy(
            src_ref=view, dst_ref=view, send_sem=sib_send.at[h, source, kb],
            recv_sem=tok_recv.at[h, source, kb, core], device_id=sibling, device_id_type=MESH,
        )

    def event_code(event, v):
        unit, half, block = EVENTS[v // 2][event]
        bits = (
            half, block, ONWARD_UP[half][unit][v], ONWARD_DOWN[half][unit][v],
            CROSSES[unit][v] * (1 - half), int(unit == 0 and v < 2 and half == 0),
        )
        return OFFSETS[unit][v] + 4 + sum(b << (4 + i) for i, b in enumerate(bits))

    def group_code(step, v):
        unit, half = GROUPS[v // 2][step]
        return OFFSETS[unit][v] + 4 + (half << 4)

    event_codes = [pick(w, [event_code(e, v) for v in range(4)]) for e in range(16)]
    group_codes = [pick(w, [group_code(g, v) for v in range(4)]) for g in range(8)]

    def bit(code, i):
        return lax.rem(code // 2**i, 2)

    def unit_of(code):
        source_z = lax.rem(z + lax.rem(code, 16) + 4, 8)
        source = (source_z // 4) * 2 + lax.rem(source_z, 2)
        return lax.rem(yh + bit(code, 4), 2), source

    def group_of(step):
        return unit_of(pick(step, group_codes))

    def event_of(event):
        code = pick(event, event_codes)
        h, source = unit_of(code)
        block = bit(code, 5)
        goes = (bit(code, 6) == 1, bit(code, 7) == 1, block >= 0, bit(code, 8) == 1)
        return h, source, block, goes, bit(code, 9) == 1

    def onward(h, source, kb, goes):
        ways = ((up_send, above), (down_send, below), (sib_send, sibling), (hi_send, hi_partner))
        return [
            (wanted, token_copy(h, source, kb, sems, target))
            for wanted, (sems, target) in zip(goes, ways)
        ]

    def owned_here(h, source):
        return h * 2 + source // 2 == x

    def handle(event):
        h, source, block, goes, at_home = event_of(event)
        kb = lax.rem(yl + block, 2)

        @pl.when(jnp.logical_not(jnp.logical_and(at_home, block == 0)))
        def _():
            token_arrival(h, source, kb, c).wait_recv()

        for wanted, copy in onward(h, source, kb, goes):
            @pl.when(wanted)
            def _():
                copy.start()

        @pl.when(jnp.logical_and(owned_here(h, source), block == 1))
        def _():
            low = lax.rem(source, 2)

            @pl.when(at_home)
            def _():
                squares_to_inverse()

            @pl.when(jnp.logical_not(at_home))
            def _():
                inverse_copy(low, c, 0, sibling).wait_recv()

            for wanted, copy in inverse_onward(goes, low):
                @pl.when(wanted)
                def _():
                    copy.start()

    def role_of(h, source):
        return lax.rem(x - (h * 2 + source // 2) + 4, 4)

    def goes_up(source, part):
        return lax.rem(source + part, 2) == 0

    def sum_copy(h, source, quarter):
        rows = pl.ds(quarter * QUARTER, QUARTER)
        slot = role_of(h, source) // 2
        low = lax.rem(source, 2)
        return pltpu.make_async_remote_copy(
            src_ref=staged.at[h, source, rows], dst_ref=landed.at[slot, low, rows],
            send_sem=sum_send.at[h, source, quarter], recv_sem=sum_recv.at[slot, low, quarter],
            device_id=device(yh, z, c, h * 2 + source // 2, yl), device_id_type=MESH,
        )

    def relay_copy(h, source, quarter):
        towards = lax.rem(x + jnp.where(goes_up(source, quarter // 2), 1, 3), 4)
        return pltpu.make_async_remote_copy(
            src_ref=staged.at[h, source, pl.ds(quarter * QUARTER, QUARTER)],
            dst_ref=relayed.at[h, source, quarter % 2],
            send_sem=relay_send.at[h, source, quarter], recv_sem=relay_recv.at[h, source, quarter % 2],
            device_id=device(yh, z, c, towards, yl), device_id_type=MESH,
        )

    def relays(role, source, part):
        return jnp.logical_and(lax.rem(role, 2) == 1, (role == 3) == goes_up(source, part))

    def multiply(step, part):
        h, source = group_of(step)
        rows = pl.ds(part * HALF, HALF)
        across_k = (((1,), (1,)), ((), ()))
        product = lax.dot_general(
            weights[0, rows], tokens[h, source, 0], across_k, preferred_element_type=jnp.float32
        ) + lax.dot_general(
            weights[1, rows], tokens[h, source, 1], across_k, preferred_element_type=jnp.float32
        )
        role = role_of(h, source)

        @pl.when(role == 0)
        def _():
            own_sum[lax.rem(source, 2), rows] = product

        @pl.when(role != 0)
        def _():
            staged[h, source, rows] = product.astype(jnp.bfloat16)

        @pl.when(role == 2)
        def _():
            for quarter in (2 * part, 2 * part + 1):
                relay_copy(h, source, quarter).start()

        @pl.when(jnp.logical_and(lax.rem(role, 2) == 1, jnp.logical_not(relays(role, source, part))))
        def _():
            for quarter in (2 * part, 2 * part + 1):
                sum_copy(h, source, quarter).start()

    def add_relayed(step, part):
        h, source = group_of(step)

        @pl.when(relays(role_of(h, source), source, part))
        def _():
            for quarter in (2 * part, 2 * part + 1):
                rows = pl.ds(quarter * QUARTER, QUARTER)
                relay_copy(h, source, quarter).wait_recv()
                staged[h, source, rows] = (
                    staged[h, source, rows].astype(jnp.float32)
                    + relayed[h, source, quarter % 2].astype(jnp.float32)
                ).astype(jnp.bfloat16)
                sum_copy(h, source, quarter).start()

    def sibling_arrived(step):
        h, source = group_of(step)
        for i in range(2):
            token_arrival(h, source, i, 1 - c).wait_recv()

    owner_mp = (yh * 2 + z // 4) * 2 + lax.rem(z // 2, 2)

    def square_copy():
        view = squares.at[mp]
        return pltpu.make_async_remote_copy(
            src_ref=view, dst_ref=view, send_sem=sq_send.at[0], recv_sem=sq_recv.at[mp],
            device_id=(chip * 2 + c, owner_mp), device_id_type=MESH,
        )

    def squares_to_inverse():
        for i in range(1, 8):
            slot = lax.rem(mp + i, 8)
            view = squares.at[slot]
            pltpu.make_async_remote_copy(
                src_ref=view, dst_ref=view, send_sem=sq_send.at[0], recv_sem=sq_recv.at[slot],
                device_id=lo_partner, device_id_type=MESH,
            ).wait_recv()
        inverse[lax.rem(z, 2), c] = lax.rsqrt(jnp.sum(squares[...], axis=0) / D + 1e-05)

    def inverse_copy(low, core, way, target):
        view = inverse.at[low, core]
        return pltpu.make_async_remote_copy(
            src_ref=view, dst_ref=view, send_sem=inv_send.at[low, way], recv_sem=inv_recv.at[low, core],
            device_id=target, device_id_type=MESH,
        )

    def inverse_onward(wanted, low):
        targets = (above, below, sibling, hi_partner)
        return [(want, inverse_copy(low, c, way, target)) for way, (want, target) in enumerate(zip(wanted, targets))]

    def weights_arrived(part):
        for i, (start, rows, _) in enumerate(PIECES):
            if start // HALF == part:
                view = weights.at[1 - yl, pl.ds(start, rows)]
                pltpu.make_async_remote_copy(
                    src_ref=view, dst_ref=view, send_sem=w_send.at[i], recv_sem=w_recv.at[i],
                    device_id=lo_partner, device_id_type=MESH,
                ).wait_recv()

    for load in loads[2:4]:
        load.wait()
    for head in range(8):
        by_head[head // 2, (head % 2) * ROWS:(head % 2 + 1) * ROWS] = query[:, head * HD:(head + 1) * HD]
    running_max[...] = jnp.full_like(running_max, -1e30)
    denominator[...] = jnp.zeros_like(denominator)
    weighted[...] = jnp.zeros_like(weighted)
    query_pos = (chip * 2 + c) * ROWS + lax.broadcasted_iota(jnp.int32, (1, ROWS), 1)
    starts = document_starts(lengths_ref, query_pos)

    def attend(j):
        key_pos = (chip - j) * 256 + lax.broadcasted_iota(jnp.int32, (256, ROWS), 0)
        visible = jnp.logical_and(key_pos >= starts, key_pos <= query_pos)
        bias = jnp.where(visible, 0.0, -1e30)
        bias = jnp.concatenate([bias, bias], axis=1)

        scores = [
            lax.dot_general(
                keys_values[j, 0], by_head[i], (((1,), (1,)), ((), ())),
                preferred_element_type=jnp.float32,
            ) * HD ** (-0.5) + bias
            for i in range(4)
        ]
        olds = [running_max[i] for i in range(4)]
        news = [jnp.maximum(olds[i], jnp.max(scores[i], axis=0, keepdims=True)) for i in range(4)]
        for i in range(4):
            factor = jnp.exp(olds[i] - news[i])
            parts = jnp.exp(scores[i] - news[i])
            running_max[i] = news[i]
            denominator[i] = denominator[i] * factor + jnp.sum(parts, axis=0, keepdims=True)
            weighted[i] = weighted[i] * factor + lax.dot_general(
                keys_values[j, 1], parts.astype(jnp.bfloat16), (((0,), (0,)), ((), ())),
                preferred_element_type=jnp.float32,
            )

    def attend_step(j, _):
        @pl.when(jnp.logical_and(j < 4, chip > j))
        def _():
            kv_arrival(j + 1, c).wait_recv()

            @pl.when(jnp.logical_and(j == 1, kv_sent(3)))
            def _():
                kv_onward(3).start()

            kv_sibling(j + 1).start()

        @pl.when(jnp.logical_and(j < 4, chip <= j))
        def _():
            keys_values[j + 1] = jnp.zeros_like(keys_values[0])

        @pl.when(chip >= j)
        def _():
            kv_arrival(j, 1 - c).wait_recv()

        attend(j)
        return 0

    lax.fori_loop(0, 5, attend_step, 0)

    total = jnp.zeros((ROWS, HD), jnp.float32)
    for head in range(8):
        lanes = slice((head % 2) * ROWS, (head % 2 + 1) * ROWS)
        columns = slice(head * HD, (head + 1) * HD)
        attended = (weighted[head // 2, :, lanes] / denominator[head // 2, :, lanes]).T
        rounded = (residual_in[:, columns].astype(jnp.float32) + attended).astype(jnp.bfloat16)
        residual_ref[:, columns] = rounded
        wide = rounded.astype(jnp.float32)
        total = total + wide * wide
        scaled[:, columns] = (wide * gain_ref[columns].astype(jnp.float32)[None, :]).astype(jnp.bfloat16)

    @pl.when(match)
    def _():
        tokens[yh, my_source, yl, mine] = scaled[...]

    @pl.when(jnp.logical_not(match))
    def _():
        cross_copy().start()

    squares[mp] = jnp.broadcast_to(jnp.sum(total.T, axis=0, keepdims=True), (8, ROWS))

    @pl.when(mp != owner_mp)
    def _():
        square_copy().start()

    def handle_until(step):
        def one(event, _):
            handle(event)
            return 0

        lax.fori_loop(pick(step, (0,) + BEFORE[:-1]), pick(step, BEFORE), one, 0)

    def step_through(step, _):
        handle_until(step)
        for i, (_, _, when) in enumerate(PIECES):
            if when >= 0:
                @pl.when(step == when)
                def _():
                    weight_copy(i).start()

        def each(counts, work):
            def one(group, _):
                work(group)
                return 0

            lax.fori_loop(pick(step, (0,) + counts[:-1]), pick(step, counts), one, 0)

        def gate_group(group):
            sibling_arrived(group)
            multiply(group, 0)

        @pl.when(step == 2)
        def _():
            weights_arrived(0)

        each(GATED, gate_group)

        @pl.when(step == 3)
        def _():
            weights_arrived(1)

        each(UPPED, lambda group: multiply(group, 1))

        def relay_group(group):
            for part in range(2):
                add_relayed(group, part)

        each(RELAYED, relay_group)
        return 0

    lax.fori_loop(0, 8, step_through, 0)

    def last(step, _):
        for part in range(2):
            add_relayed(step, part)
        return 0

    lax.fori_loop(RELAYED[-1], 8, last, 0)

    for i in range(4):
        @pl.when(kv_sent(i))
        def _():
            kv_onward(i).wait_send()
    for j in range(5):
        @pl.when(chip >= j)
        def _():
            kv_sibling(j).wait_send()

    @pl.when(mp != owner_mp)
    def _():
        square_copy().wait_send()

    for i in range(len(PIECES)):
        weight_copy(i).wait_send()

    @pl.when(jnp.logical_not(match))
    def _():
        cross_copy().wait_send()

    def tokens_sent(event, _):
        h, source, block, goes, _ = event_of(event)
        for wanted, copy in onward(h, source, lax.rem(yl + block, 2), goes):
            @pl.when(wanted)
            def _():
                copy.wait_send()

        @pl.when(jnp.logical_and(owned_here(h, source), block == 1))
        def _():
            for wanted, copy in inverse_onward(goes, lax.rem(source, 2)):
                @pl.when(wanted)
                def _():
                    copy.wait_send()

        return 0

    lax.fori_loop(0, 16, tokens_sent, 0)

    for low in range(2):
        inverse_copy(low, 1 - c, 0, sibling).wait_recv()
        scale = jnp.concatenate([inverse[low, 0], inverse[low, 1]], axis=1)[0:1]
        def total_of(quarter):
            rows = pl.ds(quarter * QUARTER, QUARTER)
            total = own_sum[low, rows]
            for slot in range(2):
                view = landed.at[slot, low, rows]
                pltpu.make_async_remote_copy(
                    src_ref=view, dst_ref=view, send_sem=sum_send.at[0, 0, quarter],
                    recv_sem=sum_recv.at[slot, low, quarter], device_id=x_peers[0], device_id_type=MESH,
                ).wait_recv()
                total = total + landed[slot, low, rows].astype(jnp.float32)
            return total * scale

        for quarter in range(4):
            out_ref[quarter * QUARTER:(quarter + 1) * QUARTER, low * 256:(low + 1) * 256] = total_of(quarter)

    def sums_sent(step, _):
        h, source = group_of(step)
        role = role_of(h, source)
        for quarter in range(4):
            @pl.when(role == 2)
            def _():
                relay_copy(h, source, quarter).wait_send()

            @pl.when(lax.rem(role, 2) == 1)
            def _():
                sum_copy(h, source, quarter).wait_send()

        return 0

    lax.fori_loop(0, 8, sums_sent, 0)


def on_device(
    query_heads, key_heads, value_heads, residual_in, norm_gain, gate_weight, up_weight, doc_lengths
):
    dma = pltpu.SemaphoreType.DMA
    vmem = pl.BlockSpec(memory_space=pltpu.VMEM)
    anywhere = pl.BlockSpec(memory_space=pl.ANY)
    residual, sums = pl.pallas_call(
        layer_kernel,
        out_shape=(
            jax.ShapeDtypeStruct((ROWS, KB), jnp.bfloat16),
            jax.ShapeDtypeStruct((WIDTH, 4 * ROWS), jnp.float32),
        ),
        in_specs=[pl.BlockSpec(memory_space=pltpu.SMEM)] + [anywhere] * 4 + [vmem] + [anywhere] * 2,
        out_specs=(vmem, vmem),
        scratch_shapes=[
            pltpu.VMEM((2, 4, 2, 2 * ROWS, KB), jnp.bfloat16),
            pltpu.VMEM((2, WIDTH, KB), jnp.bfloat16),
            pltpu.VMEM((2, 4, WIDTH, 2 * ROWS), jnp.bfloat16),
            pltpu.VMEM((2, 4, 2, QUARTER, 2 * ROWS), jnp.bfloat16),
            pltpu.VMEM((2, 2, WIDTH, 2 * ROWS), jnp.bfloat16),
            pltpu.VMEM((2, WIDTH, 2 * ROWS), jnp.float32),
            pltpu.VMEM((ROWS, KB), jnp.bfloat16),
            pltpu.VMEM((4, 2 * ROWS, HD), jnp.bfloat16),
            pltpu.VMEM((5, 2, 2 * ROWS, HD), jnp.bfloat16),
            pltpu.VMEM((ROWS, KB), jnp.bfloat16),
            pltpu.VMEM((ROWS, KB), jnp.bfloat16),
            pltpu.VMEM((8, 8, ROWS), jnp.float32),
            pltpu.VMEM((2, 2, 8, ROWS), jnp.float32),
            pltpu.VMEM((4, 1, 2 * ROWS), jnp.float32),
            pltpu.VMEM((4, 1, 2 * ROWS), jnp.float32),
            pltpu.VMEM((4, HD, 2 * ROWS), jnp.float32),
            dma((6,)), dma((4,)), dma((5,)), dma((5, 2)), dma((1,)), dma((8,)), dma((2, 4)), dma((2, 2)),
            dma((3,)), dma((3,)), dma((1,)), dma((2, 4, 2, 2)),
            dma((2, 4, 2)), dma((2, 4, 2)), dma((2, 4, 2)), dma((2, 4, 2)),
            dma((2, 4, 4)), dma((2, 4, 2)), dma((2, 4, 4)), dma((2, 2, 4)),
        ],
        compiler_params=pltpu.CompilerParams(
            collective_id=0, has_side_effects=True, vmem_limit_bytes=56 * 2**20
        ),
        name="layer",
    )(
        doc_lengths, query_heads, key_heads, value_heads, residual_in,
        norm_gain, gate_weight.T, up_weight.T,
    )
    gate, up = sums[:HALF], sums[HALF:]
    hidden = (jax.nn.silu(gate) * up).astype(jnp.bfloat16)
    return residual, hidden.T


def solution(mesh):
    in_specs = (
        P("ctx", "mp"),
        P("ctx", "mp"),
        P("ctx", "mp"),
        P("ctx", "mp"),
        P("mp"),
        P("mp", "ctx"),
        P("mp", "ctx"),
        P(),
    )
    out_specs = (P("ctx", "mp"), P("mp", "ctx"))
    return jax.shard_map(
        on_device, mesh=mesh, in_specs=in_specs, out_specs=out_specs, check_vma=False
    )
```

```python
import functools

import jax
import jax.numpy as jnp
from jax import lax
from jax.experimental import pallas as pl
from jax.experimental.pallas import tpu as pltpu
from jax.sharding import PartitionSpec as P

D = 8192
HD = 128
MESH = pl.DeviceIdType.MESH
ROWS = 128
KB = 1024
HALF = 448
WIDTH = 2 * HALF
QUARTER = HALF // 2


def place():
    ctx = lax.axis_index("ctx")
    mp = lax.axis_index("mp")
    return ctx // 16, lax.rem(ctx // 2, 8), lax.rem(ctx, 2), mp // 2, lax.rem(mp, 2)


def device(yh, z, c, x, yl):
    return (yh * 16 + z * 2 + c, x * 2 + yl)


def pick(w, values):
    out = jnp.int32(values[0])
    for i in range(1, len(values)):
        out = jnp.where(w == i, jnp.int32(values[i]), out)
    return out


OFFSETS = ((0, 0, -1, 1), (1, -1, 2, -2), (-3, 3, -2, 2), (4, -4, 3, -3))
ONWARD_UP = (
    ((1, 1, 1, 0), (0, 1, 0, 1), (1, 0, 1, 0), (0, 0, 0, 0)),
    ((1, 1, 1, 0), (0, 1, 0, 1), (1, 0, 1, 0), (0, 0, 0, 0)),
)
ONWARD_DOWN = (
    ((1, 1, 0, 1), (1, 0, 1, 0), (0, 1, 0, 1), (0, 0, 0, 0)),
    ((1, 1, 0, 1), (1, 0, 1, 0), (0, 1, 0, 1), (0, 0, 0, 0)),
)
CROSSES = ((1, 1, 0, 0), (0, 0, 0, 0), (0, 0, 0, 0), (0, 0, 0, 0))
EVENTS = (
    ((0, 0, 0), (0, 0, 1), (1, 0, 0), (0, 1, 0), (0, 1, 1), (1, 0, 1), (2, 0, 0), (1, 1, 0), (2, 0, 1), (3, 0, 0), (1, 1, 1), (2, 1, 0), (3, 0, 1), (2, 1, 1), (3, 1, 0), (3, 1, 1)),
    ((0, 0, 0), (0, 0, 1), (1, 0, 0), (2, 0, 0), (1, 0, 1), (0, 1, 0), (0, 1, 1), (1, 1, 0), (3, 0, 0), (1, 1, 1), (2, 0, 1), (2, 1, 0), (2, 1, 1), (3, 0, 1), (3, 1, 0), (3, 1, 1)),
)
GROUPS = (
    ((0, 0), (0, 1), (1, 0), (2, 0), (1, 1), (3, 0), (2, 1), (3, 1)),
    ((0, 0), (1, 0), (0, 1), (1, 1), (2, 0), (2, 1), (3, 0), (3, 1)),
)
BEFORE = (3, 6, 8, 11, 12, 14, 15, 16)
PIECES = ((0, 320, -1), (320, 128, 0), (448, 448, 0))
GATED = (0, 0, 3, 4, 5, 6, 7, 8)
UPPED = (0, 0, 0, 4, 5, 6, 7, 8)
RELAYED = (0, 0, 0, 0, 1, 2, 3, 4)


def document_starts(lengths_ref, positions):
    starts = jnp.zeros_like(positions)
    end = jnp.int32(0)
    for i in range(lengths_ref.shape[0]):
        end = end + lengths_ref[i]
        starts = jnp.where(positions >= end, end, starts)
    return starts


def layer_kernel(
    lengths_ref, query_ref, key_ref, value_ref, residual_in_ref, gain_ref, gate_ref, up_ref,
    residual_ref, out_ref,
    tokens, weights, staged, relayed, landed, own_sum,
    query, by_head, keys_values, residual_in, scaled, squares, inverse,
    running_max, denominator, weighted,
    load_sem, kv_send, kv_sib_send, kv_recv, sq_send, sq_recv, inv_send, inv_recv,
    w_send, w_recv, cross_send, tok_recv, up_send, down_send, sib_send, hi_send, relay_send, relay_recv, sum_send, sum_recv,
):
    yh, z, c, x, yl = place()
    match = lax.rem(z // 2, 2) == yl
    w = lax.rem(z - 2 * yl + 8, 4)
    my_source = (z // 4) * 2 + lax.rem(z, 2)
    sibling = device(yh, z, 1 - c, x, yl)
    lo_partner = device(yh, z, c, x, 1 - yl)
    hi_partner = device(1 - yh, z, c, x, yl)
    above = device(yh, lax.rem(z + 1, 8), c, x, yl)
    below = device(yh, lax.rem(z + 7, 8), c, x, yl)
    x_peers = [device(yh, z, c, lax.rem(x + d, 4), yl) for d in (1, 2, 3)]
    mine = pl.ds(pl.multiple_of(c * ROWS, ROWS), ROWS)

    mp = x * 2 + yl
    chip = yh * 8 + z
    step_on = lambda k: device(lax.rem((chip + 16 + k) // 8, 2), lax.rem(chip + 16 + k, 8), c, x, yl)
    kv_hops = ((0, 1, step_on(1)), (0, 2, step_on(2)), (0, 4, step_on(4)), (2, 1, step_on(1)))

    loads = [
        pltpu.make_async_copy(key_ref, keys_values.at[0, 0, mine], load_sem.at[0]),
        pltpu.make_async_copy(value_ref, keys_values.at[0, 1, mine], load_sem.at[1]),
        pltpu.make_async_copy(query_ref, query, load_sem.at[2]),
        pltpu.make_async_copy(residual_in_ref, residual_in, load_sem.at[3]),
        pltpu.make_async_copy(gate_ref, weights.at[yl, pl.ds(0, HALF)], load_sem.at[4]),
        pltpu.make_async_copy(up_ref, weights.at[yl, pl.ds(HALF, HALF)], load_sem.at[5]),
    ]
    for load in loads:
        load.start()

    barrier = pltpu.get_barrier_semaphore()
    across = [device(yh, z, c, lax.rem(x + d, 4), 1 - yl) for d in (1, 2, 3)]
    peers = [sibling, lo_partner, hi_partner, above, below] + x_peers + across
    for peer in peers:
        pl.semaphore_signal(barrier, inc=1, device_id=peer, device_id_type=MESH)

    @pl.when(chip == 8)
    def _():
        pl.semaphore_signal(barrier, inc=1, device_id=step_on(-1), device_id_type=MESH)

    for k in (2, 4):
        @pl.when(chip >= k)
        def _():
            pl.semaphore_signal(barrier, inc=1, device_id=step_on(-k), device_id_type=MESH)

    pl.semaphore_wait(
        barrier,
        len(peers) + jnp.where(chip == 7, 1, 0) + jnp.where(chip < 14, 1, 0) + jnp.where(chip < 12, 1, 0),
    )
    for load in loads[:2]:
        load.wait()

    def kv_onward(i):
        j, ahead, target = kv_hops[i]
        return pltpu.make_async_remote_copy(
            src_ref=keys_values.at[j, :, mine], dst_ref=keys_values.at[j + ahead, :, mine],
            send_sem=kv_send.at[i], recv_sem=kv_recv.at[j + ahead, c],
            device_id=target, device_id_type=MESH,
        )

    def kv_sent(i):
        j, ahead, _ = kv_hops[i]
        return jnp.logical_and(chip >= j, chip < 16 - ahead)

    def kv_sibling(j):
        view = keys_values.at[j, :, mine]
        return pltpu.make_async_remote_copy(
            src_ref=view, dst_ref=view, send_sem=kv_sib_send.at[j], recv_sem=kv_recv.at[j, c],
            device_id=sibling, device_id_type=MESH,
        )

    def kv_arrival(j, core):
        view = keys_values.at[j, :, pl.ds(pl.multiple_of(core * ROWS, ROWS), ROWS)]
        return pltpu.make_async_remote_copy(
            src_ref=view, dst_ref=view, send_sem=kv_sib_send.at[j], recv_sem=kv_recv.at[j, core],
            device_id=sibling, device_id_type=MESH,
        )

    for i in range(3):
        @pl.when(kv_sent(i))
        def _():
            kv_onward(i).start()

    kv_sibling(0).start()

    for load in loads[4:]:
        load.wait()

    def weight_copy(i):
        start, rows, _ = PIECES[i]
        view = weights.at[yl, pl.ds(start, rows)]
        return pltpu.make_async_remote_copy(
            src_ref=view, dst_ref=view, send_sem=w_send.at[i], recv_sem=w_recv.at[i],
            device_id=lo_partner, device_id_type=MESH,
        )

    for i, (_, _, when) in enumerate(PIECES):
        if when < 0:
            weight_copy(i).start()

    def cross_copy():
        return pltpu.make_async_remote_copy(
            src_ref=scaled, dst_ref=tokens.at[yh, my_source, yl, mine],
            send_sem=cross_send.at[0], recv_sem=tok_recv.at[yh, my_source, yl, c],
            device_id=lo_partner, device_id_type=MESH,
        )

    def token_copy(h, source, kb, sems, target):
        view = tokens.at[h, source, kb, mine]
        return pltpu.make_async_remote_copy(
            src_ref=view, dst_ref=view, send_sem=sems.at[h, source, kb],
            recv_sem=tok_recv.at[h, source, kb, c], device_id=target, device_id_type=MESH,
        )

    def token_arrival(h, source, kb, core):
        view = tokens.at[h, source, kb, pl.ds(pl.multiple_of(core * ROWS, ROWS), ROWS)]
        return pltpu.make_async_remote_copy(
            src_ref=view, dst_ref=view, send_sem=sib_send.at[h, source, kb],
            recv_sem=tok_recv.at[h, source, kb, core], device_id=sibling, device_id_type=MESH,
        )

    def event_code(event, v):
        unit, half, block = EVENTS[v // 2][event]
        bits = (
            half, block, ONWARD_UP[half][unit][v], ONWARD_DOWN[half][unit][v],
            CROSSES[unit][v] * (1 - half), int(unit == 0 and v < 2 and half == 0),
        )
        return OFFSETS[unit][v] + 4 + sum(b << (4 + i) for i, b in enumerate(bits))

    def group_code(step, v):
        unit, half = GROUPS[v // 2][step]
        return OFFSETS[unit][v] + 4 + (half << 4)

    event_codes = [pick(w, [event_code(e, v) for v in range(4)]) for e in range(16)]
    group_codes = [pick(w, [group_code(g, v) for v in range(4)]) for g in range(8)]

    def bit(code, i):
        return lax.rem(code // 2**i, 2)

    def unit_of(code):
        source_z = lax.rem(z + lax.rem(code, 16) + 4, 8)
        source = (source_z // 4) * 2 + lax.rem(source_z, 2)
        return lax.rem(yh + bit(code, 4), 2), source

    def group_of(step):
        return unit_of(pick(step, group_codes))

    def event_of(event):
        code = pick(event, event_codes)
        h, source = unit_of(code)
        block = bit(code, 5)
        goes = (bit(code, 6) == 1, bit(code, 7) == 1, block >= 0, bit(code, 8) == 1)
        return h, source, block, goes, bit(code, 9) == 1

    def onward(h, source, kb, goes):
        ways = ((up_send, above), (down_send, below), (sib_send, sibling), (hi_send, hi_partner))
        return [
            (wanted, token_copy(h, source, kb, sems, target))
            for wanted, (sems, target) in zip(goes, ways)
        ]

    def owned_here(h, source):
        return h * 2 + source // 2 == x

    def handle(event):
        h, source, block, goes, at_home = event_of(event)
        kb = lax.rem(yl + block, 2)

        @pl.when(jnp.logical_not(jnp.logical_and(at_home, block == 0)))
        def _():
            token_arrival(h, source, kb, c).wait_recv()

        for wanted, copy in onward(h, source, kb, goes):
            @pl.when(wanted)
            def _():
                copy.start()

        @pl.when(jnp.logical_and(owned_here(h, source), block == 1))
        def _():
            low = lax.rem(source, 2)

            @pl.when(at_home)
            def _():
                squares_to_inverse()

            @pl.when(jnp.logical_not(at_home))
            def _():
                inverse_copy(low, c, 0, sibling).wait_recv()

            for wanted, copy in inverse_onward(goes, low):
                @pl.when(wanted)
                def _():
                    copy.start()

    def role_of(h, source):
        return lax.rem(x - (h * 2 + source // 2) + 4, 4)

    def goes_up(source, part):
        return lax.rem(source + part + c, 2) == 0

    def sum_copy(h, source, quarter):
        rows = pl.ds(quarter * QUARTER, QUARTER)
        slot = role_of(h, source) // 2
        low = lax.rem(source, 2)
        return pltpu.make_async_remote_copy(
            src_ref=staged.at[h, source, rows], dst_ref=landed.at[slot, low, rows],
            send_sem=sum_send.at[h, source, quarter], recv_sem=sum_recv.at[slot, low, quarter],
            device_id=device(yh, z, c, h * 2 + source // 2, yl), device_id_type=MESH,
        )

    def relay_copy(h, source, quarter):
        towards = lax.rem(x + jnp.where(goes_up(source, quarter // 2), 1, 3), 4)
        return pltpu.make_async_remote_copy(
            src_ref=staged.at[h, source, pl.ds(quarter * QUARTER, QUARTER)],
            dst_ref=relayed.at[h, source, quarter % 2],
            send_sem=relay_send.at[h, source, quarter], recv_sem=relay_recv.at[h, source, quarter % 2],
            device_id=device(yh, z, c, towards, yl), device_id_type=MESH,
        )

    def relays(role, source, part):
        return jnp.logical_and(lax.rem(role, 2) == 1, (role == 3) == goes_up(source, part))

    def multiply(step, part):
        h, source = group_of(step)
        rows = pl.ds(part * HALF, HALF)
        across_k = (((1,), (1,)), ((), ()))
        product = lax.dot_general(
            weights[0, rows], tokens[h, source, 0], across_k, preferred_element_type=jnp.float32
        ) + lax.dot_general(
            weights[1, rows], tokens[h, source, 1], across_k, preferred_element_type=jnp.float32
        )
        role = role_of(h, source)

        @pl.when(role == 0)
        def _():
            own_sum[lax.rem(source, 2), rows] = product

        @pl.when(role != 0)
        def _():
            staged[h, source, rows] = product.astype(jnp.bfloat16)

        @pl.when(role == 2)
        def _():
            for quarter in (2 * part, 2 * part + 1):
                relay_copy(h, source, quarter).start()

        @pl.when(jnp.logical_and(lax.rem(role, 2) == 1, jnp.logical_not(relays(role, source, part))))
        def _():
            for quarter in (2 * part, 2 * part + 1):
                sum_copy(h, source, quarter).start()

    def add_relayed(step, part):
        h, source = group_of(step)

        @pl.when(relays(role_of(h, source), source, part))
        def _():
            for quarter in (2 * part, 2 * part + 1):
                rows = pl.ds(quarter * QUARTER, QUARTER)
                relay_copy(h, source, quarter).wait_recv()
                staged[h, source, rows] = (
                    staged[h, source, rows].astype(jnp.float32)
                    + relayed[h, source, quarter % 2].astype(jnp.float32)
                ).astype(jnp.bfloat16)
                sum_copy(h, source, quarter).start()

    def sibling_arrived(step):
        h, source = group_of(step)
        for i in range(2):
            token_arrival(h, source, i, 1 - c).wait_recv()

    owner_mp = (yh * 2 + z // 4) * 2 + lax.rem(z // 2, 2)

    def square_copy():
        view = squares.at[mp]
        return pltpu.make_async_remote_copy(
            src_ref=view, dst_ref=view, send_sem=sq_send.at[0], recv_sem=sq_recv.at[mp],
            device_id=(chip * 2 + c, owner_mp), device_id_type=MESH,
        )

    def squares_to_inverse():
        for i in range(1, 8):
            slot = lax.rem(mp + i, 8)
            view = squares.at[slot]
            pltpu.make_async_remote_copy(
                src_ref=view, dst_ref=view, send_sem=sq_send.at[0], recv_sem=sq_recv.at[slot],
                device_id=lo_partner, device_id_type=MESH,
            ).wait_recv()
        inverse[lax.rem(z, 2), c] = lax.rsqrt(jnp.sum(squares[...], axis=0) / D + 1e-05)

    def inverse_copy(low, core, way, target):
        view = inverse.at[low, core]
        return pltpu.make_async_remote_copy(
            src_ref=view, dst_ref=view, send_sem=inv_send.at[low, way], recv_sem=inv_recv.at[low, core],
            device_id=target, device_id_type=MESH,
        )

    def inverse_onward(wanted, low):
        targets = (above, below, sibling, hi_partner)
        return [(want, inverse_copy(low, c, way, target)) for way, (want, target) in enumerate(zip(wanted, targets))]

    def weights_arrived(part):
        for i, (start, rows, _) in enumerate(PIECES):
            if start // HALF == part:
                view = weights.at[1 - yl, pl.ds(start, rows)]
                pltpu.make_async_remote_copy(
                    src_ref=view, dst_ref=view, send_sem=w_send.at[i], recv_sem=w_recv.at[i],
                    device_id=lo_partner, device_id_type=MESH,
                ).wait_recv()

    for load in loads[2:4]:
        load.wait()
    for head in range(8):
        by_head[head // 2, (head % 2) * ROWS:(head % 2 + 1) * ROWS] = query[:, head * HD:(head + 1) * HD]
    running_max[...] = jnp.full_like(running_max, -1e30)
    denominator[...] = jnp.zeros_like(denominator)
    weighted[...] = jnp.zeros_like(weighted)
    query_pos = (chip * 2 + c) * ROWS + lax.broadcasted_iota(jnp.int32, (1, ROWS), 1)
    starts = document_starts(lengths_ref, query_pos)

    def attend(j):
        key_pos = (chip - j) * 256 + lax.broadcasted_iota(jnp.int32, (256, ROWS), 0)
        visible = jnp.logical_and(key_pos >= starts, key_pos <= query_pos)
        bias = jnp.where(visible, 0.0, -1e30)
        bias = jnp.concatenate([bias, bias], axis=1)

        scores = [
            lax.dot_general(
                keys_values[j, 0], by_head[i], (((1,), (1,)), ((), ())),
                preferred_element_type=jnp.float32,
            ) * HD ** (-0.5) + bias
            for i in range(4)
        ]
        olds = [running_max[i] for i in range(4)]
        news = [jnp.maximum(olds[i], jnp.max(scores[i], axis=0, keepdims=True)) for i in range(4)]
        for i in range(4):
            factor = jnp.exp(olds[i] - news[i])
            parts = jnp.exp(scores[i] - news[i])
            running_max[i] = news[i]
            denominator[i] = denominator[i] * factor + jnp.sum(parts, axis=0, keepdims=True)
            weighted[i] = weighted[i] * factor + lax.dot_general(
                keys_values[j, 1], parts.astype(jnp.bfloat16), (((0,), (0,)), ((), ())),
                preferred_element_type=jnp.float32,
            )

    def attend_step(j, _):
        @pl.when(jnp.logical_and(j < 4, chip > j))
        def _():
            kv_arrival(j + 1, c).wait_recv()

            @pl.when(jnp.logical_and(j == 1, kv_sent(3)))
            def _():
                kv_onward(3).start()

            kv_sibling(j + 1).start()

        @pl.when(jnp.logical_and(j < 4, chip <= j))
        def _():
            keys_values[j + 1] = jnp.zeros_like(keys_values[0])

        @pl.when(chip >= j)
        def _():
            kv_arrival(j, 1 - c).wait_recv()

        attend(j)
        return 0

    lax.fori_loop(0, 5, attend_step, 0)

    total = jnp.zeros((ROWS, HD), jnp.float32)
    for head in range(8):
        lanes = slice((head % 2) * ROWS, (head % 2 + 1) * ROWS)
        columns = slice(head * HD, (head + 1) * HD)
        attended = (weighted[head // 2, :, lanes] / denominator[head // 2, :, lanes]).T
        rounded = (residual_in[:, columns].astype(jnp.float32) + attended).astype(jnp.bfloat16)
        residual_ref[:, columns] = rounded
        wide = rounded.astype(jnp.float32)
        total = total + wide * wide
        scaled[:, columns] = (wide * gain_ref[columns].astype(jnp.float32)[None, :]).astype(jnp.bfloat16)

    @pl.when(match)
    def _():
        tokens[yh, my_source, yl, mine] = scaled[...]

    @pl.when(jnp.logical_not(match))
    def _():
        cross_copy().start()

    squares[mp] = jnp.broadcast_to(jnp.sum(total.T, axis=0, keepdims=True), (8, ROWS))

    @pl.when(mp != owner_mp)
    def _():
        square_copy().start()

    def handle_until(step):
        def one(event, _):
            handle(event)
            return 0

        lax.fori_loop(pick(step, (0,) + BEFORE[:-1]), pick(step, BEFORE), one, 0)

    def step_through(step, _):
        handle_until(step)
        for i, (_, _, when) in enumerate(PIECES):
            if when >= 0:
                @pl.when(step == when)
                def _():
                    weight_copy(i).start()

        def each(counts, work):
            def one(group, _):
                work(group)
                return 0

            lax.fori_loop(pick(step, (0,) + counts[:-1]), pick(step, counts), one, 0)

        def gate_group(group):
            sibling_arrived(group)
            multiply(group, 0)

        @pl.when(step == 2)
        def _():
            weights_arrived(0)

        each(GATED, gate_group)

        @pl.when(step == 3)
        def _():
            weights_arrived(1)

        each(UPPED, lambda group: multiply(group, 1))

        def relay_group(group):
            for part in range(2):
                add_relayed(group, part)

        each(RELAYED, relay_group)
        return 0

    lax.fori_loop(0, 8, step_through, 0)

    def last(step, _):
        for part in range(2):
            add_relayed(step, part)
        return 0

    lax.fori_loop(RELAYED[-1], 8, last, 0)

    for i in range(4):
        @pl.when(kv_sent(i))
        def _():
            kv_onward(i).wait_send()
    for j in range(5):
        @pl.when(chip >= j)
        def _():
            kv_sibling(j).wait_send()

    @pl.when(mp != owner_mp)
    def _():
        square_copy().wait_send()

    for i in range(len(PIECES)):
        weight_copy(i).wait_send()

    @pl.when(jnp.logical_not(match))
    def _():
        cross_copy().wait_send()

    def tokens_sent(event, _):
        h, source, block, goes, _ = event_of(event)
        for wanted, copy in onward(h, source, lax.rem(yl + block, 2), goes):
            @pl.when(wanted)
            def _():
                copy.wait_send()

        @pl.when(jnp.logical_and(owned_here(h, source), block == 1))
        def _():
            for wanted, copy in inverse_onward(goes, lax.rem(source, 2)):
                @pl.when(wanted)
                def _():
                    copy.wait_send()

        return 0

    lax.fori_loop(0, 16, tokens_sent, 0)

    for low in range(2):
        inverse_copy(low, 1 - c, 0, sibling).wait_recv()
        scale = jnp.concatenate([inverse[low, 0], inverse[low, 1]], axis=1)[0:1]
        def total_of(quarter):
            rows = pl.ds(quarter * QUARTER, QUARTER)
            total = own_sum[low, rows]
            for slot in range(2):
                view = landed.at[slot, low, rows]
                pltpu.make_async_remote_copy(
                    src_ref=view, dst_ref=view, send_sem=sum_send.at[0, 0, quarter],
                    recv_sem=sum_recv.at[slot, low, quarter], device_id=x_peers[0], device_id_type=MESH,
                ).wait_recv()
                total = total + landed[slot, low, rows].astype(jnp.float32)
            return total * scale

        for i in range(2):
            gate, up = total_of(i), total_of(2 + i)
            out_ref[i * QUARTER:(i + 1) * QUARTER, low * 256:(low + 1) * 256] = (
                gate / (1.0 + jnp.exp(-gate)) * up
            ).astype(jnp.bfloat16)

    def sums_sent(step, _):
        h, source = group_of(step)
        role = role_of(h, source)
        for quarter in range(4):
            @pl.when(role == 2)
            def _():
                relay_copy(h, source, quarter).wait_send()

            @pl.when(lax.rem(role, 2) == 1)
            def _():
                sum_copy(h, source, quarter).wait_send()

        return 0

    lax.fori_loop(0, 8, sums_sent, 0)


def on_device(
    query_heads, key_heads, value_heads, residual_in, norm_gain, gate_weight, up_weight, doc_lengths
):
    dma = pltpu.SemaphoreType.DMA
    vmem = pl.BlockSpec(memory_space=pltpu.VMEM)
    anywhere = pl.BlockSpec(memory_space=pl.ANY)
    residual, hidden = pl.pallas_call(
        layer_kernel,
        out_shape=(
            jax.ShapeDtypeStruct((ROWS, KB), jnp.bfloat16),
            jax.ShapeDtypeStruct((HALF, 4 * ROWS), jnp.bfloat16),
        ),
        in_specs=[pl.BlockSpec(memory_space=pltpu.SMEM)] + [anywhere] * 4 + [vmem] + [anywhere] * 2,
        out_specs=(vmem, vmem),
        scratch_shapes=[
            pltpu.VMEM((2, 4, 2, 2 * ROWS, KB), jnp.bfloat16),
            pltpu.VMEM((2, WIDTH, KB), jnp.bfloat16),
            pltpu.VMEM((2, 4, WIDTH, 2 * ROWS), jnp.bfloat16),
            pltpu.VMEM((2, 4, 2, QUARTER, 2 * ROWS), jnp.bfloat16),
            pltpu.VMEM((2, 2, WIDTH, 2 * ROWS), jnp.bfloat16),
            pltpu.VMEM((2, WIDTH, 2 * ROWS), jnp.float32),
            pltpu.VMEM((ROWS, KB), jnp.bfloat16),
            pltpu.VMEM((4, 2 * ROWS, HD), jnp.bfloat16),
            pltpu.VMEM((5, 2, 2 * ROWS, HD), jnp.bfloat16),
            pltpu.VMEM((ROWS, KB), jnp.bfloat16),
            pltpu.VMEM((ROWS, KB), jnp.bfloat16),
            pltpu.VMEM((8, 8, ROWS), jnp.float32),
            pltpu.VMEM((2, 2, 8, ROWS), jnp.float32),
            pltpu.VMEM((4, 1, 2 * ROWS), jnp.float32),
            pltpu.VMEM((4, 1, 2 * ROWS), jnp.float32),
            pltpu.VMEM((4, HD, 2 * ROWS), jnp.float32),
            dma((6,)), dma((4,)), dma((5,)), dma((5, 2)), dma((1,)), dma((8,)), dma((2, 4)), dma((2, 2)),
            dma((3,)), dma((3,)), dma((1,)), dma((2, 4, 2, 2)),
            dma((2, 4, 2)), dma((2, 4, 2)), dma((2, 4, 2)), dma((2, 4, 2)),
            dma((2, 4, 4)), dma((2, 4, 2)), dma((2, 4, 4)), dma((2, 2, 4)),
        ],
        compiler_params=pltpu.CompilerParams(
            collective_id=0, has_side_effects=True, vmem_limit_bytes=56 * 2**20
        ),
        name="layer",
    )(
        doc_lengths, query_heads, key_heads, value_heads, residual_in,
        norm_gain, gate_weight.T, up_weight.T,
    )
    return residual, hidden.T


def solution(mesh):
    in_specs = (
        P("ctx", "mp"),
        P("ctx", "mp"),
        P("ctx", "mp"),
        P("ctx", "mp"),
        P("mp"),
        P("mp", "ctx"),
        P("mp", "ctx"),
        P(),
    )
    out_specs = (P("ctx", "mp"), P("mp", "ctx"))
    return jax.shard_map(
        on_device, mesh=mesh, in_specs=in_specs, out_specs=out_specs, check_vma=False
    )
```

```python
import functools

import jax
import jax.numpy as jnp
from jax import lax
from jax.experimental import pallas as pl
from jax.experimental.pallas import tpu as pltpu
from jax.sharding import PartitionSpec as P

D = 8192
HD = 128
MESH = pl.DeviceIdType.MESH
ROWS = 128
KB = 1024
HALF = 448
WIDTH = 2 * HALF
QUARTER = HALF // 2


def place():
    ctx = lax.axis_index("ctx")
    mp = lax.axis_index("mp")
    return ctx // 16, lax.rem(ctx // 2, 8), lax.rem(ctx, 2), mp // 2, lax.rem(mp, 2)


def device(yh, z, c, x, yl):
    return (yh * 16 + z * 2 + c, x * 2 + yl)


def pick(w, values):
    out = jnp.int32(values[0])
    for i in range(1, len(values)):
        out = jnp.where(w == i, jnp.int32(values[i]), out)
    return out


OFFSETS = ((0, 0, -1, 1), (1, -1, 2, -2), (-3, 3, -2, 2), (4, -4, 3, -3))
ONWARD_UP = (
    ((1, 1, 1, 0), (0, 1, 0, 1), (1, 0, 1, 0), (0, 0, 0, 0)),
    ((1, 1, 1, 0), (0, 1, 0, 1), (1, 0, 1, 0), (0, 0, 0, 0)),
)
ONWARD_DOWN = (
    ((1, 1, 0, 1), (1, 0, 1, 0), (0, 1, 0, 1), (0, 0, 0, 0)),
    ((1, 1, 0, 1), (1, 0, 1, 0), (0, 1, 0, 1), (0, 0, 0, 0)),
)
CROSSES = ((1, 1, 0, 0), (0, 0, 0, 0), (0, 0, 0, 0), (0, 0, 0, 0))
EVENTS = (
    ((0, 0, 0), (0, 0, 1), (1, 0, 0), (0, 1, 0), (0, 1, 1), (1, 0, 1), (2, 0, 0), (1, 1, 0), (2, 0, 1), (3, 0, 0), (1, 1, 1), (2, 1, 0), (3, 0, 1), (2, 1, 1), (3, 1, 0), (3, 1, 1)),
    ((0, 0, 0), (0, 0, 1), (1, 0, 0), (2, 0, 0), (1, 0, 1), (0, 1, 0), (0, 1, 1), (1, 1, 0), (3, 0, 0), (1, 1, 1), (2, 0, 1), (2, 1, 0), (2, 1, 1), (3, 0, 1), (3, 1, 0), (3, 1, 1)),
)
GROUPS = (
    ((0, 0), (0, 1), (1, 0), (2, 0), (1, 1), (3, 0), (2, 1), (3, 1)),
    ((0, 0), (1, 0), (0, 1), (1, 1), (2, 0), (2, 1), (3, 0), (3, 1)),
)
BEFORE = (3, 6, 8, 11, 12, 14, 15, 16)
PIECES = ((0, 320, -1), (320, 128, 0), (448, 448, 0))
GATED = (0, 0, 3, 4, 5, 6, 7, 8)
UPPED = (0, 0, 0, 4, 5, 6, 7, 8)
RELAYED = (0, 0, 0, 0, 1, 2, 3, 4)


def document_starts(lengths_ref, positions):
    starts = jnp.zeros_like(positions)
    end = jnp.int32(0)
    for i in range(lengths_ref.shape[0]):
        end = end + lengths_ref[i]
        starts = jnp.where(positions >= end, end, starts)
    return starts


def layer_kernel(
    lengths_ref, query_ref, key_ref, value_ref, residual_in_ref, gain_ref, gate_ref, up_ref,
    residual_ref, out_ref,
    tokens, weights, staged, relayed, landed, own_sum,
    query, by_head, keys_values, residual_in, scaled, squares, inverse,
    running_max, denominator, weighted,
    load_sem, kv_send, kv_sib_send, kv_recv, sq_send, sq_recv, inv_send, inv_recv,
    w_send, w_recv, cross_send, tok_recv, up_send, down_send, sib_send, hi_send, relay_send, relay_recv, sum_send, sum_recv,
):
    yh, z, c, x, yl = place()
    match = lax.rem(z // 2, 2) == yl
    w = lax.rem(z - 2 * yl + 8, 4)
    my_source = (z // 4) * 2 + lax.rem(z, 2)
    sibling = device(yh, z, 1 - c, x, yl)
    lo_partner = device(yh, z, c, x, 1 - yl)
    hi_partner = device(1 - yh, z, c, x, yl)
    above = device(yh, lax.rem(z + 1, 8), c, x, yl)
    below = device(yh, lax.rem(z + 7, 8), c, x, yl)
    x_peers = [device(yh, z, c, lax.rem(x + d, 4), yl) for d in (1, 2, 3)]
    mine = pl.ds(pl.multiple_of(c * ROWS, ROWS), ROWS)

    mp = x * 2 + yl
    chip = yh * 8 + z
    step_on = lambda k: device(lax.rem((chip + 16 + k) // 8, 2), lax.rem(chip + 16 + k, 8), c, x, yl)
    kv_hops = ((0, 1, step_on(1)), (0, 2, step_on(2)), (1, 2, step_on(2)), (2, 2, step_on(2)))

    loads = [
        pltpu.make_async_copy(key_ref, keys_values.at[0, 0, mine], load_sem.at[0]),
        pltpu.make_async_copy(value_ref, keys_values.at[0, 1, mine], load_sem.at[1]),
        pltpu.make_async_copy(query_ref, query, load_sem.at[2]),
        pltpu.make_async_copy(residual_in_ref, residual_in, load_sem.at[3]),
        pltpu.make_async_copy(gate_ref, weights.at[yl, pl.ds(0, HALF)], load_sem.at[4]),
        pltpu.make_async_copy(up_ref, weights.at[yl, pl.ds(HALF, HALF)], load_sem.at[5]),
    ]
    for load in loads:
        load.start()

    barrier = pltpu.get_barrier_semaphore()
    across = [device(yh, z, c, lax.rem(x + d, 4), 1 - yl) for d in (1, 2, 3)]
    peers = [sibling, lo_partner, hi_partner, above, below] + x_peers + across
    for peer in peers:
        pl.semaphore_signal(barrier, inc=1, device_id=peer, device_id_type=MESH)

    @pl.when(chip == 8)
    def _():
        pl.semaphore_signal(barrier, inc=1, device_id=step_on(-1), device_id_type=MESH)

    @pl.when(chip >= 2)
    def _():
        pl.semaphore_signal(barrier, inc=1, device_id=step_on(-2), device_id_type=MESH)

    pl.semaphore_wait(
        barrier,
        len(peers) + jnp.where(chip == 7, 1, 0) + jnp.where(chip < 14, 1, 0),
    )
    for load in loads[:2]:
        load.wait()

    def kv_onward(i):
        j, ahead, target = kv_hops[i]
        return pltpu.make_async_remote_copy(
            src_ref=keys_values.at[j, :, mine], dst_ref=keys_values.at[j + ahead, :, mine],
            send_sem=kv_send.at[i], recv_sem=kv_recv.at[j + ahead, c],
            device_id=target, device_id_type=MESH,
        )

    def kv_sent(i):
        j, ahead, _ = kv_hops[i]
        return jnp.logical_and(chip >= j, chip < 16 - ahead)

    def kv_sibling(j):
        view = keys_values.at[j, :, mine]
        return pltpu.make_async_remote_copy(
            src_ref=view, dst_ref=view, send_sem=kv_sib_send.at[j], recv_sem=kv_recv.at[j, c],
            device_id=sibling, device_id_type=MESH,
        )

    def kv_arrival(j, core):
        view = keys_values.at[j, :, pl.ds(pl.multiple_of(core * ROWS, ROWS), ROWS)]
        return pltpu.make_async_remote_copy(
            src_ref=view, dst_ref=view, send_sem=kv_sib_send.at[j], recv_sem=kv_recv.at[j, core],
            device_id=sibling, device_id_type=MESH,
        )

    for i in range(2):
        @pl.when(kv_sent(i))
        def _():
            kv_onward(i).start()

    kv_sibling(0).start()

    for load in loads[4:]:
        load.wait()

    def weight_copy(i):
        start, rows, _ = PIECES[i]
        view = weights.at[yl, pl.ds(start, rows)]
        return pltpu.make_async_remote_copy(
            src_ref=view, dst_ref=view, send_sem=w_send.at[i], recv_sem=w_recv.at[i],
            device_id=lo_partner, device_id_type=MESH,
        )

    for i, (_, _, when) in enumerate(PIECES):
        if when < 0:
            weight_copy(i).start()

    def cross_copy():
        return pltpu.make_async_remote_copy(
            src_ref=scaled, dst_ref=tokens.at[yh, my_source, yl, mine],
            send_sem=cross_send.at[0], recv_sem=tok_recv.at[yh, my_source, yl, c],
            device_id=lo_partner, device_id_type=MESH,
        )

    def token_copy(h, source, kb, sems, target):
        view = tokens.at[h, source, kb, mine]
        return pltpu.make_async_remote_copy(
            src_ref=view, dst_ref=view, send_sem=sems.at[h, source, kb],
            recv_sem=tok_recv.at[h, source, kb, c], device_id=target, device_id_type=MESH,
        )

    def token_arrival(h, source, kb, core):
        view = tokens.at[h, source, kb, pl.ds(pl.multiple_of(core * ROWS, ROWS), ROWS)]
        return pltpu.make_async_remote_copy(
            src_ref=view, dst_ref=view, send_sem=sib_send.at[h, source, kb],
            recv_sem=tok_recv.at[h, source, kb, core], device_id=sibling, device_id_type=MESH,
        )

    def event_code(event, v):
        unit, half, block = EVENTS[v // 2][event]
        bits = (
            half, block, ONWARD_UP[half][unit][v], ONWARD_DOWN[half][unit][v],
            CROSSES[unit][v] * (1 - half), int(unit == 0 and v < 2 and half == 0),
        )
        return OFFSETS[unit][v] + 4 + sum(b << (4 + i) for i, b in enumerate(bits))

    def group_code(step, v):
        unit, half = GROUPS[v // 2][step]
        return OFFSETS[unit][v] + 4 + (half << 4)

    event_codes = [pick(w, [event_code(e, v) for v in range(4)]) for e in range(16)]
    group_codes = [pick(w, [group_code(g, v) for v in range(4)]) for g in range(8)]

    def bit(code, i):
        return lax.rem(code // 2**i, 2)

    def unit_of(code):
        source_z = lax.rem(z + lax.rem(code, 16) + 4, 8)
        source = (source_z // 4) * 2 + lax.rem(source_z, 2)
        return lax.rem(yh + bit(code, 4), 2), source

    def group_of(step):
        return unit_of(pick(step, group_codes))

    def event_of(event):
        code = pick(event, event_codes)
        h, source = unit_of(code)
        block = bit(code, 5)
        goes = (bit(code, 6) == 1, bit(code, 7) == 1, block >= 0, bit(code, 8) == 1)
        return h, source, block, goes, bit(code, 9) == 1

    def onward(h, source, kb, goes):
        ways = ((up_send, above), (down_send, below), (sib_send, sibling), (hi_send, hi_partner))
        return [
            (wanted, token_copy(h, source, kb, sems, target))
            for wanted, (sems, target) in zip(goes, ways)
        ]

    def owned_here(h, source):
        return h * 2 + source // 2 == x

    def handle(event):
        h, source, block, goes, at_home = event_of(event)
        kb = lax.rem(yl + block, 2)

        @pl.when(jnp.logical_not(jnp.logical_and(at_home, block == 0)))
        def _():
            token_arrival(h, source, kb, c).wait_recv()

        for wanted, copy in onward(h, source, kb, goes):
            @pl.when(wanted)
            def _():
                copy.start()

        @pl.when(jnp.logical_and(owned_here(h, source), block == 1))
        def _():
            low = lax.rem(source, 2)

            @pl.when(at_home)
            def _():
                squares_to_inverse()

            @pl.when(jnp.logical_not(at_home))
            def _():
                inverse_copy(low, c, 0, sibling).wait_recv()

            for wanted, copy in inverse_onward(goes, low):
                @pl.when(wanted)
                def _():
                    copy.start()

    def role_of(h, source):
        return lax.rem(x - (h * 2 + source // 2) + 4, 4)

    def goes_up(source, part):
        return lax.rem(source + part + c, 2) == 0

    def sum_copy(h, source, quarter):
        rows = pl.ds(quarter * QUARTER, QUARTER)
        slot = role_of(h, source) // 2
        low = lax.rem(source, 2)
        return pltpu.make_async_remote_copy(
            src_ref=staged.at[h, source, rows], dst_ref=landed.at[slot, low, rows],
            send_sem=sum_send.at[h, source, quarter], recv_sem=sum_recv.at[slot, low, quarter],
            device_id=device(yh, z, c, h * 2 + source // 2, yl), device_id_type=MESH,
        )

    def relay_copy(h, source, quarter):
        towards = lax.rem(x + jnp.where(goes_up(source, quarter // 2), 1, 3), 4)
        return pltpu.make_async_remote_copy(
            src_ref=staged.at[h, source, pl.ds(quarter * QUARTER, QUARTER)],
            dst_ref=relayed.at[h, source, quarter % 2],
            send_sem=relay_send.at[h, source, quarter], recv_sem=relay_recv.at[h, source, quarter % 2],
            device_id=device(yh, z, c, towards, yl), device_id_type=MESH,
        )

    def relays(role, source, part):
        return jnp.logical_and(lax.rem(role, 2) == 1, (role == 3) == goes_up(source, part))

    def multiply(step, part):
        h, source = group_of(step)
        rows = pl.ds(part * HALF, HALF)
        across_k = (((1,), (1,)), ((), ()))
        product = lax.dot_general(
            weights[0, rows], tokens[h, source, 0], across_k, preferred_element_type=jnp.float32
        ) + lax.dot_general(
            weights[1, rows], tokens[h, source, 1], across_k, preferred_element_type=jnp.float32
        )
        role = role_of(h, source)

        @pl.when(role == 0)
        def _():
            own_sum[lax.rem(source, 2), rows] = product

        @pl.when(role != 0)
        def _():
            staged[h, source, rows] = product.astype(jnp.bfloat16)

        @pl.when(role == 2)
        def _():
            for quarter in (2 * part, 2 * part + 1):
                relay_copy(h, source, quarter).start()

        @pl.when(jnp.logical_and(lax.rem(role, 2) == 1, jnp.logical_not(relays(role, source, part))))
        def _():
            for quarter in (2 * part, 2 * part + 1):
                sum_copy(h, source, quarter).start()

    def add_relayed(step, part):
        h, source = group_of(step)

        @pl.when(relays(role_of(h, source), source, part))
        def _():
            for quarter in (2 * part, 2 * part + 1):
                rows = pl.ds(quarter * QUARTER, QUARTER)
                relay_copy(h, source, quarter).wait_recv()
                staged[h, source, rows] = (
                    staged[h, source, rows].astype(jnp.float32)
                    + relayed[h, source, quarter % 2].astype(jnp.float32)
                ).astype(jnp.bfloat16)
                sum_copy(h, source, quarter).start()

    def sibling_arrived(step):
        h, source = group_of(step)
        for i in range(2):
            token_arrival(h, source, i, 1 - c).wait_recv()

    owner_mp = (yh * 2 + z // 4) * 2 + lax.rem(z // 2, 2)

    def square_copy():
        view = squares.at[mp]
        return pltpu.make_async_remote_copy(
            src_ref=view, dst_ref=view, send_sem=sq_send.at[0], recv_sem=sq_recv.at[mp],
            device_id=(chip * 2 + c, owner_mp), device_id_type=MESH,
        )

    def squares_to_inverse():
        for i in range(1, 8):
            slot = lax.rem(mp + i, 8)
            view = squares.at[slot]
            pltpu.make_async_remote_copy(
                src_ref=view, dst_ref=view, send_sem=sq_send.at[0], recv_sem=sq_recv.at[slot],
                device_id=lo_partner, device_id_type=MESH,
            ).wait_recv()
        inverse[lax.rem(z, 2), c] = lax.rsqrt(jnp.sum(squares[...], axis=0) / D + 1e-05)

    def inverse_copy(low, core, way, target):
        view = inverse.at[low, core]
        return pltpu.make_async_remote_copy(
            src_ref=view, dst_ref=view, send_sem=inv_send.at[low, way], recv_sem=inv_recv.at[low, core],
            device_id=target, device_id_type=MESH,
        )

    def inverse_onward(wanted, low):
        targets = (above, below, sibling, hi_partner)
        return [(want, inverse_copy(low, c, way, target)) for way, (want, target) in enumerate(zip(wanted, targets))]

    def weights_arrived(part):
        for i, (start, rows, _) in enumerate(PIECES):
            if start // HALF == part:
                view = weights.at[1 - yl, pl.ds(start, rows)]
                pltpu.make_async_remote_copy(
                    src_ref=view, dst_ref=view, send_sem=w_send.at[i], recv_sem=w_recv.at[i],
                    device_id=lo_partner, device_id_type=MESH,
                ).wait_recv()

    for load in loads[2:4]:
        load.wait()
    for head in range(8):
        by_head[head // 2, (head % 2) * ROWS:(head % 2 + 1) * ROWS] = query[:, head * HD:(head + 1) * HD]
    running_max[...] = jnp.full_like(running_max, -1e30)
    denominator[...] = jnp.zeros_like(denominator)
    weighted[...] = jnp.zeros_like(weighted)
    query_pos = (chip * 2 + c) * ROWS + lax.broadcasted_iota(jnp.int32, (1, ROWS), 1)
    starts = document_starts(lengths_ref, query_pos)

    def attend(j):
        key_pos = (chip - j) * 256 + lax.broadcasted_iota(jnp.int32, (256, ROWS), 0)
        visible = jnp.logical_and(key_pos >= starts, key_pos <= query_pos)
        bias = jnp.where(visible, 0.0, -1e30)
        bias = jnp.concatenate([bias, bias], axis=1)

        scores = [
            lax.dot_general(
                keys_values[j, 0], by_head[i], (((1,), (1,)), ((), ())),
                preferred_element_type=jnp.float32,
            ) * HD ** (-0.5) + bias
            for i in range(4)
        ]
        olds = [running_max[i] for i in range(4)]
        news = [jnp.maximum(olds[i], jnp.max(scores[i], axis=0, keepdims=True)) for i in range(4)]
        for i in range(4):
            factor = jnp.exp(olds[i] - news[i])
            parts = jnp.exp(scores[i] - news[i])
            running_max[i] = news[i]
            denominator[i] = denominator[i] * factor + jnp.sum(parts, axis=0, keepdims=True)
            weighted[i] = weighted[i] * factor + lax.dot_general(
                keys_values[j, 1], parts.astype(jnp.bfloat16), (((0,), (0,)), ((), ())),
                preferred_element_type=jnp.float32,
            )

    def attend_step(j, _):
        @pl.when(jnp.logical_and(j < 4, chip > j))
        def _():
            kv_arrival(j + 1, c).wait_recv()

            for i in (2, 3):
                @pl.when(jnp.logical_and(j == i - 2, kv_sent(i)))
                def _():
                    kv_onward(i).start()

            kv_sibling(j + 1).start()

        @pl.when(jnp.logical_and(j < 4, chip <= j))
        def _():
            keys_values[j + 1] = jnp.zeros_like(keys_values[0])

        @pl.when(chip >= j)
        def _():
            kv_arrival(j, 1 - c).wait_recv()

        attend(j)
        return 0

    lax.fori_loop(0, 5, attend_step, 0)

    total = jnp.zeros((ROWS, HD), jnp.float32)
    for head in range(8):
        lanes = slice((head % 2) * ROWS, (head % 2 + 1) * ROWS)
        columns = slice(head * HD, (head + 1) * HD)
        attended = (weighted[head // 2, :, lanes] / denominator[head // 2, :, lanes]).T
        rounded = (residual_in[:, columns].astype(jnp.float32) + attended).astype(jnp.bfloat16)
        residual_ref[:, columns] = rounded
        wide = rounded.astype(jnp.float32)
        total = total + wide * wide
        scaled[:, columns] = (wide * gain_ref[columns].astype(jnp.float32)[None, :]).astype(jnp.bfloat16)

    @pl.when(match)
    def _():
        tokens[yh, my_source, yl, mine] = scaled[...]

    @pl.when(jnp.logical_not(match))
    def _():
        cross_copy().start()

    squares[mp] = jnp.broadcast_to(jnp.sum(total.T, axis=0, keepdims=True), (8, ROWS))

    @pl.when(mp != owner_mp)
    def _():
        square_copy().start()

    def handle_until(step):
        def one(event, _):
            handle(event)
            return 0

        lax.fori_loop(pick(step, (0,) + BEFORE[:-1]), pick(step, BEFORE), one, 0)

    def step_through(step, _):
        handle_until(step)
        for i, (_, _, when) in enumerate(PIECES):
            if when >= 0:
                @pl.when(step == when)
                def _():
                    weight_copy(i).start()

        def each(counts, work):
            def one(group, _):
                work(group)
                return 0

            lax.fori_loop(pick(step, (0,) + counts[:-1]), pick(step, counts), one, 0)

        def gate_group(group):
            sibling_arrived(group)
            multiply(group, 0)

        @pl.when(step == 2)
        def _():
            weights_arrived(0)

        each(GATED, gate_group)

        @pl.when(step == 3)
        def _():
            weights_arrived(1)

        each(UPPED, lambda group: multiply(group, 1))

        def relay_group(group):
            for part in range(2):
                add_relayed(group, part)

        each(RELAYED, relay_group)
        return 0

    lax.fori_loop(0, 8, step_through, 0)

    def last(step, _):
        for part in range(2):
            add_relayed(step, part)
        return 0

    lax.fori_loop(RELAYED[-1], 8, last, 0)

    for i in range(4):
        @pl.when(kv_sent(i))
        def _():
            kv_onward(i).wait_send()
    for j in range(5):
        @pl.when(chip >= j)
        def _():
            kv_sibling(j).wait_send()

    @pl.when(mp != owner_mp)
    def _():
        square_copy().wait_send()

    for i in range(len(PIECES)):
        weight_copy(i).wait_send()

    @pl.when(jnp.logical_not(match))
    def _():
        cross_copy().wait_send()

    def tokens_sent(event, _):
        h, source, block, goes, _ = event_of(event)
        for wanted, copy in onward(h, source, lax.rem(yl + block, 2), goes):
            @pl.when(wanted)
            def _():
                copy.wait_send()

        @pl.when(jnp.logical_and(owned_here(h, source), block == 1))
        def _():
            for wanted, copy in inverse_onward(goes, lax.rem(source, 2)):
                @pl.when(wanted)
                def _():
                    copy.wait_send()

        return 0

    lax.fori_loop(0, 16, tokens_sent, 0)

    for low in range(2):
        inverse_copy(low, 1 - c, 0, sibling).wait_recv()
        scale = jnp.concatenate([inverse[low, 0], inverse[low, 1]], axis=1)[0:1]
        def total_of(quarter):
            rows = pl.ds(quarter * QUARTER, QUARTER)
            total = own_sum[low, rows]
            for slot in range(2):
                view = landed.at[slot, low, rows]
                pltpu.make_async_remote_copy(
                    src_ref=view, dst_ref=view, send_sem=sum_send.at[0, 0, quarter],
                    recv_sem=sum_recv.at[slot, low, quarter], device_id=x_peers[0], device_id_type=MESH,
                ).wait_recv()
                total = total + landed[slot, low, rows].astype(jnp.float32)
            return total * scale

        for i in range(2):
            gate, up = total_of(i), total_of(2 + i)
            out_ref[i * QUARTER:(i + 1) * QUARTER, low * 256:(low + 1) * 256] = (
                gate / (1.0 + jnp.exp(-gate)) * up
            ).astype(jnp.bfloat16)

    def sums_sent(step, _):
        h, source = group_of(step)
        role = role_of(h, source)
        for quarter in range(4):
            @pl.when(role == 2)
            def _():
                relay_copy(h, source, quarter).wait_send()

            @pl.when(lax.rem(role, 2) == 1)
            def _():
                sum_copy(h, source, quarter).wait_send()

        return 0

    lax.fori_loop(0, 8, sums_sent, 0)


def on_device(
    query_heads, key_heads, value_heads, residual_in, norm_gain, gate_weight, up_weight, doc_lengths
):
    dma = pltpu.SemaphoreType.DMA
    vmem = pl.BlockSpec(memory_space=pltpu.VMEM)
    anywhere = pl.BlockSpec(memory_space=pl.ANY)
    residual, hidden = pl.pallas_call(
        layer_kernel,
        out_shape=(
            jax.ShapeDtypeStruct((ROWS, KB), jnp.bfloat16),
            jax.ShapeDtypeStruct((HALF, 4 * ROWS), jnp.bfloat16),
        ),
        in_specs=[pl.BlockSpec(memory_space=pltpu.SMEM)] + [anywhere] * 4 + [vmem] + [anywhere] * 2,
        out_specs=(vmem, vmem),
        scratch_shapes=[
            pltpu.VMEM((2, 4, 2, 2 * ROWS, KB), jnp.bfloat16),
            pltpu.VMEM((2, WIDTH, KB), jnp.bfloat16),
            pltpu.VMEM((2, 4, WIDTH, 2 * ROWS), jnp.bfloat16),
            pltpu.VMEM((2, 4, 2, QUARTER, 2 * ROWS), jnp.bfloat16),
            pltpu.VMEM((2, 2, WIDTH, 2 * ROWS), jnp.bfloat16),
            pltpu.VMEM((2, WIDTH, 2 * ROWS), jnp.float32),
            pltpu.VMEM((ROWS, KB), jnp.bfloat16),
            pltpu.VMEM((4, 2 * ROWS, HD), jnp.bfloat16),
            pltpu.VMEM((5, 2, 2 * ROWS, HD), jnp.bfloat16),
            pltpu.VMEM((ROWS, KB), jnp.bfloat16),
            pltpu.VMEM((ROWS, KB), jnp.bfloat16),
            pltpu.VMEM((8, 8, ROWS), jnp.float32),
            pltpu.VMEM((2, 2, 8, ROWS), jnp.float32),
            pltpu.VMEM((4, 1, 2 * ROWS), jnp.float32),
            pltpu.VMEM((4, 1, 2 * ROWS), jnp.float32),
            pltpu.VMEM((4, HD, 2 * ROWS), jnp.float32),
            dma((6,)), dma((4,)), dma((5,)), dma((5, 2)), dma((1,)), dma((8,)), dma((2, 4)), dma((2, 2)),
            dma((3,)), dma((3,)), dma((1,)), dma((2, 4, 2, 2)),
            dma((2, 4, 2)), dma((2, 4, 2)), dma((2, 4, 2)), dma((2, 4, 2)),
            dma((2, 4, 4)), dma((2, 4, 2)), dma((2, 4, 4)), dma((2, 2, 4)),
        ],
        compiler_params=pltpu.CompilerParams(
            collective_id=0, has_side_effects=True, vmem_limit_bytes=56 * 2**20
        ),
        name="layer",
    )(
        doc_lengths, query_heads, key_heads, value_heads, residual_in,
        norm_gain, gate_weight.T, up_weight.T,
    )
    return residual, hidden.T


def solution(mesh):
    in_specs = (
        P("ctx", "mp"),
        P("ctx", "mp"),
        P("ctx", "mp"),
        P("ctx", "mp"),
        P("mp"),
        P("mp", "ctx"),
        P("mp", "ctx"),
        P(),
    )
    out_specs = (P("ctx", "mp"), P("mp", "ctx"))
    return jax.shard_map(
        on_device, mesh=mesh, in_specs=in_specs, out_specs=out_specs, check_vma=False
    )
```

```python
import functools

import jax
import jax.numpy as jnp
from jax import lax
from jax.experimental import pallas as pl
from jax.experimental.pallas import tpu as pltpu
from jax.sharding import PartitionSpec as P

D = 8192
HD = 128
MESH = pl.DeviceIdType.MESH
ROWS = 128
KB = 1024
HALF = 448
WIDTH = 2 * HALF
QUARTER = HALF // 2


def place():
    ctx = lax.axis_index("ctx")
    mp = lax.axis_index("mp")
    return ctx // 16, lax.rem(ctx // 2, 8), lax.rem(ctx, 2), mp // 2, lax.rem(mp, 2)


def device(yh, z, c, x, yl):
    return (yh * 16 + z * 2 + c, x * 2 + yl)


def pick(w, values):
    out = jnp.int32(values[0])
    for i in range(1, len(values)):
        out = jnp.where(w == i, jnp.int32(values[i]), out)
    return out


OFFSETS = ((0, 0, -1, 1), (1, -1, 2, -2), (-3, 3, -2, 2), (4, -4, 3, -3))
ONWARD_UP = (
    ((1, 1, 1, 0), (0, 1, 0, 1), (1, 0, 1, 0), (0, 0, 0, 0)),
    ((1, 1, 1, 0), (0, 1, 0, 1), (1, 0, 1, 0), (0, 0, 0, 0)),
)
ONWARD_DOWN = (
    ((1, 1, 0, 1), (1, 0, 1, 0), (0, 1, 0, 1), (0, 0, 0, 0)),
    ((1, 1, 0, 1), (1, 0, 1, 0), (0, 1, 0, 1), (0, 0, 0, 0)),
)
CROSSES = ((1, 1, 0, 0), (0, 0, 0, 0), (0, 0, 0, 0), (0, 0, 0, 0))
EVENTS = (
    ((0, 0, 0), (0, 0, 1), (1, 0, 0), (0, 1, 0), (0, 1, 1), (1, 0, 1), (2, 0, 0), (1, 1, 0), (2, 0, 1), (3, 0, 0), (1, 1, 1), (2, 1, 0), (3, 0, 1), (2, 1, 1), (3, 1, 0), (3, 1, 1)),
    ((0, 0, 0), (0, 0, 1), (1, 0, 0), (2, 0, 0), (1, 0, 1), (0, 1, 0), (0, 1, 1), (1, 1, 0), (3, 0, 0), (1, 1, 1), (2, 0, 1), (2, 1, 0), (2, 1, 1), (3, 0, 1), (3, 1, 0), (3, 1, 1)),
)
GROUPS = (
    ((0, 0), (0, 1), (1, 0), (2, 0), (1, 1), (3, 0), (2, 1), (3, 1)),
    ((0, 0), (1, 0), (0, 1), (1, 1), (2, 0), (2, 1), (3, 0), (3, 1)),
)
BEFORE = (3, 6, 8, 11, 12, 14, 15, 16)
PIECES = ((0, 320, -1), (320, 128, 0), (448, 448, 0))
GATED = (0, 0, 3, 4, 5, 6, 7, 8)
UPPED = (0, 0, 0, 4, 5, 6, 7, 8)
RELAYED = (0, 0, 0, 0, 1, 2, 3, 4)


def document_starts(lengths_ref, positions):
    starts = jnp.zeros_like(positions)
    end = jnp.int32(0)
    for i in range(lengths_ref.shape[0]):
        end = end + lengths_ref[i]
        starts = jnp.where(positions >= end, end, starts)
    return starts


def layer_kernel(
    lengths_ref, query_ref, key_ref, value_ref, residual_in_ref, gain_ref, gate_ref, up_ref,
    residual_ref, out_ref,
    tokens, weights, staged, relayed, landed, own_sum,
    query, by_head, keys_values, residual_in, scaled, squares, inverse,
    running_max, denominator, weighted,
    load_sem, kv_send, kv_sib_send, kv_recv, sq_send, sq_recv, inv_send, inv_recv,
    w_send, w_recv, cross_send, tok_recv, up_send, down_send, sib_send, hi_send, relay_send, relay_recv, sum_send, sum_recv,
):
    yh, z, c, x, yl = place()
    match = lax.rem(z // 2, 2) == yl
    w = lax.rem(z - 2 * yl + 8, 4)
    my_source = (z // 4) * 2 + lax.rem(z, 2)
    sibling = device(yh, z, 1 - c, x, yl)
    lo_partner = device(yh, z, c, x, 1 - yl)
    hi_partner = device(1 - yh, z, c, x, yl)
    above = device(yh, lax.rem(z + 1, 8), c, x, yl)
    below = device(yh, lax.rem(z + 7, 8), c, x, yl)
    x_peers = [device(yh, z, c, lax.rem(x + d, 4), yl) for d in (1, 2, 3)]
    mine = pl.ds(pl.multiple_of(c * ROWS, ROWS), ROWS)

    mp = x * 2 + yl
    chip = yh * 8 + z
    step_on = lambda k: device(lax.rem((chip + 16 + k) // 8, 2), lax.rem(chip + 16 + k, 8), c, x, yl)
    kv_hops = ((0, 1, step_on(1)), (0, 2, step_on(2)), (1, 2, step_on(2)), (2, 2, step_on(2)))

    loads = [
        pltpu.make_async_copy(key_ref, keys_values.at[0, 0, mine], load_sem.at[0]),
        pltpu.make_async_copy(value_ref, keys_values.at[0, 1, mine], load_sem.at[1]),
        pltpu.make_async_copy(query_ref, query, load_sem.at[2]),
        pltpu.make_async_copy(residual_in_ref, residual_in, load_sem.at[3]),
        pltpu.make_async_copy(gate_ref, weights.at[yl, pl.ds(0, HALF)], load_sem.at[4]),
        pltpu.make_async_copy(up_ref, weights.at[yl, pl.ds(HALF, HALF)], load_sem.at[5]),
    ]
    for load in loads:
        load.start()

    barrier = pltpu.get_barrier_semaphore()
    across = [device(yh, z, c, lax.rem(x + d, 4), 1 - yl) for d in (1, 2, 3)]
    peers = [sibling, lo_partner, hi_partner, above, below] + x_peers + across
    for peer in peers:
        pl.semaphore_signal(barrier, inc=1, device_id=peer, device_id_type=MESH)

    @pl.when(chip == 8)
    def _():
        pl.semaphore_signal(barrier, inc=1, device_id=step_on(-1), device_id_type=MESH)

    @pl.when(chip >= 2)
    def _():
        pl.semaphore_signal(barrier, inc=1, device_id=step_on(-2), device_id_type=MESH)

    pl.semaphore_wait(
        barrier,
        len(peers) + jnp.where(chip == 7, 1, 0) + jnp.where(chip < 14, 1, 0),
    )
    for load in loads[:2]:
        load.wait()

    def kv_onward(i):
        j, ahead, target = kv_hops[i]
        return pltpu.make_async_remote_copy(
            src_ref=keys_values.at[j, :, mine], dst_ref=keys_values.at[j + ahead, :, mine],
            send_sem=kv_send.at[i], recv_sem=kv_recv.at[j + ahead, c],
            device_id=target, device_id_type=MESH,
        )

    def kv_sent(i):
        j, ahead, _ = kv_hops[i]
        return jnp.logical_and(chip >= j, chip < 16 - ahead)

    def kv_sibling(j):
        view = keys_values.at[j, :, mine]
        return pltpu.make_async_remote_copy(
            src_ref=view, dst_ref=view, send_sem=kv_sib_send.at[j], recv_sem=kv_recv.at[j, c],
            device_id=sibling, device_id_type=MESH,
        )

    def kv_arrival(j, core):
        view = keys_values.at[j, :, pl.ds(pl.multiple_of(core * ROWS, ROWS), ROWS)]
        return pltpu.make_async_remote_copy(
            src_ref=view, dst_ref=view, send_sem=kv_sib_send.at[j], recv_sem=kv_recv.at[j, core],
            device_id=sibling, device_id_type=MESH,
        )

    for i in range(2):
        @pl.when(kv_sent(i))
        def _():
            kv_onward(i).start()

    kv_sibling(0).start()

    for load in loads[4:]:
        load.wait()

    def weight_copy(i):
        start, rows, _ = PIECES[i]
        view = weights.at[yl, pl.ds(start, rows)]
        return pltpu.make_async_remote_copy(
            src_ref=view, dst_ref=view, send_sem=w_send.at[i], recv_sem=w_recv.at[i],
            device_id=lo_partner, device_id_type=MESH,
        )

    for i, (_, _, when) in enumerate(PIECES):
        if when < 0:
            weight_copy(i).start()

    def cross_copy():
        return pltpu.make_async_remote_copy(
            src_ref=scaled, dst_ref=tokens.at[yh, my_source, yl, mine],
            send_sem=cross_send.at[0], recv_sem=tok_recv.at[yh, my_source, yl, c],
            device_id=lo_partner, device_id_type=MESH,
        )

    def token_copy(h, source, kb, sems, target):
        view = tokens.at[h, source, kb, mine]
        return pltpu.make_async_remote_copy(
            src_ref=view, dst_ref=view, send_sem=sems.at[h, source, kb],
            recv_sem=tok_recv.at[h, source, kb, c], device_id=target, device_id_type=MESH,
        )

    def token_arrival(h, source, kb, core):
        view = tokens.at[h, source, kb, pl.ds(pl.multiple_of(core * ROWS, ROWS), ROWS)]
        return pltpu.make_async_remote_copy(
            src_ref=view, dst_ref=view, send_sem=sib_send.at[h, source, kb],
            recv_sem=tok_recv.at[h, source, kb, core], device_id=sibling, device_id_type=MESH,
        )

    def event_code(event, v):
        unit, half, block = EVENTS[v // 2][event]
        bits = (
            half, block, ONWARD_UP[half][unit][v], ONWARD_DOWN[half][unit][v],
            CROSSES[unit][v] * (1 - half), int(unit == 0 and v < 2 and half == 0),
        )
        return OFFSETS[unit][v] + 4 + sum(b << (4 + i) for i, b in enumerate(bits))

    def group_code(step, v):
        unit, half = GROUPS[v // 2][step]
        return OFFSETS[unit][v] + 4 + (half << 4)

    event_codes = [pick(w, [event_code(e, v) for v in range(4)]) for e in range(16)]
    group_codes = [pick(w, [group_code(g, v) for v in range(4)]) for g in range(8)]

    def bit(code, i):
        return lax.rem(code // 2**i, 2)

    def unit_of(code):
        source_z = lax.rem(z + lax.rem(code, 16) + 4, 8)
        source = (source_z // 4) * 2 + lax.rem(source_z, 2)
        return lax.rem(yh + bit(code, 4), 2), source

    def group_of(step):
        return unit_of(pick(step, group_codes))

    def event_of(event):
        code = pick(event, event_codes)
        h, source = unit_of(code)
        block = bit(code, 5)
        goes = (bit(code, 6) == 1, bit(code, 7) == 1, block >= 0, bit(code, 8) == 1)
        return h, source, block, goes, bit(code, 9) == 1

    def onward(h, source, kb, goes):
        ways = ((up_send, above), (down_send, below), (sib_send, sibling), (hi_send, hi_partner))
        return [
            (wanted, token_copy(h, source, kb, sems, target))
            for wanted, (sems, target) in zip(goes, ways)
        ]

    def owned_here(h, source):
        return h * 2 + source // 2 == x

    def handle(event):
        h, source, block, goes, at_home = event_of(event)
        kb = lax.rem(yl + block, 2)

        @pl.when(jnp.logical_not(jnp.logical_and(at_home, block == 0)))
        def _():
            token_arrival(h, source, kb, c).wait_recv()

        for wanted, copy in onward(h, source, kb, goes):
            @pl.when(wanted)
            def _():
                copy.start()

        @pl.when(jnp.logical_and(owned_here(h, source), block == 1))
        def _():
            low = lax.rem(source, 2)

            @pl.when(at_home)
            def _():
                squares_to_inverse()

            @pl.when(jnp.logical_not(at_home))
            def _():
                inverse_copy(low, c, 0, sibling).wait_recv()

            for wanted, copy in inverse_onward(goes, low):
                @pl.when(wanted)
                def _():
                    copy.start()

    def role_of(h, source):
        return lax.rem(x - (h * 2 + source // 2) + 4, 4)

    def goes_up(source, part):
        return lax.rem(source + part + c, 2) == 0

    def sum_copy(h, source, quarter):
        rows = pl.ds(quarter * QUARTER, QUARTER)
        slot = role_of(h, source) // 2
        low = lax.rem(source, 2)
        return pltpu.make_async_remote_copy(
            src_ref=staged.at[h, source, rows], dst_ref=landed.at[slot, low, rows],
            send_sem=sum_send.at[h, source, quarter], recv_sem=sum_recv.at[slot, low, quarter],
            device_id=device(yh, z, c, h * 2 + source // 2, yl), device_id_type=MESH,
        )

    def relay_copy(h, source, quarter):
        towards = lax.rem(x + jnp.where(goes_up(source, quarter // 2), 1, 3), 4)
        return pltpu.make_async_remote_copy(
            src_ref=staged.at[h, source, pl.ds(quarter * QUARTER, QUARTER)],
            dst_ref=relayed.at[h, source, quarter % 2],
            send_sem=relay_send.at[h, source, quarter], recv_sem=relay_recv.at[h, source, quarter % 2],
            device_id=device(yh, z, c, towards, yl), device_id_type=MESH,
        )

    def relays(role, source, part):
        return jnp.logical_and(lax.rem(role, 2) == 1, (role == 3) == goes_up(source, part))

    def multiply(step, part):
        h, source = group_of(step)
        rows = pl.ds(part * HALF, HALF)
        across_k = (((1,), (1,)), ((), ()))
        product = lax.dot_general(
            weights[0, rows], tokens[h, source, 0], across_k, preferred_element_type=jnp.float32
        ) + lax.dot_general(
            weights[1, rows], tokens[h, source, 1], across_k, preferred_element_type=jnp.float32
        )
        role = role_of(h, source)

        @pl.when(role == 0)
        def _():
            own_sum[lax.rem(source, 2), rows] = product

        @pl.when(role != 0)
        def _():
            staged[h, source, rows] = product.astype(jnp.bfloat16)

        @pl.when(role == 2)
        def _():
            for quarter in (2 * part, 2 * part + 1):
                relay_copy(h, source, quarter).start()

        @pl.when(jnp.logical_and(lax.rem(role, 2) == 1, jnp.logical_not(relays(role, source, part))))
        def _():
            for quarter in (2 * part, 2 * part + 1):
                sum_copy(h, source, quarter).start()

    def add_relayed(step, part):
        h, source = group_of(step)

        @pl.when(relays(role_of(h, source), source, part))
        def _():
            for quarter in (2 * part, 2 * part + 1):
                rows = pl.ds(quarter * QUARTER, QUARTER)
                relay_copy(h, source, quarter).wait_recv()
                staged[h, source, rows] = (
                    staged[h, source, rows].astype(jnp.float32)
                    + relayed[h, source, quarter % 2].astype(jnp.float32)
                ).astype(jnp.bfloat16)
                sum_copy(h, source, quarter).start()

    def sibling_arrived(step):
        h, source = group_of(step)
        for i in range(2):
            token_arrival(h, source, i, 1 - c).wait_recv()

    owner_mp = (yh * 2 + z // 4) * 2 + lax.rem(z // 2, 2)

    def square_copy():
        view = squares.at[mp]
        return pltpu.make_async_remote_copy(
            src_ref=view, dst_ref=view, send_sem=sq_send.at[0], recv_sem=sq_recv.at[mp],
            device_id=(chip * 2 + c, owner_mp), device_id_type=MESH,
        )

    def squares_to_inverse():
        for i in range(1, 8):
            slot = lax.rem(mp + i, 8)
            view = squares.at[slot]
            pltpu.make_async_remote_copy(
                src_ref=view, dst_ref=view, send_sem=sq_send.at[0], recv_sem=sq_recv.at[slot],
                device_id=lo_partner, device_id_type=MESH,
            ).wait_recv()
        inverse[lax.rem(z, 2), c] = lax.rsqrt(jnp.sum(squares[...], axis=0) / D + 1e-05)

    def inverse_copy(low, core, way, target):
        view = inverse.at[low, core]
        return pltpu.make_async_remote_copy(
            src_ref=view, dst_ref=view, send_sem=inv_send.at[low, way], recv_sem=inv_recv.at[low, core],
            device_id=target, device_id_type=MESH,
        )

    def inverse_onward(wanted, low):
        targets = (above, below, sibling, hi_partner)
        return [(want, inverse_copy(low, c, way, target)) for way, (want, target) in enumerate(zip(wanted, targets))]

    def weights_arrived(part):
        for i, (start, rows, _) in enumerate(PIECES):
            if start // HALF == part:
                view = weights.at[1 - yl, pl.ds(start, rows)]
                pltpu.make_async_remote_copy(
                    src_ref=view, dst_ref=view, send_sem=w_send.at[i], recv_sem=w_recv.at[i],
                    device_id=lo_partner, device_id_type=MESH,
                ).wait_recv()

    for load in loads[2:4]:
        load.wait()
    for head in range(8):
        by_head[head // 2, (head % 2) * ROWS:(head % 2 + 1) * ROWS] = query[:, head * HD:(head + 1) * HD]
    running_max[...] = jnp.full_like(running_max, -1e30)
    denominator[...] = jnp.zeros_like(denominator)
    weighted[...] = jnp.zeros_like(weighted)
    query_pos = (chip * 2 + c) * ROWS + lax.broadcasted_iota(jnp.int32, (1, ROWS), 1)
    starts = document_starts(lengths_ref, query_pos)

    def attend(j):
        key_pos = (chip - j) * 256 + lax.broadcasted_iota(jnp.int32, (256, ROWS), 0)
        visible = jnp.logical_and(key_pos >= starts, key_pos <= query_pos)
        bias = jnp.where(visible, 0.0, -1e30)
        bias = jnp.concatenate([bias, bias], axis=1)

        scores = [
            lax.dot_general(
                keys_values[j, 0], by_head[i], (((1,), (1,)), ((), ())),
                preferred_element_type=jnp.float32,
            ) * HD ** (-0.5) + bias
            for i in range(4)
        ]
        olds = [running_max[i] for i in range(4)]
        news = [jnp.maximum(olds[i], jnp.max(scores[i], axis=0, keepdims=True)) for i in range(4)]
        for i in range(4):
            factor = jnp.exp(olds[i] - news[i])
            parts = jnp.exp(scores[i] - news[i])
            running_max[i] = news[i]
            denominator[i] = denominator[i] * factor + jnp.sum(parts, axis=0, keepdims=True)
            weighted[i] = weighted[i] * factor + lax.dot_general(
                keys_values[j, 1], parts.astype(jnp.bfloat16), (((0,), (0,)), ((), ())),
                preferred_element_type=jnp.float32,
            )

    def attend_step(j, _):
        @pl.when(jnp.logical_and(j < 4, chip > j))
        def _():
            kv_arrival(j + 1, c).wait_recv()

            for i in (2, 3):
                @pl.when(jnp.logical_and(j == i - 2, kv_sent(i)))
                def _():
                    kv_onward(i).start()

            kv_sibling(j + 1).start()

        @pl.when(jnp.logical_and(j < 4, chip <= j))
        def _():
            keys_values[j + 1] = jnp.zeros_like(keys_values[0])

        @pl.when(chip >= j)
        def _():
            kv_arrival(j, 1 - c).wait_recv()

        attend(j)
        return 0

    lax.fori_loop(0, 5, attend_step, 0)

    total = jnp.zeros((ROWS, HD), jnp.float32)
    for head in range(8):
        lanes = slice((head % 2) * ROWS, (head % 2 + 1) * ROWS)
        columns = slice(head * HD, (head + 1) * HD)
        attended = (weighted[head // 2, :, lanes] / denominator[head // 2, :, lanes]).T
        rounded = (residual_in[:, columns].astype(jnp.float32) + attended).astype(jnp.bfloat16)
        residual_ref[:, columns] = rounded
        wide = rounded.astype(jnp.float32)
        total = total + wide * wide
        scaled[:, columns] = (wide * gain_ref[columns].astype(jnp.float32)[None, :]).astype(jnp.bfloat16)

    @pl.when(match)
    def _():
        tokens[yh, my_source, yl, mine] = scaled[...]

    @pl.when(jnp.logical_not(match))
    def _():
        cross_copy().start()

    squares[mp] = jnp.broadcast_to(jnp.sum(total.T, axis=0, keepdims=True), (8, ROWS))

    @pl.when(mp != owner_mp)
    def _():
        square_copy().start()

    def handle_until(step):
        def one(event, _):
            handle(event)
            return 0

        lax.fori_loop(pick(step, (0,) + BEFORE[:-1]), pick(step, BEFORE), one, 0)

    def step_through(step, _):
        handle_until(step)
        for i, (_, _, when) in enumerate(PIECES):
            if when >= 0:
                @pl.when(step == when)
                def _():
                    weight_copy(i).start()

        def each(counts, work):
            def one(group, _):
                work(group)
                return 0

            lax.fori_loop(pick(step, (0,) + counts[:-1]), pick(step, counts), one, 0)

        def gate_group(group):
            sibling_arrived(group)
            multiply(group, 0)

        @pl.when(step == 2)
        def _():
            weights_arrived(0)

        each(GATED, gate_group)

        @pl.when(step == 3)
        def _():
            weights_arrived(1)

        each(UPPED, lambda group: multiply(group, 1))

        def relay_group(group):
            for part in range(2):
                add_relayed(group, part)

        each(RELAYED, relay_group)
        return 0

    lax.fori_loop(0, 8, step_through, 0)

    def last(step, _):
        for part in range(2):
            add_relayed(step, part)
        return 0

    lax.fori_loop(RELAYED[-1], 8, last, 0)

    for i in range(4):
        @pl.when(kv_sent(i))
        def _():
            kv_onward(i).wait_send()
    for j in range(5):
        @pl.when(chip >= j)
        def _():
            kv_sibling(j).wait_send()

    @pl.when(mp != owner_mp)
    def _():
        square_copy().wait_send()

    for i in range(len(PIECES)):
        weight_copy(i).wait_send()

    @pl.when(jnp.logical_not(match))
    def _():
        cross_copy().wait_send()

    def tokens_sent(event, _):
        h, source, block, goes, _ = event_of(event)
        for wanted, copy in onward(h, source, lax.rem(yl + block, 2), goes):
            @pl.when(wanted)
            def _():
                copy.wait_send()

        @pl.when(jnp.logical_and(owned_here(h, source), block == 1))
        def _():
            for wanted, copy in inverse_onward(goes, lax.rem(source, 2)):
                @pl.when(wanted)
                def _():
                    copy.wait_send()

        return 0

    lax.fori_loop(0, 16, tokens_sent, 0)

    for low in range(2):
        inverse_copy(low, 1 - c, 0, sibling).wait_recv()
        scale = jnp.concatenate([inverse[low, 0], inverse[low, 1]], axis=1)[0:1]
        def total_of(quarter):
            rows = pl.ds(quarter * QUARTER, QUARTER)
            total = own_sum[low, rows]
            for slot in range(2):
                view = landed.at[slot, low, rows]
                pltpu.make_async_remote_copy(
                    src_ref=view, dst_ref=view, send_sem=sum_send.at[0, 0, quarter],
                    recv_sem=sum_recv.at[slot, low, quarter], device_id=x_peers[0], device_id_type=MESH,
                ).wait_recv()
                total = total + landed[slot, low, rows].astype(jnp.float32)
            return total * scale

        for i in range(2):
            gate, up = total_of(i), total_of(2 + i)
            out_ref[i * QUARTER:(i + 1) * QUARTER, low * 256:(low + 1) * 256] = (
                gate / (1.0 + jnp.exp(-gate)) * up
            ).astype(jnp.bfloat16)

    def sums_sent(step, _):
        h, source = group_of(step)
        role = role_of(h, source)
        for quarter in range(4):
            @pl.when(role == 2)
            def _():
                relay_copy(h, source, quarter).wait_send()

            @pl.when(lax.rem(role, 2) == 1)
            def _():
                sum_copy(h, source, quarter).wait_send()

        return 0

    lax.fori_loop(0, 8, sums_sent, 0)


def hand_over_kernel(residual_ref, hidden_ref, residual_out, hidden_out):
    residual_out[...] = residual_ref[...]
    hidden_out[...] = hidden_ref[...]


def on_device(
    query_heads, key_heads, value_heads, residual_in, norm_gain, gate_weight, up_weight, doc_lengths
):
    dma = pltpu.SemaphoreType.DMA
    vmem = pl.BlockSpec(memory_space=pltpu.VMEM)
    anywhere = pl.BlockSpec(memory_space=pl.ANY)
    residual, hidden = pl.pallas_call(
        layer_kernel,
        out_shape=(
            jax.ShapeDtypeStruct((ROWS, KB), jnp.bfloat16),
            jax.ShapeDtypeStruct((HALF, 4 * ROWS), jnp.bfloat16),
        ),
        in_specs=[pl.BlockSpec(memory_space=pltpu.SMEM)] + [anywhere] * 4 + [vmem] + [anywhere] * 2,
        out_specs=(vmem, vmem),
        scratch_shapes=[
            pltpu.VMEM((2, 4, 2, 2 * ROWS, KB), jnp.bfloat16),
            pltpu.VMEM((2, WIDTH, KB), jnp.bfloat16),
            pltpu.VMEM((2, 4, WIDTH, 2 * ROWS), jnp.bfloat16),
            pltpu.VMEM((2, 4, 2, QUARTER, 2 * ROWS), jnp.bfloat16),
            pltpu.VMEM((2, 2, WIDTH, 2 * ROWS), jnp.bfloat16),
            pltpu.VMEM((2, WIDTH, 2 * ROWS), jnp.float32),
            pltpu.VMEM((ROWS, KB), jnp.bfloat16),
            pltpu.VMEM((4, 2 * ROWS, HD), jnp.bfloat16),
            pltpu.VMEM((5, 2, 2 * ROWS, HD), jnp.bfloat16),
            pltpu.VMEM((ROWS, KB), jnp.bfloat16),
            pltpu.VMEM((ROWS, KB), jnp.bfloat16),
            pltpu.VMEM((8, 8, ROWS), jnp.float32),
            pltpu.VMEM((2, 2, 8, ROWS), jnp.float32),
            pltpu.VMEM((4, 1, 2 * ROWS), jnp.float32),
            pltpu.VMEM((4, 1, 2 * ROWS), jnp.float32),
            pltpu.VMEM((4, HD, 2 * ROWS), jnp.float32),
            dma((6,)), dma((4,)), dma((5,)), dma((5, 2)), dma((1,)), dma((8,)), dma((2, 4)), dma((2, 2)),
            dma((3,)), dma((3,)), dma((1,)), dma((2, 4, 2, 2)),
            dma((2, 4, 2)), dma((2, 4, 2)), dma((2, 4, 2)), dma((2, 4, 2)),
            dma((2, 4, 4)), dma((2, 4, 2)), dma((2, 4, 4)), dma((2, 2, 4)),
        ],
        compiler_params=pltpu.CompilerParams(
            collective_id=0, has_side_effects=True, vmem_limit_bytes=56 * 2**20
        ),
        name="layer",
    )(
        doc_lengths, query_heads, key_heads, value_heads, residual_in,
        norm_gain, gate_weight.T, up_weight.T,
    )
    residual, hidden = pl.pallas_call(
        hand_over_kernel,
        out_shape=(
            jax.ShapeDtypeStruct((ROWS, KB), jnp.bfloat16),
            jax.ShapeDtypeStruct((HALF, 4 * ROWS), jnp.bfloat16),
        ),
        in_specs=[vmem] * 2,
        out_specs=(vmem, vmem),
        name="hand_over",
    )(residual, hidden)
    return residual, hidden.T


def solution(mesh):
    in_specs = (
        P("ctx", "mp"),
        P("ctx", "mp"),
        P("ctx", "mp"),
        P("ctx", "mp"),
        P("mp"),
        P("mp", "ctx"),
        P("mp", "ctx"),
        P(),
    )
    out_specs = (P("ctx", "mp"), P("mp", "ctx"))
    return jax.shard_map(
        on_device, mesh=mesh, in_specs=in_specs, out_specs=out_specs, check_vma=False
    )
```
